32 devices in a mesh: seq: 4 (over y, x), ch: 8 (over z, core).
Axes of the slice: x: 2, y: 2, z: 4, core: 2. Of those that a mesh axis runs over, the one named last changes fastest.
Arguments:
- token_ids: int32 [2048], P('seq'), may hold values from 0 to 511
- embedding: bfloat16 [512, 4096], P(None, 'ch'), may hold values from -6 to 6
- gain_first: bfloat16 [4096], P('ch'), may hold values from 0.5 to 1.5
- gain_second: bfloat16 [4096], P('ch'), may hold values from 0.5 to 1.5
- weights_first: bfloat16 [4096, 3, 4096], P(None, None, 'ch'), may hold values from -0.09375 to 0.09375
- weights_second: bfloat16 [4096, 3, 4096], P(None, None, 'ch'), may hold values from -0.09375 to 0.09375
- short_first: float32 [7, 3, 4096], P(None, None, 'ch'), may hold values from -2.5 to 2.5
- short_second: float32 [7, 3, 4096], P(None, None, 'ch'), may hold values from -2.5 to 2.5
- medium: bfloat16 [128, 4096], P(None, 'ch'), may hold values from -0.5 to 0.5
- residues: float32 [16, 4096], P(None, 'ch'), as said below
- decay_rates: float32 [16, 4096], P(None, 'ch'), as said below
- cotangent: bfloat16 [2048, 4096], P('seq', 'ch'), may hold values from -6 to 6
Outputs:
- output: bfloat16 [2048, 4096], P('seq', 'ch')
- grad_embedding: float32 [512, 4096], P(None, 'ch')
- grad_gain_first: float32 [4096], P('ch')
- grad_gain_second: float32 [4096], P('ch')
- grad_weights_first: float32 [4096, 3, 4096], P('seq', None, 'ch')
- grad_weights_second: float32 [4096, 3, 4096], P('seq', None, 'ch')
The draws below stay inside these ranges and needn't reach their ends.
Inputs may be any that keep to these rules, and one draw needn't show every extreme that they name: `decay_rates`: positive, at most 0.06 and at least 0.05 / 2048. `residues`: magnitude at most 4 sqrt((0.12 + 1 / 2048) / 16).
All inputs are finite; a program needn't handle non-finite values.
Results may differ from the reference program's by a relative error of at most 0.028.
Values may be sent and summed in bfloat16 or wider, within the bound.
No kernel may reach another device: no remote copies, remote signals or barrier semaphores. Data moves between devices by JAX's collectives and lax.ppermute only.
A program may use at most 192 MiB of HBM per device.

```python
import math
import jax
import jax.numpy as jnp
import numpy as np
from jax import lax

D = 4096
VOCAB = 512
SHORT_TAPS = 7
MEDIUM_TAPS = 128
MODES = 16
SEQ_LEN = 2048
N_SEQ = 4
N_CH = 8


def mode_rates(key):
    base_key = jax.random.fold_in(key, 11)
    uniform_draw = jax.random.uniform(jax.random.fold_in(base_key, 1), (MODES, D), jnp.float32)
    low_fast = jnp.log(0.2 / SEQ_LEN)
    high_fast = jnp.log(0.06)
    spread = jnp.exp(low_fast + uniform_draw * (high_fast - low_fast))
    return spread


def draw_decay_rates(key, part):
    return mode_rates(key)


def draw_residues(key, part):
    rates_drawn = mode_rates(key)
    normal_draw = jnp.clip(jax.random.normal(jax.random.fold_in(key, 23), (MODES, D), jnp.float32), -4.0, 4.0)
    return normal_draw * jnp.sqrt((2.0 * rates_drawn + 1.0 / SEQ_LEN) / MODES)


def touch_ends(array, key, smallest, top_value):
    extent = array.shape
    spot = [jax.random.randint(jax.random.fold_in(key, axis), (), 0, extent[axis]) for axis in range(len(extent))]
    array = array.at[tuple(spot)].set(smallest)
    longest = extent.index(max(extent))
    spot[longest] = (spot[longest] + 1) % extent[longest]
    return array.at[tuple(spot)].set(top_value)


def steps_of(key, extent, shards, smallest, top_value):
    def one(axis_at, shards_of):
        draws = jax.random.uniform(jax.random.fold_in(jax.random.fold_in(key, 6), axis_at), (shards_of,), jnp.float32, smallest / len(shards), top_value / len(shards))
        return jnp.repeat(jnp.exp(draws), extent[axis_at] // shards_of).reshape((-1,) + (1,) * (len(extent) - axis_at - 1))

    level = one(*shards[0])
    for cut in shards[1:]:
        level = level * one(*cut)
    return level


def cumulative_ranks(amount, slope):
    portions = [(1 << 20) // math.isqrt(rank ** slope) + 1 for rank in range(1, amount + 1)]
    scale = 1 + sum(portions) // (1 << 30)
    return np.cumsum(np.array([max(1, weight // scale) for weight in portions]))


def skewed_ids(key, extent, number_of, skew):
    table = cumulative_ranks(number_of, skew)
    lot = jax.random.randint(jax.random.fold_in(key, 1), extent, 0, int(table[number_of - 1]))
    grade = jnp.searchsorted(jnp.asarray(table, jnp.int32), lot, side="right")
    return jax.random.permutation(jax.random.fold_in(key, 2), number_of)[grade].astype(jnp.int32)


def normal_values(stream_key, extent, scale, limit, cuts=(), kind=jnp.bfloat16):
    level = steps_of(stream_key, extent, cuts, -0.22, 0.18) if cuts else 1.0
    array = jax.random.normal(stream_key, extent, jnp.float32) * scale * level
    return jnp.minimum(jnp.maximum(array, -limit), limit).astype(kind)


def setup_inputs(seed: int = 0) -> dict:
    arg_keys = jax.random.split(jax.random.key(seed), 13)
    return {
        "token_ids": touch_ends(skewed_ids(arg_keys[0], (SEQ_LEN,), VOCAB, 2), jax.random.fold_in(arg_keys[0], 3), 0, VOCAB - 1).astype(jnp.int32),
        "embedding": normal_values(arg_keys[1], (VOCAB, D), 1.0, 6.0, ((1, 8),)),
        "gain_first": jnp.clip(1.0 + 0.1 * jax.random.normal(arg_keys[2], (D,), jnp.float32), 0.5, 1.5).astype(jnp.bfloat16),
        "gain_second": jnp.clip(1.0 + 0.1 * jax.random.normal(arg_keys[3], (D,), jnp.float32), 0.5, 1.5).astype(jnp.bfloat16),
        "weights_first": normal_values(arg_keys[4], (D, 3, D), D ** -0.5, 0.09375, ((2, 8),)),
        "weights_second": normal_values(arg_keys[5], (D, 3, D), D ** -0.5, 0.09375, ((2, 8),)),
        "short_first": normal_values(arg_keys[6], (SHORT_TAPS, 3, D), 0.4, 2.5, ((2, 8),), jnp.float32),
        "short_second": normal_values(arg_keys[7], (SHORT_TAPS, 3, D), 0.4, 2.5, ((2, 8),), jnp.float32),
        "medium": normal_values(arg_keys[8], (MEDIUM_TAPS, D), MEDIUM_TAPS ** -0.5, 0.5, ((1, 8),)),
        "residues": draw_residues(jax.random.fold_in(arg_keys[12], 71), 0),
        "decay_rates": draw_decay_rates(jax.random.fold_in(arg_keys[12], 71), 0),
        "cotangent": normal_values(arg_keys[11], (SEQ_LEN, D), 1.0, 6.0, ((0, 4), (1, 8))),
    }


epsilon = 1e-06
highest = lax.Precision.HIGHEST

def short_causal(projected, short_filter):
    tap_count = short_filter.shape[0]
    row_count = projected.shape[0]
    widened = jnp.pad(projected.astype(jnp.float32), ((tap_count - 1, 0), (0, 0), (0, 0)))
    running = jnp.zeros(projected.shape, jnp.float32)
    for offset in range(tap_count):
        first_row = tap_count - 1 - offset
        running = running + short_filter[offset] * widened[first_row:first_row + row_count]
    return running

def short_anti(gradient, short_filter):
    tap_count = short_filter.shape[0]
    row_count = gradient.shape[0]
    widened = jnp.pad(gradient.astype(jnp.float32), ((0, tap_count - 1), (0, 0), (0, 0)))
    running = jnp.zeros(gradient.shape, jnp.float32)
    for offset in range(tap_count):
        running = running + short_filter[offset] * widened[offset:offset + row_count]
    return running

def medium_causal(signal, medium, forward):
    tap_count = medium.shape[0]
    row_count = signal.shape[0]
    if forward:
        widened = jnp.pad(signal.astype(jnp.float32), ((tap_count - 1, 0), (0, 0)))
    else:
        widened = jnp.pad(signal.astype(jnp.float32), ((0, tap_count - 1), (0, 0)))
    taps_float = medium.astype(jnp.float32)

    def add_lag(offset, running):
        first_row = tap_count - 1 - offset if forward else offset
        window = lax.dynamic_slice_in_dim(widened, first_row, row_count, 0)
        return running + lax.dynamic_index_in_dim(taps_float, offset, 0, False) * window
    return lax.fori_loop(0, tap_count, add_lag, jnp.zeros(signal.shape, jnp.float32))

def long_causal(signal, decay_rates, residues):
    decay = jnp.exp(-decay_rates)

    def advance(state, row_value):
        state = decay * state + row_value[None, :]
        return (state, lax.optimization_barrier(jnp.sum(residues * state, axis=0)))
    unused, outputs = lax.scan(advance, jnp.zeros(decay_rates.shape, jnp.float32), signal)
    return outputs

def mixer_input(inputs, gain, weights, short_filter):
    features = inputs.shape[1]
    as_float = inputs.astype(jnp.float32)
    row_scale = lax.rsqrt(lax.optimization_barrier(jnp.mean(as_float * as_float, axis=1)) + epsilon)
    normed = (as_float * row_scale[:, None] * gain.astype(jnp.float32)).astype(jnp.bfloat16)
    projected = jnp.dot(normed, weights.reshape(features, 3 * features), preferred_element_type=jnp.float32)
    projected = projected.astype(jnp.bfloat16).reshape(-1, 3, features)
    featured = short_causal(projected, short_filter)
    gated = (featured[:, 1, :] * featured[:, 2, :]).astype(jnp.bfloat16)
    return (normed, row_scale, featured, gated)

def project_back(grad_featured, inputs, gain, weights, short_filter, normed, row_scale, grad_above):
    row_count, features = inputs.shape
    grad_projected = short_anti(grad_featured, short_filter).astype(jnp.bfloat16)
    group_width = features // N_CH
    grad_normed = jnp.zeros((row_count, features), jnp.float32)
    for group_index in range(N_CH):
        low_edge = group_index * group_width
        left_part = grad_projected[:, :, low_edge:low_edge + group_width].reshape(row_count, 3 * group_width)
        right_part = weights[:, :, low_edge:low_edge + group_width].reshape(features, 3 * group_width)
        partial_sum = lax.dot_general(left_part, right_part, (((1,), (1,)), ((), ())), preferred_element_type=jnp.float32)
        grad_normed = grad_normed + lax.optimization_barrier(partial_sum.astype(jnp.bfloat16)).astype(jnp.float32)
    flat_grad = grad_projected.reshape(row_count, 3 * features)
    seg_rows = row_count // N_SEQ
    grad_weights = jnp.zeros((features, 3 * features), jnp.float32)
    for group_index in range(N_SEQ):
        low_edge = group_index * seg_rows
        partial_sum = lax.dot_general(normed[low_edge:low_edge + seg_rows], flat_grad[low_edge:low_edge + seg_rows], (((0,), (0,)), ((), ())), preferred_element_type=jnp.float32)
        grad_weights = grad_weights + lax.optimization_barrier(partial_sum.astype(jnp.bfloat16)).astype(jnp.float32)
    as_float = inputs.astype(jnp.float32)
    scaled = grad_normed * gain.astype(jnp.float32)
    row_terms = lax.optimization_barrier(jnp.sum(scaled * as_float, axis=1))
    grad_inputs = grad_above + row_scale[:, None] * scaled - as_float * (row_scale ** 3)[:, None] * row_terms[:, None] / features
    grad_gain = lax.optimization_barrier(jnp.sum(grad_normed * as_float * row_scale[:, None], axis=0))
    return (grad_inputs.astype(jnp.bfloat16), grad_gain, grad_weights.reshape(features, 3, features))

def reference(token_ids, embedding, gain_first, gain_second, weights_first, weights_second, short_first, short_second, medium, residues, decay_rates, cotangent):
    embedded = embedding[token_ids]
    normed_first, scale_first, featured_first, gated_first = mixer_input(embedded, gain_first, weights_first, short_first)
    filtered_first = medium_causal(gated_first, medium, True)
    middle = (embedded.astype(jnp.float32) + featured_first[:, 0, :] * filtered_first).astype(jnp.bfloat16)
    normed_second, scale_second, featured_second, gated_second = mixer_input(middle, gain_second, weights_second, short_second)
    filtered_second = long_causal(gated_second.astype(jnp.float32), decay_rates, residues)
    output = (middle.astype(jnp.float32) + featured_second[:, 0, :] * filtered_second).astype(jnp.bfloat16)
    above_second = cotangent.astype(jnp.float32)
    grad_filtered = (above_second * featured_second[:, 0, :]).astype(jnp.bfloat16)
    grad_gated = long_causal(grad_filtered.astype(jnp.float32)[::-1], decay_rates, residues)[::-1]
    grad_featured = jnp.stack([above_second * filtered_second, grad_gated * featured_second[:, 2, :], grad_gated * featured_second[:, 1, :]], axis=1).astype(jnp.bfloat16)
    grad_middle, grad_gain_second, grad_weights_second = project_back(grad_featured, middle, gain_second, weights_second, short_second, normed_second, scale_second, above_second)
    above_first = grad_middle.astype(jnp.float32)
    grad_filtered = (above_first * featured_first[:, 0, :]).astype(jnp.bfloat16)
    grad_gated = medium_causal(grad_filtered, medium, False)
    grad_featured = jnp.stack([above_first * filtered_first, grad_gated * featured_first[:, 2, :], grad_gated * featured_first[:, 1, :]], axis=1).astype(jnp.bfloat16)
    grad_embedded, grad_gain_first, grad_weights_first = project_back(grad_featured, embedded, gain_first, weights_first, short_first, normed_first, scale_first, above_first)
    onehot = (token_ids[:, None] == jnp.arange(embedding.shape[0], dtype=jnp.int32)[None, :]).astype(jnp.float32)
    grad_embedding = jnp.dot(onehot.T, grad_embedded.astype(jnp.float32), precision=highest)
    return (output, grad_embedding, grad_gain_first, grad_gain_second, grad_weights_first, grad_weights_second)
```

```python
import functools

import jax
import jax.numpy as jnp
from jax import lax
from jax.experimental import pallas as pl
from jax.experimental.pallas import tpu as pltpu
from jax.sharding import PartitionSpec as P

epsilon = 1e-06
f32 = jnp.float32
bf16 = jnp.bfloat16
LANES = 128
EDGE = 16
VMEM_BYTES = 56 * 2**20


def round_up(value, multiple):
    return -(-value // multiple) * multiple


def call(kernel, grid, in_specs, out_specs, out_shape, scratch, flops, moved, prefetch=0):
    return pl.pallas_call(
        kernel,
        grid_spec=pltpu.PrefetchScalarGridSpec(
            num_scalar_prefetch=prefetch,
            grid=grid,
            in_specs=in_specs,
            out_specs=out_specs,
            scratch_shapes=scratch,
        ),
        out_shape=out_shape,
        compiler_params=pltpu.CompilerParams(vmem_limit_bytes=VMEM_BYTES),
        cost_estimate=pl.CostEstimate(flops=flops, bytes_accessed=moved, transcendentals=0),
    )


def whole(shape):
    return pl.BlockSpec(shape, lambda i, *_: (0,) * len(shape))


def lanes(shape):
    return pl.BlockSpec(shape[:-1] + (LANES,), lambda i, *_: (0,) * (len(shape) - 1) + (i,))


def project_kernel(per_step, features, x_ref, gain_ref, w_ref, p_ref, scale_ref, total, squares):
    step = pl.program_id(0)
    width = x_ref.shape[2]

    @pl.when(step == 0)
    def _():
        total[...] = jnp.zeros_like(total)
        squares[...] = jnp.zeros_like(squares)

    for part in range(per_step):
        x = x_ref[part].astype(f32)
        square = x * x
        running = squares[...]
        for lane in range(width // LANES):
            running = running + square[:, lane * LANES : (lane + 1) * LANES]
        squares[...] = running
        scaled = (x * gain_ref[part]).astype(bf16)
        for j in range(3):
            total[j] += jnp.dot(
                scaled, w_ref[j, part * width : (part + 1) * width, :], preferred_element_type=f32
            )

    @pl.when(step == pl.num_programs(0) - 1)
    def _():
        mean = jnp.sum(squares[...], axis=1, keepdims=True) / features
        scale = lax.rsqrt(mean + epsilon)
        scale_ref[...] = scale
        for j in range(3):
            p_ref[j] = (total[j] * scale).astype(bf16)


def project(chunks, gains, weights, rows):
    count, _, width = chunks.shape
    features, columns = weights.shape[1:]
    per_step = 2 if count % 2 == 0 else 1
    return call(
        functools.partial(project_kernel, per_step, features),
        (count // per_step,),
        [
            pl.BlockSpec((per_step, rows, width), lambda i: (i, 0, 0)),
            pl.BlockSpec((per_step, 1, width), lambda i: (i, 0, 0)),
            pl.BlockSpec((3, per_step * width, columns), lambda i: (0, i, 0)),
        ],
        [whole((3, rows, columns)), whole((rows, 1))],
        [
            jax.ShapeDtypeStruct((3, rows, columns), bf16),
            jax.ShapeDtypeStruct((rows, 1), f32),
        ],
        [pltpu.VMEM((3, rows, columns), f32), pltpu.VMEM((rows, LANES), f32)],
        6 * rows * features * columns,
        6 * features * columns + 2 * rows * features,
    )(chunks, gains, weights)


def back_kernel(g_ref, w_ref, o_ref):
    total = None
    for j in range(3):
        term = lax.dot_general(
            g_ref[j], w_ref[j], (((1,), (1,)), ((), ())), preferred_element_type=f32
        )
        total = term if total is None else total + term
    o_ref[0] = total.astype(bf16)


def project_back(grads, weights, count):
    _, rows, columns = grads.shape
    features = weights.shape[1]
    width = features // count
    return call(
        back_kernel,
        (count,),
        [whole((3, rows, columns)), pl.BlockSpec((3, width, columns), lambda i: (0, i, 0))],
        pl.BlockSpec((1, rows, width), lambda i: (i, 0, 0)),
        jax.ShapeDtypeStruct((count, rows, width), bf16),
        [],
        6 * rows * features * columns,
        6 * features * columns + 2 * rows * features,
    )(grads, weights)


def weight_grad_kernel(gain_ref, x_ref, g_ref, o_ref):
    for j in range(3):
        total = None
        for shard in range(x_ref.shape[0]):
            term = lax.dot_general(
                x_ref[shard, 0], g_ref[shard, j], (((0,), (0,)), ((), ())), preferred_element_type=f32
            )
            total = term if total is None else total + term
        o_ref[j] = total * gain_ref[0]


def weight_grad(columns, grads, gains):
    shards, pieces, rows, width = columns.shape
    out = grads.shape[3]
    return call(
        weight_grad_kernel,
        (pieces,),
        [
            pl.BlockSpec((1, width, 1), lambda i: (i, 0, 0)),
            pl.BlockSpec((shards, 1, rows, width), lambda i: (0, i, 0, 0)),
            whole(grads.shape),
        ],
        pl.BlockSpec((3, width, out), lambda i: (0, i, 0)),
        jax.ShapeDtypeStruct((3, pieces * width, out), f32),
        [],
        6 * shards * pieces * rows * width * out,
        2 * columns.size + 2 * grads.size + 12 * pieces * width * out,
    )(gains, columns, grads)


def fir(source, taps, target, base, rows, forward):
    stride = rows // 8
    each = max(n for n in range(1, 25) if stride % n == 0)
    chunk = 8
    tap_count = taps.shape[0]

    def tile(i, carry):
        first = i * each

        def some_taps(c, sums):
            k0 = c * chunk
            low = base + first - k0 - (chunk - 1) if forward else base + first + k0
            loaded = [
                source[pl.ds(low + n, 8, stride=stride), :] for n in range(each + chunk - 1)
            ]
            sums = list(sums)
            for k in range(chunk):
                tap = taps[pl.ds(k0 + k, 1), :]
                for p in range(each):
                    sums[p] = sums[p] + tap * loaded[p + (chunk - 1 - k if forward else k)]
            return tuple(sums)

        sums = lax.fori_loop(
            0, tap_count // chunk, some_taps, tuple(jnp.zeros((8, LANES), f32) for _ in range(each))
        )
        for p in range(each):
            target[pl.ds(first + p, 8, stride=stride), :] = sums[p]
        return carry

    lax.fori_loop(0, stride // each, tile, 0)


def short_sum(source, short, j, first, rows, sign):
    total = None
    for i in range(short.shape[1]):
        term = short[j, i : i + 1, :] * source[first + sign * i : first + sign * i + rows, :]
        total = term if total is None else total + term
    return total


def first_forward_kernel(
    front, rows, token_ref, p_ref, e_ref, short_ref, medium_ref,
    middle_ref, feature_ref, filtered_ref, onehot, projected, gated, taps, kept,
):
    window, vocab = onehot.shape

    @pl.when(pl.program_id(0) == 0)
    def _():
        grid = lax.broadcasted_iota(jnp.int32, (window, vocab), 1)
        onehot[...] = (grid == token_ref[...]).astype(f32).astype(bf16)

    taps[...] = medium_ref[...].astype(f32)
    later = window - front
    product = None
    for j in (1, 2, 0):
        projected[...] = jnp.dot(onehot[...], p_ref[j], preferred_element_type=f32)
        if j == 0:
            feature = short_sum(projected, short_ref, j, front - EDGE, later + EDGE, -1)
            feature_ref[0] = feature[EDGE:, :]
            kept[...] = feature[: rows + EDGE, :]
        else:
            feature = short_sum(projected, short_ref, j, 8, window - 8, -1)
            feature_ref[j] = feature[front - 8 :, :]
            product = feature if product is None else product * feature
    gated[8:, :] = product.astype(bf16).astype(f32)
    fir(gated, taps, projected, front - EDGE, rows + 2 * EDGE, True)
    filtered_ref[...] = projected[EDGE : rows + 2 * EDGE, :]
    embedded = jnp.dot(
        onehot[front - EDGE : front + rows, :], e_ref[...], preferred_element_type=f32
    )
    middle_ref[...] = (embedded + kept[...] * projected[: rows + EDGE, :]).astype(bf16)


def first_forward(tokens, table, embedding, short, medium, rows, front):
    window = tokens.shape[0]
    _, vocab, columns = table.shape
    later = window - front
    shapes = [
        jax.ShapeDtypeStruct((rows + EDGE, columns), bf16),
        jax.ShapeDtypeStruct((3, later, columns), f32),
        jax.ShapeDtypeStruct((rows + EDGE, columns), f32),
    ]
    return call(
        functools.partial(first_forward_kernel, front, rows),
        (columns // LANES,),
        [whole((window, 1))] + [lanes(a.shape) for a in (table, embedding, short, medium)],
        [lanes(s.shape) for s in shapes],
        shapes,
        [
            pltpu.VMEM((window, vocab), bf16),
            pltpu.VMEM((window, LANES), f32),
            pltpu.VMEM((window, LANES), f32),
            pltpu.VMEM((medium.shape[0], LANES), f32),
            pltpu.VMEM((rows + EDGE, LANES), f32),
        ],
        8 * window * vocab * columns,
        16 * window * columns,
    )(tokens, table, embedding, short, medium)


def first_backward_kernel(
    rows, token_ref, above_ref, feature_ref, filtered_ref, short_ref, medium_ref,
    out_ref, onehot, signal, grad_gated, taps, held,
):
    vocab = onehot.shape[0]
    parts = out_ref.shape[0]

    @pl.when(pl.program_id(0) == 0)
    def _():
        grid = lax.broadcasted_iota(jnp.int32, (vocab, rows), 0)
        onehot[...] = (grid == token_ref[...]).astype(f32).astype(bf16)

    taps[...] = medium_ref[...].astype(f32)
    above = above_ref[...].astype(f32)
    signal[...] = (above * feature_ref[0]).astype(bf16).astype(f32)
    extended = rows + EDGE
    fir(signal, taps, grad_gated, 0, extended, False)

    def keep(j, value):
        held[...] = value.astype(bf16).astype(f32)
        grad = short_sum(held, short_ref, j, 0, rows, 1).astype(bf16)
        total = jnp.dot(onehot[...], grad, preferred_element_type=f32).astype(bf16)
        for part in range(parts):
            size = vocab // parts
            out_ref[part, j] = total[part * size : (part + 1) * size, :]

    keep(0, above[:extended, :] * filtered_ref[...])
    keep(1, grad_gated[...] * feature_ref[2, :extended, :])
    keep(2, grad_gated[...] * feature_ref[1, :extended, :])
    total = jnp.dot(onehot[...], above_ref[:rows, :], preferred_element_type=f32).astype(bf16)
    for part in range(parts):
        size = vocab // parts
        out_ref[part, 3] = total[part * size : (part + 1) * size, :]


def first_backward(tokens, above, features, filtered, short, medium, vocab, parts):
    rows = tokens.shape[1]
    later, columns = above.shape
    shape = jax.ShapeDtypeStruct((parts, 4, vocab // parts, columns), bf16)
    return call(
        functools.partial(first_backward_kernel, rows),
        (columns // LANES,),
        [whole((1, rows))] + [lanes(a.shape) for a in (above, features, filtered, short, medium)],
        lanes(shape.shape),
        shape,
        [
            pltpu.VMEM((vocab, rows), bf16),
            pltpu.VMEM((later, LANES), f32),
            pltpu.VMEM((rows + EDGE, LANES), f32),
            pltpu.VMEM((medium.shape[0], LANES), f32),
            pltpu.VMEM((rows + EDGE, LANES), f32),
        ],
        8 * rows * vocab * columns,
        16 * later * columns,
    )(tokens, above, features, filtered, short, medium)


SEGMENTS = 8


def scan_modes(source, decays, states, length, forward, residues=None, target=None):
    def step(i, held):
        position = i if forward else length - 1 - i
        value = source[pl.ds(position, SEGMENTS, stride=length), :]
        held = tuple(d * s + value for d, s in zip(decays, held))
        if target is not None:
            terms = [r * s for r, s in zip(residues, held)]
            while len(terms) > 1:
                terms = [a + b for a, b in zip(terms[::2], terms[1::2])] + (
                    terms[-1:] if len(terms) % 2 else []
                )
            target[pl.ds(position, SEGMENTS, stride=length), :] = terms[0]
        return held

    return lax.fori_loop(0, length, step, tuple(states), unroll=4)


def spread(ref, count):
    return [jnp.broadcast_to(ref[m : m + 1, :], (SEGMENTS, LANES)) for m in range(count)]


def second_features_kernel(
    p_ref, short_ref, above_ref, rate_ref,
    feature_ref, gated_ref, signal_ref, segment_ref, closing_ref, projected, gated, signal, decay,
):
    rows = above_ref.shape[0]
    modes = rate_ref.shape[0]
    length = rows // SEGMENTS
    product = None
    for j in range(3):
        projected[...] = p_ref[j].astype(f32)
        feature = short_sum(projected, short_ref, j, EDGE, rows, -1)
        feature_ref[j] = feature
        if j == 0:
            rounded = (above_ref[...].astype(f32) * feature).astype(bf16)
            signal_ref[...] = rounded
            signal[...] = rounded.astype(f32)
        else:
            product = feature if product is None else product * feature
    rounded = product.astype(bf16)
    gated_ref[...] = rounded
    gated[...] = rounded.astype(f32)
    rates = rate_ref[...]
    decay[...] = jnp.exp(-rates)
    zeros = [jnp.zeros((SEGMENTS, LANES), f32)] * modes
    for way, source in enumerate((gated, signal)):
        ends = scan_modes(source, spread(decay, modes), zeros, length, way == 0)
        for m in range(modes):
            segment_ref[way, pl.ds(m, SEGMENTS, stride=modes), :] = ends[m]
        stride = jnp.exp(-rates * length)
        total = jnp.zeros((modes, LANES), f32)
        for n in range(SEGMENTS):
            at = n if way == 0 else SEGMENTS - 1 - n
            total = stride * total + segment_ref[way, at * modes : (at + 1) * modes, :]
        closing_ref[way] = total


def second_features(projected, short, above, rates):
    rows, columns = above.shape
    modes = rates.shape[0]
    shapes = [
        jax.ShapeDtypeStruct((3, rows, columns), f32),
        jax.ShapeDtypeStruct((rows, columns), bf16),
        jax.ShapeDtypeStruct((rows, columns), bf16),
        jax.ShapeDtypeStruct((2, SEGMENTS * modes, columns), f32),
        jax.ShapeDtypeStruct((2, modes, columns), f32),
    ]
    return call(
        second_features_kernel,
        (columns // LANES,),
        [lanes(a.shape) for a in (projected, short, above, rates)],
        [lanes(s.shape) for s in shapes],
        shapes,
        [
            pltpu.VMEM((rows + EDGE, LANES), f32),
            pltpu.VMEM((rows, LANES), f32),
            pltpu.VMEM((rows, LANES), f32),
            pltpu.VMEM((modes, LANES), f32),
        ],
        100 * rows * columns,
        24 * rows * columns,
    )(projected, short, above, rates)


def second_filter_kernel(
    shards, seq_ref, feature_ref, gated_ref, signal_ref, segment_ref, closing_ref, rate_ref,
    residue_ref, above_ref, middle_ref,
    out_ref, grad_ref, entering, source, filtered, grad_gated, decay, residue,
):
    rows = above_ref.shape[0]
    modes = rate_ref.shape[0]
    length = rows // SEGMENTS
    me = seq_ref[0]
    rates = rate_ref[...]
    decay[...] = jnp.exp(-rates)
    residue[...] = residue_ref[...]
    stride = jnp.exp(-rates * length)
    for way, (values, target) in enumerate(((gated_ref, filtered), (signal_ref, grad_gated))):
        source[...] = values[...].astype(f32)
        state = jnp.zeros((modes, LANES), f32)
        for shard in range(shards):
            ahead = me - 1 - shard if way == 0 else shard - me - 1
            weight = jnp.exp(-rates * (rows * jnp.maximum(ahead, 0)).astype(f32))
            state = state + jnp.where(ahead >= 0, weight * closing_ref[shard, way], 0.0)
        for n in range(SEGMENTS):
            at = n if way == 0 else SEGMENTS - 1 - n
            entering[at * modes : (at + 1) * modes, :] = state
            state = stride * state + segment_ref[way, at * modes : (at + 1) * modes, :]
        starts = [entering[pl.ds(m, SEGMENTS, stride=modes), :] for m in range(modes)]
        scan_modes(
            source, spread(decay, modes), starts, length, way == 0, spread(residue, modes), target
        )
    above = above_ref[...].astype(f32)
    out_ref[...] = (middle_ref[EDGE:, :].astype(f32) + feature_ref[0] * filtered[...]).astype(bf16)
    grad_ref[0] = (above * filtered[...]).astype(bf16)
    grad_ref[1] = (grad_gated[...] * feature_ref[2]).astype(bf16)
    grad_ref[2] = (grad_gated[...] * feature_ref[1]).astype(bf16)


def second_filter(seq, features, gated, signal, segments, closings, rates, residues, above, middle):
    rows, columns = above.shape
    modes = rates.shape[0]
    shapes = [
        jax.ShapeDtypeStruct((rows, columns), bf16),
        jax.ShapeDtypeStruct((3, rows, columns), bf16),
    ]
    operands = (features, gated, signal, segments, closings, rates, residues, above, middle)
    return call(
        functools.partial(second_filter_kernel, closings.shape[0]),
        (columns // LANES,),
        [lanes(a.shape) for a in operands],
        [lanes(s.shape) for s in shapes],
        shapes,
        [pltpu.VMEM((SEGMENTS * modes, LANES), f32)]
        + [pltpu.VMEM((rows, LANES), f32)] * 3
        + [pltpu.VMEM((modes, LANES), f32)] * 2,
        140 * rows * columns,
        28 * rows * columns,
        prefetch=1,
    )(seq, *operands)


def second_grads_kernel(grad_ref, halo_ref, p_ref, short_ref, scale_ref, out_ref, term_ref, held):
    rows = grad_ref.shape[1]
    scale = scale_ref[...]
    terms = None
    for j in range(3):
        held[:rows, :] = grad_ref[j].astype(f32)
        held[rows:, :] = halo_ref[j].astype(f32)
        grad = short_sum(held, short_ref, j, 0, rows, 1)
        term = grad * p_ref[j, EDGE:, :].astype(f32)
        terms = term if terms is None else terms + term
        out_ref[j] = (grad * scale).astype(bf16)
    total = jnp.sum(terms, axis=1, keepdims=True)

    @pl.when(pl.program_id(0) == 0)
    def _():
        term_ref[...] = total

    @pl.when(pl.program_id(0) > 0)
    def _():
        term_ref[...] += total


def second_grads(grads, halo, projected, short, scale):
    _, rows, columns = grads.shape
    shapes = [
        jax.ShapeDtypeStruct((3, rows, columns), bf16),
        jax.ShapeDtypeStruct((rows, 1), f32),
    ]
    return call(
        second_grads_kernel,
        (columns // LANES,),
        [lanes(a.shape) for a in (grads, halo, projected, short)] + [whole((rows, 1))],
        [lanes(shapes[0].shape), whole((rows, 1))],
        shapes,
        [pltpu.VMEM((rows + EDGE, LANES), f32)],
        60 * rows * columns,
        24 * rows * columns,
    )(grads, halo, projected, short, scale)


def shift(value, axis, by):
    devices = lax.axis_size(axis)
    pairs = [(i, i + by) for i in range(devices) if 0 <= i + by < devices]
    return lax.ppermute(value, axis, pairs)


def gather_ch(value):
    return lax.all_gather(value, "ch", axis=0, tiled=False)


def scatter_ch(value):
    return lax.psum_scatter(value, "ch", scatter_dimension=0, tiled=False)


def gather_seq(value):
    return lax.all_gather(value, "seq", axis=0, tiled=False)


def exchange_seq(value):
    return lax.all_to_all(value, "seq", split_axis=0, concat_axis=0, tiled=True)


def per_device(
    token_ids,
    embedding,
    gain_first,
    gain_second,
    weights_first,
    weights_second,
    short_first,
    short_second,
    medium,
    residues,
    decay_rates,
    cotangent,
):
    shards = lax.axis_size("seq")
    pieces = lax.axis_size("ch")
    seq = lax.axis_index("seq")
    vocab, width = embedding.shape
    rows = token_ids.shape[0]
    features = width * pieces
    taps, tap_count = medium.shape[0], short_first.shape[0]
    front = round_up(EDGE + taps - 1 + tap_count - 1, 16)
    back = round_up(EDGE + taps - 1, 16)
    w_first, w_second = (jnp.transpose(w, (1, 0, 2)) for w in (weights_first, weights_second))
    s_first, s_second = (jnp.transpose(s, (1, 0, 2)) for s in (short_first, short_second))

    gains = jnp.concatenate(
        [gain_first[None], gain_second[None], jnp.zeros((EDGE - 2, width), bf16)], axis=0
    )
    gathered = gather_ch(jnp.concatenate([embedding, gains], axis=0))
    gains_first = gathered[:, vocab : vocab + 1, :].astype(f32)
    gains_second = gathered[:, vocab + 1 : vocab + 2, :].astype(f32)
    table, scale_table = project(gathered, gains_first, w_first, vocab)

    tokens = lax.all_gather(token_ids, "seq", axis=0, tiled=True)
    tokens = jnp.pad(tokens, (front, back), constant_values=-1)
    tokens = lax.dynamic_slice_in_dim(tokens, seq * rows, front + rows + back, 0)
    middle, features_first, filtered_first = first_forward(
        tokens[:, None], table, embedding, s_first, medium, rows, front
    )

    middles = gather_ch(middle)
    projected, scale = project(middles, gains_second, w_second, rows + EDGE)
    features_second, gated, signal, segments, closing = second_features(
        projected, s_second, cotangent, decay_rates
    )
    closings = gather_seq(closing)
    output, grad_featured = second_filter(
        seq[None], features_second, gated, signal, segments, closings,
        decay_rates, residues, cotangent, middle,
    )
    halo = shift(grad_featured[:, :EDGE, :], "seq", -1)
    scale = scale[EDGE:]
    grads, terms = second_grads(grad_featured, halo, projected, s_second, scale)
    terms = lax.psum(terms[:, 0], "ch")
    grad_normed = scatter_ch(project_back(grads, w_second, pieces)).astype(f32)
    as_float = middle[EDGE:].astype(f32)
    grad_middle = (
        cotangent.astype(f32)
        + gain_second.astype(f32) * grad_normed
        - as_float * (scale * scale) * terms[:, None] / features
    ).astype(bf16)
    grad_gain_second = jnp.sum(grad_normed * as_float, axis=0)

    each = pieces // shards
    own = middles[:, EDGE:, :].reshape(shards, each, rows, width)
    columns = exchange_seq(own)
    block_gains = lax.dynamic_slice_in_dim(gains_second, seq * each, each, 0)
    grad_weights_second = weight_grad(
        columns, gather_seq(grads), jnp.swapaxes(block_gains, 1, 2)
    )

    above = jnp.concatenate([grad_middle, shift(grad_middle[:back], "seq", -1)], axis=0)
    sums = first_backward(
        token_ids[None], above, features_first, filtered_first, s_first, medium, vocab, shards
    )
    own_sums = jnp.sum(exchange_seq(sums).astype(f32), axis=0)
    share = vocab // shards
    at = seq * share
    own_scale = lax.dynamic_slice_in_dim(scale_table, at, share, 0)
    own_table = lax.dynamic_slice_in_dim(table, at, share, 1).astype(f32)
    own_embedding = lax.dynamic_slice_in_dim(embedding, at, share, 0).astype(f32)
    own_grads = own_sums[:3]
    terms = lax.psum(jnp.sum(own_grads * own_table, axis=(0, 2)), "ch")
    own_grads = (own_grads * own_scale[None]).astype(bf16)
    grad_normed = scatter_ch(project_back(own_grads, w_first, pieces)).astype(f32)
    grad_embedding = (
        own_sums[3]
        + gain_first.astype(f32) * grad_normed
        - own_embedding * (own_scale * own_scale) * terms[:, None] / features
    )
    grad_gain_first = jnp.sum(grad_normed * own_embedding, axis=0)
    last = jnp.concatenate(
        [
            grad_embedding,
            grad_gain_first[None],
            grad_gain_second[None],
            jnp.zeros((6, width), f32),
        ],
        axis=0,
    )
    last = gather_seq(last)
    block = lax.dynamic_slice_in_dim(gathered, seq * each, each, 0)[:, :vocab, :]
    block_gains = lax.dynamic_slice_in_dim(gains_first, seq * each, each, 0)
    all_grads = jnp.swapaxes(gather_seq(own_grads), 0, 1).reshape(1, 3, vocab, width)
    grad_weights_first = weight_grad(block[None], all_grads, jnp.swapaxes(block_gains, 1, 2))
    return (
        output,
        last[:, :share].reshape(vocab, width),
        jnp.sum(last[:, share], axis=0),
        jnp.sum(last[:, share + 1], axis=0),
        jnp.transpose(grad_weights_first, (1, 0, 2)),
        jnp.transpose(grad_weights_second, (1, 0, 2)),
    )


def solution(mesh):
    placed = (
        P("seq"),
        P(None, "ch"),
        P("ch"),
        P("ch"),
        P(None, None, "ch"),
        P(None, None, "ch"),
        P(None, None, "ch"),
        P(None, None, "ch"),
        P(None, "ch"),
        P(None, "ch"),
        P(None, "ch"),
        P("seq", "ch"),
    )
    return jax.shard_map(
        per_device,
        mesh=mesh,
        in_specs=placed,
        out_specs=(
            P("seq", "ch"),
            P(None, "ch"),
            P("ch"),
            P("ch"),
            P("seq", None, "ch"),
            P("seq", None, "ch"),
        ),
        check_vma=False,
    )
```

```python
import functools

import jax
import jax.numpy as jnp
from jax import lax
from jax.experimental import pallas as pl
from jax.experimental.pallas import tpu as pltpu
from jax.sharding import PartitionSpec as P

epsilon = 1e-06
f32 = jnp.float32
bf16 = jnp.bfloat16
LANES = 128
EDGE = 16
VMEM_BYTES = 56 * 2**20


def round_up(value, multiple):
    return -(-value // multiple) * multiple


def call(kernel, grid, in_specs, out_specs, out_shape, scratch, flops, moved, prefetch=0):
    return pl.pallas_call(
        kernel,
        grid_spec=pltpu.PrefetchScalarGridSpec(
            num_scalar_prefetch=prefetch,
            grid=grid,
            in_specs=in_specs,
            out_specs=out_specs,
            scratch_shapes=scratch,
        ),
        out_shape=out_shape,
        compiler_params=pltpu.CompilerParams(vmem_limit_bytes=VMEM_BYTES),
        cost_estimate=pl.CostEstimate(flops=flops, bytes_accessed=moved, transcendentals=0),
    )


def whole(shape):
    return pl.BlockSpec(shape, lambda i, *_: (0,) * len(shape))


def lanes(shape):
    return pl.BlockSpec(shape[:-1] + (LANES,), lambda i, *_: (0,) * (len(shape) - 1) + (i,))


def project_kernel(per_step, features, x_ref, gain_ref, w_ref, p_ref, scale_ref, total, squares):
    step = pl.program_id(0)
    width = x_ref.shape[2]

    @pl.when(step == 0)
    def _():
        total[...] = jnp.zeros_like(total)
        squares[...] = jnp.zeros_like(squares)

    for part in range(per_step):
        x = x_ref[part].astype(f32)
        square = x * x
        running = squares[...]
        for lane in range(width // LANES):
            running = running + square[:, lane * LANES : (lane + 1) * LANES]
        squares[...] = running
        scaled = (x * gain_ref[part]).astype(bf16)
        for j in range(3):
            total[j] += jnp.dot(
                scaled, w_ref[j, part * width : (part + 1) * width, :], preferred_element_type=f32
            )

    @pl.when(step == pl.num_programs(0) - 1)
    def _():
        mean = jnp.sum(squares[...], axis=1, keepdims=True) / features
        scale = lax.rsqrt(mean + epsilon)
        scale_ref[...] = scale
        for j in range(3):
            p_ref[j] = (total[j] * scale).astype(bf16)


def project(chunks, gains, weights, rows):
    count, _, width = chunks.shape
    features, columns = weights.shape[1:]
    per_step = 2 if count % 2 == 0 else 1
    return call(
        functools.partial(project_kernel, per_step, features),
        (count // per_step,),
        [
            pl.BlockSpec((per_step, rows, width), lambda i: (i, 0, 0)),
            pl.BlockSpec((per_step, 1, width), lambda i: (i, 0, 0)),
            pl.BlockSpec((3, per_step * width, columns), lambda i: (0, i, 0)),
        ],
        [whole((3, rows, columns)), whole((rows, 1))],
        [
            jax.ShapeDtypeStruct((3, rows, columns), bf16),
            jax.ShapeDtypeStruct((rows, 1), f32),
        ],
        [pltpu.VMEM((3, rows, columns), f32), pltpu.VMEM((rows, LANES), f32)],
        6 * rows * features * columns,
        6 * features * columns + 2 * rows * features,
    )(chunks, gains, weights)


def back_kernel(order_ref, g_ref, w_ref, extra_ref, o_ref):
    total = None
    for j in range(3):
        term = lax.dot_general(
            g_ref[j], w_ref[j], (((1,), (1,)), ((), ())), preferred_element_type=f32
        )
        total = term if total is None else total + term
    rows = g_ref.shape[1]
    o_ref[0, :rows, :] = total.astype(bf16)
    if o_ref.shape[1] > rows:
        o_ref[0, rows:, :] = extra_ref[...]


def project_back(grads, weights, order, extra=None):
    _, rows, columns = grads.shape
    features = weights.shape[1]
    count = order.shape[0]
    width = features // count
    more = 0 if extra is None else extra.shape[0]
    if extra is None:
        extra = jnp.zeros((EDGE, width), bf16)
    return call(
        back_kernel,
        (count,),
        [
            whole((3, rows, columns)),
            pl.BlockSpec((3, width, columns), lambda i, order: (0, order[i], 0)),
            whole(extra.shape),
        ],
        pl.BlockSpec((1, rows + more, width), lambda i, *_: (i, 0, 0)),
        jax.ShapeDtypeStruct((count, rows + more, width), bf16),
        [],
        6 * rows * features * columns,
        6 * features * columns + 2 * rows * features,
        prefetch=1,
    )(order, grads, weights, extra)


def weight_grad_kernel(spans, order_ref, gain_ref, x_ref, *refs):
    out_ref = refs[-1]
    for j in range(3):
        total = None
        for (slot, first), g_ref in zip(spans, refs[:-1]):
            some = x_ref[order_ref[slot], 0, first : first + g_ref.shape[1], :]
            term = lax.dot_general(
                some, g_ref[j], (((0,), (0,)), ((), ())), preferred_element_type=f32
            )
            total = term if total is None else total + term
        out_ref[j] = total * gain_ref[0]


def weight_grad(columns, grads, order, gains):
    shards, pieces, rows, width = columns.shape
    out = grads[0][2].shape[2]
    arrays = [array for _, _, array in grads]
    return call(
        functools.partial(weight_grad_kernel, [(slot, first) for slot, first, _ in grads]),
        (pieces,),
        [
            pl.BlockSpec((1, width, 1), lambda i, *_: (i, 0, 0)),
            pl.BlockSpec((shards, 1, rows, width), lambda i, *_: (0, i, 0, 0)),
        ]
        + [whole(array.shape) for array in arrays],
        pl.BlockSpec((3, width, out), lambda i, *_: (0, i, 0)),
        jax.ShapeDtypeStruct((3, pieces * width, out), f32),
        [],
        6 * shards * pieces * rows * width * out,
        2 * columns.size + 6 * shards * rows * out + 12 * pieces * width * out,
        prefetch=1,
    )(order, gains, columns, *arrays)


def fir(source, taps, target, base, rows, forward):
    stride = rows // 8
    each = max(n for n in range(1, 25) if stride % n == 0)
    chunk = 8
    tap_count = taps.shape[0]

    def tile(i, carry):
        first = i * each

        def some_taps(c, sums):
            k0 = c * chunk
            low = base + first - k0 - (chunk - 1) if forward else base + first + k0
            loaded = [
                source[pl.ds(low + n, 8, stride=stride), :] for n in range(each + chunk - 1)
            ]
            sums = list(sums)
            for k in range(chunk):
                tap = taps[pl.ds(k0 + k, 1), :]
                for p in range(each):
                    sums[p] = sums[p] + tap * loaded[p + (chunk - 1 - k if forward else k)]
            return tuple(sums)

        sums = lax.fori_loop(
            0, tap_count // chunk, some_taps, tuple(jnp.zeros((8, LANES), f32) for _ in range(each))
        )
        for p in range(each):
            target[pl.ds(first + p, 8, stride=stride), :] = sums[p]
        return carry

    lax.fori_loop(0, stride // each, tile, 0)


def short_sum(source, short, j, first, rows, sign):
    total = None
    for i in range(short.shape[1]):
        term = short[j, i : i + 1, :] * source[first + sign * i : first + sign * i + rows, :]
        total = term if total is None else total + term
    return total


def first_forward_kernel(
    front, rows, token_ref, p_ref, e_ref, short_ref, medium_ref,
    middle_ref, feature_ref, filtered_ref, onehot, projected, gated, taps, kept,
):
    window, vocab = onehot.shape

    @pl.when(pl.program_id(0) == 0)
    def _():
        grid = lax.broadcasted_iota(jnp.int32, (window, vocab), 1)
        onehot[...] = (grid == token_ref[...]).astype(f32).astype(bf16)

    taps[...] = medium_ref[...].astype(f32)
    later = window - front
    product = None
    for j in (1, 2, 0):
        rows_j = p_ref[:, j].reshape(vocab, LANES)
        projected[...] = jnp.dot(onehot[...], rows_j, preferred_element_type=f32)
        if j == 0:
            feature = short_sum(projected, short_ref, j, front - EDGE, later + EDGE, -1)
            feature_ref[0] = feature[EDGE:, :]
            kept[...] = feature[: rows + EDGE, :]
        else:
            feature = short_sum(projected, short_ref, j, 8, window - 8, -1)
            feature_ref[j] = feature[front - 8 :, :]
            product = feature if product is None else product * feature
    gated[8:, :] = product.astype(bf16).astype(f32)
    fir(gated, taps, projected, front - EDGE, rows + 2 * EDGE, True)
    filtered_ref[...] = projected[EDGE : rows + 2 * EDGE, :]
    embedded = jnp.dot(
        onehot[front - EDGE : front + rows, :], e_ref[...], preferred_element_type=f32
    )
    middle_ref[...] = (embedded + kept[...] * projected[: rows + EDGE, :]).astype(bf16)


def first_forward(tokens, table, embedding, short, medium, rows, front):
    window = tokens.shape[0]
    vocab, columns = embedding.shape
    later = window - front
    shapes = [
        jax.ShapeDtypeStruct((rows + EDGE, columns), bf16),
        jax.ShapeDtypeStruct((3, later, columns), f32),
        jax.ShapeDtypeStruct((rows + EDGE, columns), f32),
    ]
    return call(
        functools.partial(first_forward_kernel, front, rows),
        (columns // LANES,),
        [whole((window, 1))] + [lanes(a.shape) for a in (table, embedding, short, medium)],
        [lanes(s.shape) for s in shapes],
        shapes,
        [
            pltpu.VMEM((window, vocab), bf16),
            pltpu.VMEM((window, LANES), f32),
            pltpu.VMEM((window, LANES), f32),
            pltpu.VMEM((medium.shape[0], LANES), f32),
            pltpu.VMEM((rows + EDGE, LANES), f32),
        ],
        8 * window * vocab * columns,
        16 * window * columns,
    )(tokens, table, embedding, short, medium)


def first_backward_kernel(
    rows, token_ref, above_ref, feature_ref, filtered_ref, short_ref, medium_ref,
    out_ref, other_ref, onehot, signal, grad_gated, taps, held,
):
    vocab = onehot.shape[0]
    parts = out_ref.shape[0]

    @pl.when(pl.program_id(0) == 0)
    def _():
        grid = lax.broadcasted_iota(jnp.int32, (vocab, rows), 0)
        onehot[...] = (grid == token_ref[...]).astype(f32).astype(bf16)

    taps[...] = medium_ref[...].astype(f32)
    above = above_ref[...].astype(f32)
    signal[...] = (above * feature_ref[0]).astype(bf16).astype(f32)
    extended = rows + EDGE
    fir(signal, taps, grad_gated, 0, extended, False)

    def keep(j, value):
        held[...] = value.astype(bf16).astype(f32)
        grad = short_sum(held, short_ref, j, 0, rows, 1).astype(bf16)
        total = jnp.dot(onehot[...], grad, preferred_element_type=f32).astype(bf16)
        for part in range(parts):
            size = vocab // parts
            out_ref[part, j] = total[part * size : (part + 1) * size, :]

    keep(0, above[:extended, :] * filtered_ref[...])
    keep(1, grad_gated[...] * feature_ref[2, :extended, :])
    keep(2, grad_gated[...] * feature_ref[1, :extended, :])
    total = jnp.dot(onehot[...], above_ref[:rows, :], preferred_element_type=f32).astype(bf16)
    for part in range(parts):
        size = vocab // parts
        other_ref[part] = total[part * size : (part + 1) * size, :]


def first_backward(tokens, above, features, filtered, short, medium, vocab, parts):
    rows = tokens.shape[1]
    later, columns = above.shape
    shapes = [
        jax.ShapeDtypeStruct((parts, 3, vocab // parts, columns), bf16),
        jax.ShapeDtypeStruct((parts, vocab // parts, columns), bf16),
    ]
    return call(
        functools.partial(first_backward_kernel, rows),
        (columns // LANES,),
        [whole((1, rows))] + [lanes(a.shape) for a in (above, features, filtered, short, medium)],
        [lanes(s.shape) for s in shapes],
        shapes,
        [
            pltpu.VMEM((vocab, rows), bf16),
            pltpu.VMEM((later, LANES), f32),
            pltpu.VMEM((rows + EDGE, LANES), f32),
            pltpu.VMEM((medium.shape[0], LANES), f32),
            pltpu.VMEM((rows + EDGE, LANES), f32),
        ],
        8 * rows * vocab * columns,
        16 * later * columns,
    )(tokens, above, features, filtered, short, medium)


SEGMENTS = 8


def scan_modes(source, decays, states, length, forward, residues=None, target=None):
    def step(i, held):
        position = i if forward else length - 1 - i
        value = source[pl.ds(position, SEGMENTS, stride=length), :]
        held = tuple(d * s + value for d, s in zip(decays, held))
        if target is not None:
            terms = [r * s for r, s in zip(residues, held)]
            while len(terms) > 1:
                terms = [a + b for a, b in zip(terms[::2], terms[1::2])] + (
                    terms[-1:] if len(terms) % 2 else []
                )
            target[pl.ds(position, SEGMENTS, stride=length), :] = terms[0]
        return held

    return lax.fori_loop(0, length, step, tuple(states), unroll=4)


def spread(ref, count):
    return [jnp.broadcast_to(ref[m : m + 1, :], (SEGMENTS, LANES)) for m in range(count)]


def second_features_kernel(
    p_ref, short_ref, above_ref, rate_ref,
    feature_ref, gated_ref, signal_ref, segment_ref, closing_ref, projected, gated, signal, decay,
):
    rows = above_ref.shape[0]
    modes = rate_ref.shape[0]
    length = rows // SEGMENTS
    product = None
    for j in range(3):
        projected[...] = p_ref[j].astype(f32)
        feature = short_sum(projected, short_ref, j, EDGE, rows, -1)
        feature_ref[j] = feature
        if j == 0:
            rounded = (above_ref[...].astype(f32) * feature).astype(bf16)
            signal_ref[...] = rounded
            signal[...] = rounded.astype(f32)
        else:
            product = feature if product is None else product * feature
    rounded = product.astype(bf16)
    gated_ref[...] = rounded
    gated[...] = rounded.astype(f32)
    rates = rate_ref[...]
    decay[...] = jnp.exp(-rates)
    zeros = [jnp.zeros((SEGMENTS, LANES), f32)] * modes
    for way, source in enumerate((gated, signal)):
        ends = scan_modes(source, spread(decay, modes), zeros, length, way == 0)
        for m in range(modes):
            segment_ref[way, pl.ds(m, SEGMENTS, stride=modes), :] = ends[m]
        stride = jnp.exp(-rates * length)
        total = jnp.zeros((modes, LANES), f32)
        for n in range(SEGMENTS):
            at = n if way == 0 else SEGMENTS - 1 - n
            total = stride * total + segment_ref[way, at * modes : (at + 1) * modes, :]
        closing_ref[way] = total


def second_features(projected, short, above, rates):
    rows, columns = above.shape
    modes = rates.shape[0]
    shapes = [
        jax.ShapeDtypeStruct((3, rows, columns), f32),
        jax.ShapeDtypeStruct((rows, columns), bf16),
        jax.ShapeDtypeStruct((rows, columns), bf16),
        jax.ShapeDtypeStruct((2, SEGMENTS * modes, columns), f32),
        jax.ShapeDtypeStruct((2, modes, columns), f32),
    ]
    return call(
        second_features_kernel,
        (columns // LANES,),
        [lanes(a.shape) for a in (projected, short, above, rates)],
        [lanes(s.shape) for s in shapes],
        shapes,
        [
            pltpu.VMEM((rows + EDGE, LANES), f32),
            pltpu.VMEM((rows, LANES), f32),
            pltpu.VMEM((rows, LANES), f32),
            pltpu.VMEM((modes, LANES), f32),
        ],
        100 * rows * columns,
        24 * rows * columns,
    )(projected, short, above, rates)


def second_filter_kernel(
    shards, seq_ref, feature_ref, gated_ref, signal_ref, segment_ref, closing_ref, rate_ref,
    residue_ref, above_ref, middle_ref,
    out_ref, grad_ref, entering, source, filtered, grad_gated, decay, residue,
):
    rows = above_ref.shape[0]
    modes = rate_ref.shape[0]
    length = rows // SEGMENTS
    me = seq_ref[0]
    rates = rate_ref[...]
    decay[...] = jnp.exp(-rates)
    residue[...] = residue_ref[...]
    stride = jnp.exp(-rates * length)
    for way, (values, target) in enumerate(((gated_ref, filtered), (signal_ref, grad_gated))):
        source[...] = values[...].astype(f32)
        state = jnp.zeros((modes, LANES), f32)
        for shard in range(shards):
            ahead = me - 1 - shard if way == 0 else shard - me - 1
            weight = jnp.exp(-rates * (rows * jnp.maximum(ahead, 0)).astype(f32))
            state = state + jnp.where(ahead >= 0, weight * closing_ref[shard, way], 0.0)
        for n in range(SEGMENTS):
            at = n if way == 0 else SEGMENTS - 1 - n
            entering[at * modes : (at + 1) * modes, :] = state
            state = stride * state + segment_ref[way, at * modes : (at + 1) * modes, :]
        starts = [entering[pl.ds(m, SEGMENTS, stride=modes), :] for m in range(modes)]
        scan_modes(
            source, spread(decay, modes), starts, length, way == 0, spread(residue, modes), target
        )
    above = above_ref[...].astype(f32)
    out_ref[...] = (middle_ref[EDGE:, :].astype(f32) + feature_ref[0] * filtered[...]).astype(bf16)
    grad_ref[0] = (above * filtered[...]).astype(bf16)
    grad_ref[1] = (grad_gated[...] * feature_ref[2]).astype(bf16)
    grad_ref[2] = (grad_gated[...] * feature_ref[1]).astype(bf16)


def second_filter(seq, features, gated, signal, segments, closings, rates, residues, above, middle):
    rows, columns = above.shape
    modes = rates.shape[0]
    shapes = [
        jax.ShapeDtypeStruct((rows, columns), bf16),
        jax.ShapeDtypeStruct((3, rows, columns), bf16),
    ]
    operands = (features, gated, signal, segments, closings, rates, residues, above, middle)
    return call(
        functools.partial(second_filter_kernel, closings.shape[0]),
        (columns // LANES,),
        [lanes(a.shape) for a in operands],
        [lanes(s.shape) for s in shapes],
        shapes,
        [pltpu.VMEM((SEGMENTS * modes, LANES), f32)]
        + [pltpu.VMEM((rows, LANES), f32)] * 3
        + [pltpu.VMEM((modes, LANES), f32)] * 2,
        140 * rows * columns,
        28 * rows * columns,
        prefetch=1,
    )(seq, *operands)


def second_grads_kernel(grad_ref, halo_ref, p_ref, short_ref, scale_ref, out_ref, term_ref, held):
    rows = grad_ref.shape[1]
    scale = scale_ref[...]
    terms = None
    for j in range(3):
        held[:rows, :] = grad_ref[j].astype(f32)
        held[rows:, :] = halo_ref[j].astype(f32)
        grad = short_sum(held, short_ref, j, 0, rows, 1)
        term = grad * p_ref[j, EDGE:, :].astype(f32)
        terms = term if terms is None else terms + term
        out_ref[j] = (grad * scale).astype(bf16)
    total = jnp.sum(terms, axis=1, keepdims=True)

    @pl.when(pl.program_id(0) == 0)
    def _():
        term_ref[...] = total

    @pl.when(pl.program_id(0) > 0)
    def _():
        term_ref[...] += total


def second_grads(grads, halo, projected, short, scale):
    _, rows, columns = grads.shape
    shapes = [
        jax.ShapeDtypeStruct((3, rows, columns), bf16),
        jax.ShapeDtypeStruct((rows, 1), f32),
    ]
    return call(
        second_grads_kernel,
        (columns // LANES,),
        [lanes(a.shape) for a in (grads, halo, projected, short)] + [whole((rows, 1))],
        [lanes(shapes[0].shape), whole((rows, 1))],
        shapes,
        [pltpu.VMEM((rows + EDGE, LANES), f32)],
        60 * rows * columns,
        24 * rows * columns,
    )(grads, halo, projected, short, scale)


def shift(value, axis, by):
    devices = lax.axis_size(axis)
    pairs = [(i, i + by) for i in range(devices) if 0 <= i + by < devices]
    return lax.ppermute(value, axis, pairs)


def gather_ch(value):
    return lax.all_gather(value, "ch", axis=0, tiled=False)


def scatter_ch(value):
    return lax.psum_scatter(value, "ch", scatter_dimension=0, tiled=False)


def exchange_seq(value):
    return lax.all_to_all(value, "seq", split_axis=0, concat_axis=0, tiled=True)


def gather_seq(value):
    return exchange_seq(jnp.broadcast_to(value[None], (lax.axis_size("seq"),) + value.shape))


def seq_ring():
    devices = lax.axis_size("seq")
    if devices % 2:
        return list(range(devices))
    return list(range(0, devices, 2)) + list(range(devices - 1, 0, -2))


def seq_hop(value, by):
    ring = seq_ring()
    pairs = [(ring[i], ring[(i + by) % len(ring)]) for i in range(len(ring))]
    return lax.ppermute(value, "seq", pairs)


def ring_order():
    ring = seq_ring()
    twice = jnp.array(ring + ring, jnp.int32)
    place = jnp.argmax(twice[: len(ring)] == lax.axis_index("seq")).astype(jnp.int32)
    return lax.dynamic_slice_in_dim(twice, place, len(ring), 0)


def ch_hop(value, by):
    devices = lax.axis_size("ch")
    pairs = [(i, (i + 2 * by) % devices) for i in range(devices)]
    return lax.ppermute(value, "ch", pairs)


def sibling(value):
    return lax.ppermute(value, "ch", [(i, i ^ 1) for i in range(lax.axis_size("ch"))])


def scatter_order():
    devices = lax.axis_size("ch")
    me = lax.axis_index("ch")
    places = jnp.arange(devices // 2, dtype=jnp.int32)
    return jnp.concatenate([(2 * places + other) % devices for other in (me, me ^ 1)])


def added(*terms):
    return functools.reduce(lambda a, b: a + b, [t.astype(f32) for t in terms])


def ring_scatter(pieces):
    half = pieces.shape[0] // 2
    mine = added(pieces[:half], sibling(pieces[half:])).astype(bf16)
    if half == 1:
        return mine[0].astype(f32)
    steps = (half - 1) // 2
    rows = mine.shape[1]
    middle = rows // 32 * 16
    up = down = None
    if half % 2 == 0:
        far = mine[half // 2]
        up, down = ch_hop(far[:middle], 1), ch_hop(far[middle:], -1)
        if half == 2:
            return added(mine[0], jnp.concatenate([up, down], axis=0))
    for step in range(steps, 0, -1):
        first, second = mine[step], mine[half - step]
        if up is not None and step == steps and half % 2 == 0:
            first = jnp.concatenate(
                [added(first[:middle], up).astype(bf16), first[middle:]], axis=0
            )
            second = jnp.concatenate(
                [second[:middle], added(second[middle:], down).astype(bf16)], axis=0
            )
        elif up is not None:
            first, second = added(first, up).astype(bf16), added(second, down).astype(bf16)
        up, down = ch_hop(first, 1), ch_hop(second, -1)
    return added(mine[0], up, down)


def tie(*values):
    return lax.optimization_barrier(values)


def per_device(
    token_ids,
    embedding,
    gain_first,
    gain_second,
    weights_first,
    weights_second,
    short_first,
    short_second,
    medium,
    residues,
    decay_rates,
    cotangent,
):
    shards = lax.axis_size("seq")
    pieces = lax.axis_size("ch")
    seq = lax.axis_index("seq")
    vocab, width = embedding.shape
    rows = token_ids.shape[0]
    features = width * pieces
    taps, tap_count = medium.shape[0], short_first.shape[0]
    front = round_up(EDGE + taps - 1 + tap_count - 1, 16)
    back = round_up(EDGE + taps - 1, 16)
    w_first, w_second = (jnp.transpose(w, (1, 0, 2)) for w in (weights_first, weights_second))
    s_first, s_second = (jnp.transpose(s, (1, 0, 2)) for s in (short_first, short_second))

    order = ring_order()
    each = pieces // shards
    share = vocab // shards
    at = seq * share

    gains = jnp.concatenate(
        [gain_first[None], gain_second[None], jnp.zeros((EDGE - 2, width), bf16)], axis=0
    )
    own_embedding = lax.dynamic_slice_in_dim(embedding, at, share, 0)
    gathered = gather_ch(jnp.concatenate([own_embedding, gains], axis=0))
    tokens = lax.all_gather(token_ids, "seq", axis=0, tiled=True)
    tokens, gathered = tie(tokens, gathered)
    gains_first = gathered[:, share : share + 1, :].astype(f32)
    gains_second = gathered[:, share + 1 : share + 2, :].astype(f32)
    own_table, own_scale = project(gathered, gains_first, w_first, share)
    table = gather_seq(own_table)

    tokens = jnp.pad(tokens, (front, back), constant_values=-1)
    tokens = lax.dynamic_slice_in_dim(tokens, seq * rows, front + rows + back, 0)
    middle, features_first, filtered_first = first_forward(
        tokens[:, None], table, embedding, s_first, medium, rows, front
    )

    middles = gather_ch(middle)
    block = exchange_seq(gathered[:, :share, :].reshape(shards, each, share, width))
    block, middles = tie(block, middles)
    core = lax.axis_index("ch") % each
    own = middles[:, EDGE:, :].reshape(shards, each, rows, width)
    own = lax.dynamic_index_in_dim(own, core, 1, keepdims=False)
    columns = exchange_seq(own)
    projected, scale = project(middles, gains_second, w_second, rows + EDGE)
    features_second, gated, signal, segments, closing = second_features(
        projected, s_second, cotangent, decay_rates
    )
    columns, closing = tie(columns, closing)
    closings = gather_seq(closing)
    other = sibling(columns)
    columns = jnp.where(
        core == 0, jnp.stack([columns, other], axis=1), jnp.stack([other, columns], axis=1)
    )
    output, grad_featured = second_filter(
        seq[None], features_second, gated, signal, segments, closings,
        decay_rates, residues, cotangent, middle,
    )
    halo = shift(grad_featured[:, :EDGE, :], "seq", -1)
    scale = scale[EDGE:]
    grads, terms = second_grads(grad_featured, halo, projected, s_second, scale)
    pieces_of = [(0, 0, grads)]
    up = down = grads
    for step in range(1, (shards + 1) // 2):
        up, down = seq_hop(up, 1), seq_hop(down, -1)
        pieces_of += [(shards - step, 0, up), (step, 0, down)]
    partial = project_back(grads, w_second, jnp.arange(pieces, dtype=jnp.int32))
    partial_sum = scatter_ch(partial)
    terms = lax.psum(terms[:, 0], "ch")
    partial_sum, *arrays = tie(partial_sum, *[array for _, _, array in pieces_of[1:]])
    pieces_of[1:] = [old[:2] + (new,) for old, new in zip(pieces_of[1:], arrays)]
    grad_normed = partial_sum.astype(f32)
    as_float = middle[EDGE:].astype(f32)
    grad_middle = (
        cotangent.astype(f32)
        + gain_second.astype(f32) * grad_normed
        - as_float * (scale * scale) * terms[:, None] / features
    ).astype(bf16)
    grad_gain_second = jnp.sum(grad_normed * as_float, axis=0)

    above = jnp.concatenate([grad_middle, shift(grad_middle[:back], "seq", -1)], axis=0)
    if shards % 2 == 0:
        half = rows // 2
        if shards > 2:
            up, down = pieces_of[-2][2], pieces_of[-1][2]
        above, up, down = tie(above, up, down)
        up, down = seq_hop(up[:, :half], 1), seq_hop(down[:, half:], -1)
        pieces_of += [(shards // 2, 0, up), (shards // 2, half, down)]
    sums, others = first_backward(
        token_ids[None], above, features_first, filtered_first, s_first, medium, vocab, shards
    )
    sums = exchange_seq(sums)
    block_gains = lax.dynamic_slice_in_dim(gains_second, seq * each, each, 0)
    grad_weights_second = weight_grad(columns, pieces_of, order, jnp.swapaxes(block_gains, 1, 2))
    sums, grad_weights_second = tie(sums, grad_weights_second)
    own_sums = jnp.sum(sums.astype(f32), axis=0)
    terms = jnp.sum(own_sums * own_table.astype(f32), axis=(0, 2))
    own_grads = (own_sums * own_scale[None]).astype(bf16)
    extra_rows = -(-share // width)
    extra = jnp.pad(terms, (0, EDGE * width - share)).reshape(EDGE, width).astype(bf16)
    partial = project_back(own_grads, w_first, scatter_order(), extra)
    grad_normed = ring_scatter(partial)
    terms = grad_normed[share : share + extra_rows].reshape(-1)[:share]
    grad_normed = grad_normed[:share]
    own_others = jnp.sum(exchange_seq(others).astype(f32), axis=0)
    all_grads = gather_seq(own_grads)
    block_gains = lax.dynamic_slice_in_dim(gains_first, seq * each, each, 0)
    grad_weights_first = weight_grad(
        block,
        [(shard, 0, all_grads[shard]) for shard in range(shards)],
        jnp.arange(shards, dtype=jnp.int32),
        jnp.swapaxes(block_gains, 1, 2),
    )

    as_float = own_embedding.astype(f32)
    grad_embedding = (
        own_others
        + gain_first.astype(f32) * grad_normed
        - as_float * (own_scale * own_scale) * terms[:, None] / features
    )
    grad_gain_first = jnp.sum(grad_normed * as_float, axis=0)
    last = jnp.concatenate(
        [
            grad_embedding,
            grad_gain_first[None],
            grad_gain_second[None],
            jnp.zeros((EDGE - 2, width), f32),
        ],
        axis=0,
    ).astype(bf16)
    last = gather_seq(last).astype(f32)
    return (
        output,
        last[:, :share].reshape(vocab, width),
        jnp.sum(last[:, share], axis=0),
        jnp.sum(last[:, share + 1], axis=0),
        jnp.transpose(grad_weights_first, (1, 0, 2)),
        jnp.transpose(grad_weights_second, (1, 0, 2)),
    )


def solution(mesh):
    placed = (
        P("seq"),
        P(None, "ch"),
        P("ch"),
        P("ch"),
        P(None, None, "ch"),
        P(None, None, "ch"),
        P(None, None, "ch"),
        P(None, None, "ch"),
        P(None, "ch"),
        P(None, "ch"),
        P(None, "ch"),
        P("seq", "ch"),
    )
    return jax.shard_map(
        per_device,
        mesh=mesh,
        in_specs=placed,
        out_specs=(
            P("seq", "ch"),
            P(None, "ch"),
            P("ch"),
            P("ch"),
            P("seq", None, "ch"),
            P("seq", None, "ch"),
        ),
        check_vma=False,
    )
```

```python
import functools

import jax
import jax.numpy as jnp
from jax import lax
from jax.experimental import pallas as pl
from jax.experimental.pallas import tpu as pltpu
from jax.sharding import PartitionSpec as P

epsilon = 1e-06
f32 = jnp.float32
bf16 = jnp.bfloat16
LANES = 128
EDGE = 16
VECTOR = 160


def round_up(value, multiple):
    return -(-value // multiple) * multiple


def call(kernel, grid, in_specs, out_specs, out_shape, scratch, flops, moved, prefetch=0, mib=54):
    return pl.pallas_call(
        kernel,
        grid_spec=pltpu.PrefetchScalarGridSpec(
            num_scalar_prefetch=prefetch,
            grid=grid,
            in_specs=in_specs,
            out_specs=out_specs,
            scratch_shapes=scratch,
        ),
        out_shape=out_shape,
        compiler_params=pltpu.CompilerParams(vmem_limit_bytes=mib * 2**20),
        cost_estimate=pl.CostEstimate(flops=flops, bytes_accessed=moved, transcendentals=0),
    )


def whole(shape):
    return pl.BlockSpec(shape, lambda i, *_: (0,) * len(shape))


def lanes(shape):
    return pl.BlockSpec(shape[:-1] + (LANES,), lambda i, *_: (0,) * (len(shape) - 1) + (i,))


def project_kernel(
    per_step, features, rows, gain_row, x_ref, gain_ref, w_ref, p_ref, scale_ref, total, squares
):
    step = pl.program_id(0)
    width = x_ref.shape[2]

    @pl.when(step == 0)
    def _():
        total[...] = jnp.zeros_like(total)
        squares[...] = jnp.zeros_like(squares)

    for part in range(per_step):
        x = x_ref[part, :rows, :].astype(f32)
        square = x * x
        running = squares[...]
        for lane in range(width // LANES):
            running = running + square[:, lane * LANES : (lane + 1) * LANES]
        squares[...] = running
        gain = gain_ref[part, gain_row : gain_row + 1, :].astype(f32)
        scaled = (x * gain).astype(bf16)
        for j in range(3):
            total[j] += jnp.dot(
                scaled, w_ref[j, part * width : (part + 1) * width, :], preferred_element_type=f32
            )

    @pl.when(step == pl.num_programs(0) - 1)
    def _():
        mean = jnp.sum(squares[...], axis=1, keepdims=True) / features
        scale = lax.rsqrt(mean + epsilon)
        scale_ref[...] = scale
        for j in range(3):
            p_ref[j] = (total[j] * scale).astype(bf16)


def project(chunks, gains, gain_block, gain_row, weights, rows):
    count, _, width = chunks.shape
    features, columns = weights.shape[1:]
    per_step = 2 if count % 2 == 0 else 1
    return call(
        functools.partial(project_kernel, per_step, features, rows, gain_row),
        (count // per_step,),
        [
            pl.BlockSpec((per_step, chunks.shape[1], width), lambda i: (i, 0, 0)),
            pl.BlockSpec((per_step, EDGE, width), lambda i: (i, gain_block // EDGE, 0)),
            pl.BlockSpec((3, per_step * width, columns), lambda i: (0, i, 0)),
        ],
        [whole((3, rows, columns)), whole((rows, 1))],
        [
            jax.ShapeDtypeStruct((3, rows, columns), bf16),
            jax.ShapeDtypeStruct((rows, 1), f32),
        ],
        [pltpu.VMEM((3, rows, columns), f32), pltpu.VMEM((rows, LANES), f32)],
        6 * rows * features * columns,
        6 * features * columns + 2 * rows * features,
    )(chunks, gains, weights)


def back_kernel(parts, order_ref, *refs):
    g_refs, w_refs = refs[:parts], refs[parts : parts + 2]
    extra_ref, o_ref, grads = refs[parts + 2 :]
    rows, columns = grads.shape[0], grads.shape[1] // 3

    @pl.when(pl.program_id(0) == 0)
    def _():
        first = 0
        for g_ref in g_refs:
            more = g_ref.shape[1]
            for j in range(3):
                grads[first : first + more, j * columns : (j + 1) * columns] = g_ref[j]
            first += more

    for piece, w_ref in enumerate(w_refs):
        weights = jnp.concatenate([w_ref[j] for j in range(3)], axis=1)
        o_ref[piece, :rows, :] = lax.dot_general(
            grads[...], weights, (((1,), (1,)), ((), ())), preferred_element_type=f32
        ).astype(bf16)
        if o_ref.shape[1] > rows:
            o_ref[piece, rows:, :] = extra_ref[...]


def project_back(parts, weights, order, extra=None):
    columns = parts[0].shape[2]
    rows = sum(part.shape[1] for part in parts)
    features = weights.shape[1]
    count = order.shape[0]
    width = features // count
    more = 0 if extra is None else extra.shape[0]
    if extra is None:
        extra = jnp.zeros((EDGE, width), bf16)
    return call(
        functools.partial(back_kernel, len(parts)),
        (count // 2,),
        [whole(part.shape) for part in parts]
        + [
            pl.BlockSpec((3, width, columns), lambda i, order: (0, order[2 * i], 0)),
            pl.BlockSpec((3, width, columns), lambda i, order: (0, order[2 * i + 1], 0)),
            whole(extra.shape),
        ],
        pl.BlockSpec((2, rows + more, width), lambda i, *_: (i, 0, 0)),
        jax.ShapeDtypeStruct((count, rows + more, width), bf16),
        [pltpu.VMEM((rows, 3 * columns), bf16)],
        6 * rows * features * columns,
        6 * features * columns + 2 * rows * features,
        prefetch=1,
    )(order, *parts, weights, weights, extra)


def weight_grad_kernel(spans, pieces, order_ref, piece_ref, gain_ref, *refs):
    x_refs, g_refs, out_ref = refs[:pieces], refs[pieces:-1], refs[-1]

    for piece, x_ref in enumerate(x_refs):

        @pl.when(pl.program_id(0) == piece)
        def _(x_ref=x_ref):
            for j in range(3):
                total = None
                for (slot, first), g_ref in zip(spans, g_refs):
                    some = x_ref[order_ref[slot], first : first + g_ref.shape[1], :]
                    term = lax.dot_general(
                        some, g_ref[j], (((0,), (0,)), ((), ())), preferred_element_type=f32
                    )
                    total = term if total is None else total + term
                out_ref[j] = total * gain_ref[0]


def weight_grad(columns, places, grads, order, gains):
    shards, rows, width = columns[0].shape
    pieces = len(columns)
    out = grads[0][2].shape[2]
    arrays = [array for _, _, array in grads]
    return call(
        functools.partial(weight_grad_kernel, [(slot, first) for slot, first, _ in grads], pieces),
        (pieces,),
        [pl.BlockSpec((1, width, 1), lambda i, order, places: (places[i], 0, 0))]
        + [whole(array.shape) for array in list(columns) + arrays],
        pl.BlockSpec((3, width, out), lambda i, order, places: (0, places[i], 0)),
        jax.ShapeDtypeStruct((3, pieces * width, out), f32),
        [],
        6 * shards * pieces * rows * width * out,
        2 * shards * pieces * rows * width + 6 * shards * rows * out + 12 * pieces * width * out,
        prefetch=2,
    )(order, places, gains, *columns, *arrays)


def fir(source, taps, target, mixed, mixed_taps, base, rows, forward):
    stride = rows // 8
    steps = stride // 4
    tap_count = taps.shape[0]
    quarter = tap_count // 4
    span = steps + quarter

    def row(position):
        return base + (position if forward else stride - 1 - position)

    def combine(x):
        even, odd, low, high = x[0] + x[2], x[1] + x[3], x[0] + x[1], x[2] + x[3]
        return [x[0], x[2], even, x[1], x[3], odd, low, high, even + odd]

    def mix(n, carry):
        first = 4 * (n - quarter)
        values = [source[pl.ds(row(first + p), 8, stride=stride), :] for p in range(4)]
        for c, value in enumerate(combine(values)):
            mixed[c, n] = value
        return carry

    lax.fori_loop(0, span, mix, 0, unroll=7 if span % 7 == 0 else 1)
    for c, value in enumerate(combine([taps[pl.ds(p, quarter, stride=4), :] for p in range(4)])):
        mixed_taps[c * quarter : (c + 1) * quarter, :] = value

    chunk = 8
    outs = steps + 1

    def product(c, carry):
        sums = [jnp.zeros((8, LANES), f32)] * outs
        for k0 in range(0, quarter, chunk):
            loaded = [mixed[c, quarter - 1 - k0 - (chunk - 1) + n] for n in range(outs + chunk - 1)]
            for k in range(chunk):
                tap = mixed_taps[pl.ds(c * quarter + k0 + k, 1), :]
                for p in range(outs):
                    sums[p] = sums[p] + tap * loaded[p + chunk - 1 - k]
        for p in range(outs):
            mixed[c, p] = sums[p]
        return carry

    lax.fori_loop(0, 9, product, 0, unroll=3)

    def finish(p, carry):
        now = [mixed[c, p + 1] for c in range(9)]
        old = [mixed[c, p] for c in range(6)]
        even_0, even_1 = now[0] + old[1], now[2] - now[0] - now[1]
        odd_0, odd_1 = now[3] + old[4], now[5] - now[3] - now[4]
        odd_old = old[5] - old[3] - old[4]
        both_0, both_1 = now[6] + mixed[7, p], now[8] - now[6] - now[7]
        values = [even_0 + odd_old, both_0 - even_0 - odd_0, even_1 + odd_0, both_1 - even_1 - odd_1]
        for n, value in enumerate(values):
            target[pl.ds(row(4 * p + n) - base, 8, stride=stride), :] = value
        return carry

    lax.fori_loop(0, steps, finish, 0, unroll=True)


def fir_scratch(rows, tap_count):
    return [
        pltpu.VMEM((9, rows // 32 + tap_count // 4, 8, LANES), f32),
        pltpu.VMEM((9 * tap_count // 4, LANES), f32),
    ]


def short_sum(source, short, j, first, rows, sign):
    total = None
    for i in range(short.shape[1]):
        term = short[j, i : i + 1, :] * source[first + sign * i : first + sign * i + rows, :]
        total = term if total is None else total + term
    return total


def look_up(token_ref, onehot):
    grid = lax.broadcasted_iota(jnp.int32, onehot.shape, 1)
    onehot[...] = (grid == token_ref[...]).astype(f32).astype(bf16)


def first_forward_kernel(
    front, rows, places, token_ref, e_ref, short_ref, medium_ref, *refs,
):
    p_refs = refs[: len(places)]
    middle_ref, filtered_ref = refs[len(places) : len(places) + 2]
    onehot, table, projected, gated, taps, kept, *mixed = refs[len(places) + 2 :]
    window, vocab = onehot.shape

    @pl.when(pl.program_id(0) == 0)
    def _():
        look_up(token_ref, onehot)

    taps[...] = medium_ref[...].astype(f32)
    extended = rows + 2 * EDGE
    for j in range(3):
        for place, p_ref in zip(places, p_refs):
            table[place : place + p_ref.shape[1], j * LANES : (j + 1) * LANES] = p_ref[j]
    looked = jnp.dot(onehot[...], table[...], preferred_element_type=f32)
    product = None
    for j in (1, 2, 0):
        projected[...] = looked[:, j * LANES : (j + 1) * LANES]
        if j == 0:
            kept[...] = short_sum(projected, short_ref, j, front - EDGE, extended, -1)
        else:
            feature = short_sum(projected, short_ref, j, 8, window - 8, -1)
            product = feature if product is None else product * feature
    gated[8:, :] = product.astype(bf16).astype(f32)
    fir(gated, taps, projected, *mixed, front - EDGE, extended, True)
    filtered = projected[:extended, :]
    filtered_ref[...] = filtered[EDGE:, :]
    embedded = jnp.dot(onehot[front - EDGE :, :], e_ref[...], preferred_element_type=f32)
    middle_ref[...] = (embedded + kept[...] * filtered).astype(bf16)


def first_forward(tokens, tables, embedding, short, medium, rows, front):
    share = tables[0][2].shape[1]
    places = [slot * share + first for slot, first, _ in tables]
    tables = [table for _, _, table in tables]
    extended = rows + 2 * EDGE
    window = front + rows + EDGE
    vocab, columns = embedding.shape
    shapes = [
        jax.ShapeDtypeStruct((extended, columns), bf16),
        jax.ShapeDtypeStruct((rows + EDGE, columns), f32),
    ]
    return call(
        functools.partial(first_forward_kernel, front, rows, places),
        (columns // LANES,),
        [pl.BlockSpec((window, 1), lambda i, *_: (0, 0))]
        + [lanes(a.shape) for a in (embedding, short, medium, *tables)],
        [lanes(s.shape) for s in shapes],
        shapes,
        [
            pltpu.VMEM((window, vocab), bf16),
            pltpu.VMEM((vocab, 3 * LANES), bf16),
            pltpu.VMEM((window, LANES), f32),
            pltpu.VMEM((window, LANES), f32),
            pltpu.VMEM((medium.shape[0], LANES), f32),
            pltpu.VMEM((extended, LANES), f32),
        ]
        + fir_scratch(extended, medium.shape[0]),
        8 * window * vocab * columns + 250 * VECTOR * rows * columns,
        8 * window * columns,
    )(tokens[:window], embedding, short, medium, *tables)


def first_features_kernel(places, token_ref, short_ref, *refs):
    p_refs = refs[: len(places)]
    feature_ref, onehot, table, projected = refs[len(places) :]

    @pl.when(pl.program_id(0) == 0)
    def _():
        look_up(token_ref, onehot)

    for j in range(3):
        for place, p_ref in zip(places, p_refs):
            table[place : place + p_ref.shape[1], :] = p_ref[j]
        projected[...] = jnp.dot(onehot[...], table[...], preferred_element_type=f32)
        feature_ref[j] = short_sum(projected, short_ref, j, EDGE, feature_ref.shape[1], -1)


def first_features(tokens, tables, short):
    share = tables[0][2].shape[1]
    places = [slot * share + first for slot, first, _ in tables]
    vocab = share * (1 + max(slot for slot, _, _ in tables))
    tables = [table for _, _, table in tables]
    window = tokens.shape[0]
    columns = tables[0].shape[2]
    shape = jax.ShapeDtypeStruct((3, window - EDGE, columns), f32)
    return call(
        functools.partial(first_features_kernel, places),
        (columns // LANES,),
        [whole((window, 1))] + [lanes(a.shape) for a in (short, *tables)],
        lanes(shape.shape),
        shape,
        [
            pltpu.VMEM((window, vocab), bf16),
            pltpu.VMEM((vocab, LANES), bf16),
            pltpu.VMEM((window, LANES), f32),
        ],
        6 * window * vocab * columns + 50 * VECTOR * window * columns,
        16 * window * columns,
    )(tokens, short, *tables)


def first_backward_kernel(
    rows, token_ref, above_ref, halo_ref, feature_ref, filtered_ref, short_ref, medium_ref,
    out_ref, onehot, signal, grad_gated, taps, held, *mixed,
):
    vocab = onehot.shape[0]
    parts = out_ref.shape[0]

    @pl.when(pl.program_id(0) == 0)
    def _():
        grid = lax.broadcasted_iota(jnp.int32, (vocab, rows), 0)
        onehot[...] = (grid == token_ref[...]).astype(f32).astype(bf16)

    taps[...] = medium_ref[...].astype(f32)
    extended = rows + EDGE
    above = jnp.concatenate([above_ref[...], halo_ref[...]], axis=0).astype(f32)
    signal[...] = (above * feature_ref[0]).astype(bf16).astype(f32)
    fir(signal, taps, grad_gated, *mixed, 0, extended + EDGE, False)

    def keep(j, value):
        held[...] = value.astype(bf16).astype(f32)
        grad = short_sum(held, short_ref, j, 0, rows, 1).astype(bf16)
        total = jnp.dot(onehot[...], grad, preferred_element_type=f32).astype(bf16)
        for part in range(parts):
            size = vocab // parts
            out_ref[part, j] = total[part * size : (part + 1) * size, :]

    keep(0, above[:extended, :] * filtered_ref[...])
    keep(1, grad_gated[:extended, :] * feature_ref[2, :extended, :])
    keep(2, grad_gated[:extended, :] * feature_ref[1, :extended, :])
    total = jnp.dot(onehot[...], above_ref[...], preferred_element_type=f32).astype(bf16)
    for part in range(parts):
        size = vocab // parts
        out_ref[part, 3] = total[part * size : (part + 1) * size, :]


def first_backward(tokens, above, halo, features, filtered, short, medium, vocab, parts):
    rows, columns = above.shape
    later = rows + halo.shape[0]
    operands = (above, halo, features, filtered, short, medium)
    shape = jax.ShapeDtypeStruct((parts, 4, vocab // parts, columns), bf16)
    return call(
        functools.partial(first_backward_kernel, rows),
        (columns // LANES,),
        [whole((1, rows))] + [lanes(a.shape) for a in operands],
        lanes(shape.shape),
        shape,
        [
            pltpu.VMEM((vocab, rows), bf16),
            pltpu.VMEM((later, LANES), f32),
            pltpu.VMEM((rows + 2 * EDGE, LANES), f32),
            pltpu.VMEM((medium.shape[0], LANES), f32),
            pltpu.VMEM((rows + EDGE, LANES), f32),
        ]
        + fir_scratch(rows + 2 * EDGE, medium.shape[0]),
        8 * rows * vocab * columns + 250 * VECTOR * rows * columns,
        16 * later * columns,
    )(tokens, *operands)


SEGMENTS = 8
SHIFT = 8


def summed(terms):
    while len(terms) > 1:
        terms = [a + b for a, b in zip(terms[::2], terms[1::2])] + terms[len(terms) // 2 * 2 :]
    return terms[0]


def scan_modes(source, decays, states, length, forward, residues=None, target=None):
    first = 0 if forward else SHIFT

    def step(i, held):
        position = first + (i if forward else length - 1 - i)
        value = source[pl.ds(position, SEGMENTS, stride=length), :]
        held = tuple(d * s + value for d, s in zip(decays, held))
        if target is not None:
            target[pl.ds(position, SEGMENTS, stride=length), :] = summed(
                [r * s for r, s in zip(residues, held)]
            )
        return held

    return lax.fori_loop(0, length, step, tuple(states), unroll=4)


def spread(ref, count):
    return [jnp.broadcast_to(ref[m : m + 1, :], (SEGMENTS, LANES)) for m in range(count)]


def second_features_kernel(
    p_ref, short_ref, above_ref, rate_ref,
    feature_ref, gated_ref, signal_ref, segment_ref, closing_ref, projected, gated, signal, decay,
):
    extended = above_ref.shape[0]
    modes = rate_ref.shape[0]
    length = (extended - EDGE) // SEGMENTS
    product = None
    for j in range(3):
        projected[...] = p_ref[j].astype(f32)
        feature = short_sum(projected, short_ref, j, EDGE, extended, -1)
        feature_ref[j] = feature
        if j == 0:
            rounded = (above_ref[...].astype(f32) * feature).astype(bf16)
            signal_ref[...] = rounded
            signal[...] = rounded.astype(f32)
        else:
            product = feature if product is None else product * feature
    rounded = product.astype(bf16)
    gated_ref[...] = rounded
    gated[...] = rounded.astype(f32)
    rates = rate_ref[...]
    decay[...] = jnp.exp(-rates)
    zeros = [jnp.zeros((SEGMENTS, LANES), f32)] * modes
    for way, source in enumerate((gated, signal)):
        ends = scan_modes(source, spread(decay, modes), zeros, length, way == 0)
        for m in range(modes):
            segment_ref[way, pl.ds(m, SEGMENTS, stride=modes), :] = ends[m]
        stride = jnp.exp(-rates * length)
        total = jnp.zeros((modes, LANES), f32)
        for n in range(SEGMENTS):
            at = n if way == 0 else SEGMENTS - 1 - n
            total = stride * total + segment_ref[way, at * modes : (at + 1) * modes, :]
        closing_ref[way] = total


def second_features(projected, short, above, rates):
    extended, columns = above.shape
    modes = rates.shape[0]
    shapes = [
        jax.ShapeDtypeStruct((3, extended, columns), f32),
        jax.ShapeDtypeStruct((extended, columns), bf16),
        jax.ShapeDtypeStruct((extended, columns), bf16),
        jax.ShapeDtypeStruct((2, SEGMENTS * modes, columns), f32),
        jax.ShapeDtypeStruct((2, modes, columns), f32),
    ]
    return call(
        second_features_kernel,
        (columns // LANES,),
        [lanes(a.shape) for a in (projected, short, above, rates)],
        [lanes(s.shape) for s in shapes],
        shapes,
        [
            pltpu.VMEM((extended + EDGE, LANES), f32),
            pltpu.VMEM((extended, LANES), f32),
            pltpu.VMEM((extended, LANES), f32),
            pltpu.VMEM((modes, LANES), f32),
        ],
        120 * VECTOR * extended * columns,
        24 * extended * columns,
    )(projected, short, above, rates)


def second_filter_kernel(
    shards, seq_ref, feature_ref, gated_ref, signal_ref, segment_ref, closing_ref, rate_ref,
    residue_ref, above_ref, middle_ref, p_ref, short_ref, scale_ref,
    out_ref, top_ref, bottom_ref, term_ref,
    entering, source, filtered, grad_gated, decay, residue, ends, held,
):
    rows = out_ref.shape[0]
    modes = rate_ref.shape[0]
    length = rows // SEGMENTS
    reach = rows + SHIFT
    me = seq_ref[0]
    rates = rate_ref[...]
    decay[...] = jnp.exp(-rates)
    residue[...] = residue_ref[...]
    stride = jnp.exp(-rates * length)
    for way, (values, target) in enumerate(((gated_ref, filtered), (signal_ref, grad_gated))):
        source[way] = values[...].astype(f32)
        state = jnp.zeros((modes, LANES), f32)
        for shard in range(shards):
            ahead = me - 1 - shard if way == 0 else shard - me - 1
            weight = jnp.exp(-rates * (rows * jnp.maximum(ahead, 0)).astype(f32))
            state = state + jnp.where(ahead >= 0, weight * closing_ref[shard, way], 0.0)
        for n in range(SEGMENTS):
            at = n if way == 0 else SEGMENTS - 1 - n
            entering[at * modes : (at + 1) * modes, :] = state
            state = stride * state + segment_ref[way, at * modes : (at + 1) * modes, :]
        ends[way] = state
        starts = [entering[pl.ds(m, SEGMENTS, stride=modes), :] for m in range(modes)]
        scan_modes(
            source.at[way], spread(decay, modes), starts, length, way == 0,
            spread(residue, modes), target,
        )

    upper = lax.broadcasted_iota(jnp.int32, (SEGMENTS, LANES), 0) < SEGMENTS // 2
    decays, residues = spread(decay, modes), spread(residue, modes)
    states = [
        jnp.where(upper, a, b)
        for a, b in zip(spread(ends.at[0], modes), spread(ends.at[1], modes))
    ]
    for i in range(SHIFT):
        after, before = rows + i, SHIFT - 1 - i
        value = jnp.where(upper, source[0, after : after + 1, :], source[1, before : before + 1, :])
        states = [d * s + value for d, s in zip(decays, states)]
        result = summed([r * s for r, s in zip(residues, states)])
        filtered[after : after + 1, :] = result[:1, :]
        grad_gated[before : before + 1, :] = result[SEGMENTS // 2 : SEGMENTS // 2 + 1, :]

    out_ref[...] = (
        middle_ref[EDGE : EDGE + rows, :].astype(f32) + feature_ref[0, :rows, :] * filtered[:rows, :]
    ).astype(bf16)
    above = above_ref[...].astype(f32)[:reach, :]
    scale = scale_ref[EDGE : EDGE + rows, :]
    terms = None
    for j in range(3):
        if j == 0:
            grad = above * filtered[...]
        else:
            grad = grad_gated[...] * feature_ref[3 - j, :reach, :]
        held[...] = grad.astype(bf16).astype(f32)
        grad = short_sum(held, short_ref, j, 0, rows, 1)
        term = grad * p_ref[j, EDGE : EDGE + rows, :].astype(f32)
        terms = term if terms is None else terms + term
        scaled = (grad * scale).astype(bf16)
        top_ref[j] = scaled[: rows // 2, :]
        bottom_ref[j] = scaled[rows // 2 :, :]
    total = jnp.sum(terms, axis=1, keepdims=True)

    @pl.when(pl.program_id(0) == 0)
    def _():
        term_ref[...] = total

    @pl.when(pl.program_id(0) > 0)
    def _():
        term_ref[...] += total


def second_filter(
    seq, features, gated, signal, segments, closings, rates, residues, above, middle, projected,
    short, scale,
):
    extended, columns = above.shape
    rows = extended - EDGE
    modes = rates.shape[0]
    shapes = [
        jax.ShapeDtypeStruct((rows, columns), bf16),
        jax.ShapeDtypeStruct((3, rows // 2, columns), bf16),
        jax.ShapeDtypeStruct((3, rows // 2, columns), bf16),
        jax.ShapeDtypeStruct((rows, 1), f32),
    ]
    operands = (
        features, gated, signal, segments, closings, rates, residues, above, middle, projected, short,
    )
    return call(
        functools.partial(second_filter_kernel, closings.shape[0]),
        (columns // LANES,),
        [lanes(a.shape) for a in operands] + [whole(scale.shape)],
        [lanes(s.shape) for s in shapes[:3]] + [whole((rows, 1))],
        shapes,
        [pltpu.VMEM((SEGMENTS * modes, LANES), f32), pltpu.VMEM((2, extended, LANES), f32)]
        + [pltpu.VMEM((rows + SHIFT, LANES), f32)] * 2
        + [pltpu.VMEM((modes, LANES), f32)] * 2
        + [pltpu.VMEM((2, modes, LANES), f32), pltpu.VMEM((rows + SHIFT, LANES), f32)],
        250 * VECTOR * rows * columns,
        40 * rows * columns,
        prefetch=1,
    )(seq, *operands, scale)


def shift(value, axis, by):
    devices = lax.axis_size(axis)
    pairs = [(i, i + by) for i in range(devices) if 0 <= i + by < devices]
    return lax.ppermute(value, axis, pairs)


def gather_ch(value):
    return lax.all_gather(value, "ch", axis=0, tiled=False)


def scatter_ch(value):
    return lax.psum_scatter(value, "ch", scatter_dimension=0, tiled=False)


def exchange_seq(value):
    return lax.all_to_all(value, "seq", split_axis=0, concat_axis=0, tiled=True)


def gather_seq(value):
    return exchange_seq(jnp.broadcast_to(value[None], (lax.axis_size("seq"),) + value.shape))


def seq_ring():
    devices = lax.axis_size("seq")
    if devices % 2:
        return list(range(devices))
    return list(range(0, devices, 2)) + list(range(devices - 1, 0, -2))


def seq_hop(value, by):
    ring = seq_ring()
    pairs = [(ring[i], ring[(i + by) % len(ring)]) for i in range(len(ring))]
    return lax.ppermute(value, "seq", pairs)


def ring_gather(parts):
    shards = lax.axis_size("seq")
    firsts = [0, parts[0].shape[1]][: len(parts)]
    out = [(0, first, part) for first, part in zip(firsts, parts)]
    up = down = parts
    for step in range(1, (shards + 1) // 2):
        up, down = [seq_hop(a, 1) for a in up], [seq_hop(a, -1) for a in down]
        out += [(shards - step, first, part) for first, part in zip(firsts, up)]
        out += [(step, first, part) for first, part in zip(firsts, down)]
    if shards % 2 == 0:
        if len(parts) == 1:
            half = parts[0].shape[1] // 2
            up, down = [up[0][:, :half]], [down[0][:, half:]]
        else:
            half = firsts[1]
        out += [(shards // 2, 0, seq_hop(up[0], 1)), (shards // 2, half, seq_hop(down[-1], -1))]
    return out


def ring_order():
    ring = seq_ring()
    twice = jnp.array(ring + ring, jnp.int32)
    place = jnp.argmax(twice[: len(ring)] == lax.axis_index("seq")).astype(jnp.int32)
    return lax.dynamic_slice_in_dim(twice, place, len(ring), 0)


def ch_hop(value, by):
    devices = lax.axis_size("ch")
    pairs = [(i, (i + 2 * by) % devices) for i in range(devices)]
    return lax.ppermute(value, "ch", pairs)


def sibling(value):
    return lax.ppermute(value, "ch", [(i, i ^ 1) for i in range(lax.axis_size("ch"))])


def scatter_order():
    devices = lax.axis_size("ch")
    me = lax.axis_index("ch")
    places = jnp.arange(devices // 2, dtype=jnp.int32)
    return jnp.concatenate([(2 * places + other) % devices for other in (me, me ^ 1)])


def added(*terms):
    return functools.reduce(lambda a, b: a + b, [t.astype(f32) for t in terms])


def ring_scatter(pieces, near, far):
    half = pieces.shape[0] // 2
    pieces, *near = tie(pieces, *near)
    mine = added(pieces[:half], sibling(pieces[half:])).astype(bf16)
    if half == 1:
        return mine[0].astype(f32), near, far
    steps = (half - 1) // 2
    rows = mine.shape[1]
    middle = rows // 32 * 16
    up = down = None
    if half % 2 == 0:
        opposite = mine[half // 2]
        up, down = ch_hop(opposite[:middle], 1), ch_hop(opposite[middle:], -1)
        if half == 2:
            return added(mine[0], jnp.concatenate([up, down], axis=0)), near, far
    for step in range(steps, 0, -1):
        first, second = mine[step], mine[half - step]
        if up is not None and step == steps and half % 2 == 0:
            first = jnp.concatenate(
                [added(first[:middle], up).astype(bf16), first[middle:]], axis=0
            )
            second = jnp.concatenate(
                [second[:middle], added(second[middle:], down).astype(bf16)], axis=0
            )
        elif up is not None:
            first, second = added(first, up).astype(bf16), added(second, down).astype(bf16)
        up, down = ch_hop(first, 1), ch_hop(second, -1)
    up, down, *far = tie(up, down, *far)
    return added(mine[0], up, down), near, far


def tie(*values):
    return lax.optimization_barrier(values)


def per_device(
    token_ids,
    embedding,
    gain_first,
    gain_second,
    weights_first,
    weights_second,
    short_first,
    short_second,
    medium,
    residues,
    decay_rates,
    cotangent,
):
    shards = lax.axis_size("seq")
    pieces = lax.axis_size("ch")
    seq = lax.axis_index("seq")
    vocab, width = embedding.shape
    rows = token_ids.shape[0]
    features = width * pieces
    taps, tap_count = medium.shape[0], short_first.shape[0]
    front = round_up(EDGE + taps - 1 + tap_count - 1, 16)
    back = round_up(2 * EDGE + taps - 1, 16)
    w_first, w_second = (jnp.transpose(w, (1, 0, 2)) for w in (weights_first, weights_second))
    s_first, s_second = (jnp.transpose(s, (1, 0, 2)) for s in (short_first, short_second))

    order = ring_order()
    each = pieces // shards
    share = vocab // shards
    at = seq * share

    gains = jnp.concatenate(
        [gain_first[None], gain_second[None], jnp.zeros((EDGE - 2, width), bf16)], axis=0
    )
    own_embedding = lax.dynamic_slice_in_dim(embedding, at, share, 0)
    gathered = gather_ch(jnp.concatenate([own_embedding, gains], axis=0))
    tokens = lax.all_gather(token_ids, "seq", axis=0, tiled=True)
    slots = jnp.zeros(shards, jnp.int32).at[order].set(jnp.arange(shards, dtype=jnp.int32))
    turned = jnp.take(embedding.reshape(shards, share, width), order, axis=0)
    turned = turned.reshape(vocab, width)
    tokens = jnp.take(slots, tokens // share) * share + tokens % share
    tokens = jnp.pad(tokens, (front, back), constant_values=-1)
    tokens = lax.dynamic_slice_in_dim(tokens, seq * rows, front + rows + back, 0)
    behind = shift(cotangent[:EDGE], "seq", -1)
    cotangents = jnp.concatenate([cotangent, behind], axis=0)
    tokens, turned, cotangents, gathered = tie(tokens[:, None], turned, cotangents, gathered)
    gains_first = gathered[:, share : share + 1, :].astype(f32)
    gains_second = gathered[:, share + 1 : share + 2, :].astype(f32)
    own_table, own_scale = project(gathered, gathered, share, 0, w_first, share)
    tables = ring_gather([own_table])

    middle, filtered_first = first_forward(tokens, tables, turned, s_first, medium, rows, front)
    later, held = tie(tokens[front - EDGE :], middle)
    features_first = first_features(later, tables, s_first)

    middles = gather_ch(middle)
    block = exchange_seq(gathered[:, :share, :].reshape(shards, each, share, width))
    block, features_first, middles = tie(block, features_first, middles)
    core = lax.axis_index("ch") % each
    own = middles.reshape(shards, each, rows + 2 * EDGE, width)
    own = lax.dynamic_slice(own, (0, core, EDGE, 0), (shards, 1, rows, width))
    projected, scale = project(middles, gathered, share, 1, w_second, rows + 2 * EDGE)
    features_second, gated, signal, segments, closing = second_features(
        projected, s_second, cotangents, decay_rates
    )
    own, closings = tie(own[:, 0], gather_seq(closing))
    columns = exchange_seq(own)
    output, *grads, terms = second_filter(
        seq[None], features_second, gated, signal, segments, closings,
        decay_rates, residues, cotangents, middle, projected, s_second, scale,
    )
    scale = scale[EDGE : EDGE + rows]
    pieces_of = ring_gather(grads)
    partial = project_back(grads, w_second, jnp.arange(pieces, dtype=jnp.int32))
    partial, columns = tie(partial, columns)
    other = sibling(columns)
    partial_sum = scatter_ch(partial)
    terms = lax.psum(terms[:, 0], "ch")
    partial_sum, other, *arrays = tie(partial_sum, other, *[a for _, _, a in pieces_of[2:-2]])
    pieces_of[2:-2] = [old[:2] + (new,) for old, new in zip(pieces_of[2:-2], arrays)]
    grad_normed = partial_sum.astype(f32)
    as_float = middle[EDGE : EDGE + rows].astype(f32)
    grad_middle = (
        cotangent.astype(f32)
        + gain_second.astype(f32) * grad_normed
        - as_float * (scale * scale) * terms[:, None] / features
    ).astype(bf16)
    grad_gain_second = jnp.sum(grad_normed * as_float, axis=0)

    halo = shift(grad_middle[:back], "seq", -1)
    halo, far_up, far_down = tie(halo, pieces_of[-2][2], pieces_of[-1][2])
    pieces_of[-2:] = [pieces_of[-2][:2] + (far_up,), pieces_of[-1][:2] + (far_down,)]
    sums = first_backward(
        token_ids[None], grad_middle, halo, features_first, filtered_first, s_first, medium, vocab, shards
    )
    sums = exchange_seq(sums)
    block_gains = lax.dynamic_slice_in_dim(gains_second, seq * each, each, 0)
    places = jnp.stack([core, 1 - core]).astype(jnp.int32)
    grad_weights_second = weight_grad(
        [columns, other], places, pieces_of, order, jnp.swapaxes(block_gains, 1, 2)
    )
    sums, grad_weights_second = tie(sums, grad_weights_second)
    own_sums = jnp.sum(sums.astype(f32), axis=0)
    terms = jnp.sum(own_sums[:3] * own_table.astype(f32), axis=(0, 2))
    own_grads = (own_sums[:3] * own_scale[None]).astype(bf16)
    all_grads = ring_gather([own_grads])
    extra_rows = -(-share // width)
    extra = jnp.pad(terms, (0, EDGE * width - share)).reshape(EDGE, width).astype(bf16)
    partial = project_back([own_grads], w_first, scatter_order(), extra)
    grad_normed, near, far = ring_scatter(
        partial, [a for _, _, a in all_grads[1:-2]], [a for _, _, a in all_grads[-2:]]
    )
    all_grads[1:] = [old[:2] + (new,) for old, new in zip(all_grads[1:], near + far)]
    terms = grad_normed[share : share + extra_rows].reshape(-1)[:share]
    grad_normed = grad_normed[:share]
    block_gains = lax.dynamic_slice_in_dim(gains_first, seq * each, each, 0)
    grad_weights_first = weight_grad(
        [block[:, i] for i in range(each)],
        jnp.arange(each, dtype=jnp.int32),
        all_grads,
        order,
        jnp.swapaxes(block_gains, 1, 2),
    )

    as_float = own_embedding.astype(f32)
    grad_embedding = (
        own_sums[3]
        + gain_first.astype(f32) * grad_normed
        - as_float * (own_scale * own_scale) * terms[:, None] / features
    )
    grad_gain_first = jnp.sum(grad_normed * as_float, axis=0)
    last = jnp.concatenate(
        [
            grad_embedding,
            grad_gain_first[None],
            grad_gain_second[None],
            jnp.zeros((EDGE - 2, width), f32),
        ],
        axis=0,
    ).astype(bf16)
    last = gather_seq(last).astype(f32)
    return (
        output,
        last[:, :share].reshape(vocab, width),
        jnp.sum(last[:, share], axis=0),
        jnp.sum(last[:, share + 1], axis=0),
        jnp.transpose(grad_weights_first, (1, 0, 2)),
        jnp.transpose(grad_weights_second, (1, 0, 2)),
    )


def solution(mesh):
    placed = (
        P("seq"),
        P(None, "ch"),
        P("ch"),
        P("ch"),
        P(None, None, "ch"),
        P(None, None, "ch"),
        P(None, None, "ch"),
        P(None, None, "ch"),
        P(None, "ch"),
        P(None, "ch"),
        P(None, "ch"),
        P("seq", "ch"),
    )
    return jax.shard_map(
        per_device,
        mesh=mesh,
        in_specs=placed,
        out_specs=(
            P("seq", "ch"),
            P(None, "ch"),
            P("ch"),
            P("ch"),
            P("seq", None, "ch"),
            P("seq", None, "ch"),
        ),
        check_vma=False,
    )
```

```python
import functools

import jax
import jax.numpy as jnp
from jax import lax
from jax.experimental import pallas as pl
from jax.experimental.pallas import tpu as pltpu
from jax.sharding import PartitionSpec as P

epsilon = 1e-06
f32 = jnp.float32
bf16 = jnp.bfloat16
LANES = 128
EDGE = 16
VECTOR = 160


def round_up(value, multiple):
    return -(-value // multiple) * multiple


def call(kernel, grid, in_specs, out_specs, out_shape, scratch, flops, moved, prefetch=0):
    return pl.pallas_call(
        kernel,
        grid_spec=pltpu.PrefetchScalarGridSpec(
            num_scalar_prefetch=prefetch,
            grid=grid,
            in_specs=in_specs,
            out_specs=out_specs,
            scratch_shapes=scratch,
        ),
        out_shape=out_shape,
        compiler_params=pltpu.CompilerParams(vmem_limit_bytes=54 * 2**20),
        cost_estimate=pl.CostEstimate(flops=flops, bytes_accessed=moved, transcendentals=0),
    )


def whole(shape):
    return pl.BlockSpec(shape, lambda i, *_: (0,) * len(shape))


def lanes(shape):
    return pl.BlockSpec(shape[:-1] + (LANES,), lambda i, *_: (0,) * (len(shape) - 1) + (i,))


def project_kernel(
    per_step, features, rows, gain_row, x_ref, gain_ref, w_ref, p_ref, scale_ref, total, squares
):
    step = pl.program_id(0)
    width = x_ref.shape[2]

    @pl.when(step == 0)
    def _():
        total[...] = jnp.zeros_like(total)
        squares[...] = jnp.zeros_like(squares)

    for part in range(per_step):
        x = x_ref[part, :rows, :].astype(f32)
        square = x * x
        running = squares[...]
        for lane in range(width // LANES):
            running = running + square[:, lane * LANES : (lane + 1) * LANES]
        squares[...] = running
        gain = gain_ref[part, gain_row : gain_row + 1, :].astype(f32)
        scaled = (x * gain).astype(bf16)
        for j in range(3):
            total[j] += jnp.dot(
                scaled, w_ref[j, part * width : (part + 1) * width, :], preferred_element_type=f32
            )

    @pl.when(step == pl.num_programs(0) - 1)
    def _():
        mean = jnp.sum(squares[...], axis=1, keepdims=True) / features
        scale = lax.rsqrt(mean + epsilon)
        scale_ref[...] = scale
        for j in range(3):
            p_ref[j] = (total[j] * scale).astype(bf16)


def project(chunks, gains, gain_block, gain_row, weights, rows):
    count, _, width = chunks.shape
    features, columns = weights.shape[1:]
    per_step = 2 if count % 2 == 0 else 1
    return call(
        functools.partial(project_kernel, per_step, features, rows, gain_row),
        (count // per_step,),
        [
            pl.BlockSpec((per_step, chunks.shape[1], width), lambda i: (i, 0, 0)),
            pl.BlockSpec((per_step, EDGE, width), lambda i: (i, gain_block // EDGE, 0)),
            pl.BlockSpec((3, per_step * width, columns), lambda i: (0, i, 0)),
        ],
        [whole((3, rows, columns)), whole((rows, 1))],
        [
            jax.ShapeDtypeStruct((3, rows, columns), bf16),
            jax.ShapeDtypeStruct((rows, 1), f32),
        ],
        [pltpu.VMEM((3, rows, columns), f32), pltpu.VMEM((rows, LANES), f32)],
        6 * rows * features * columns,
        6 * features * columns + 2 * rows * features,
    )(chunks, gains, weights)


def back_kernel(parts, apart, order_ref, *refs):
    g_refs, w_refs = refs[:parts], refs[parts : parts + 2]
    extra_ref, *o_refs, grads = refs[parts + 2 :]
    rows, columns = grads.shape[0], grads.shape[1] // 3

    @pl.when(pl.program_id(0) == 0)
    def _():
        first = 0
        for g_ref in g_refs:
            more = g_ref.shape[1]
            for j in range(3):
                grads[first : first + more, j * columns : (j + 1) * columns] = g_ref[j]
            first += more

    for piece, w_ref in enumerate(w_refs):
        o_ref, at = (o_refs[piece], 0) if apart else (o_refs[0], piece)
        weights = jnp.concatenate([w_ref[j] for j in range(3)], axis=1)
        o_ref[at, :rows, :] = lax.dot_general(
            grads[...], weights, (((1,), (1,)), ((), ())), preferred_element_type=f32
        ).astype(bf16)
        if o_ref.shape[1] > rows:
            o_ref[at, rows:, :] = extra_ref[...]


def project_back(parts, weights, order, extra, apart):
    columns = parts[0].shape[2]
    rows = sum(part.shape[1] for part in parts)
    features = weights.shape[1]
    count = order.shape[0]
    width = features // count
    high = rows + (extra.shape[0] if apart else 0)
    each = 1 if apart else 2
    out = jax.ShapeDtypeStruct((count * each // 2, high, width), bf16)
    return call(
        functools.partial(back_kernel, len(parts), apart),
        (count // 2,),
        [whole(part.shape) for part in parts]
        + [
            pl.BlockSpec((3, width, columns), lambda i, order: (0, order[2 * i], 0)),
            pl.BlockSpec((3, width, columns), lambda i, order: (0, order[2 * i + 1], 0)),
            whole(extra.shape),
        ],
        [pl.BlockSpec((each, high, width), lambda i, *_: (i, 0, 0))] * (2 // each),
        [out] * (2 // each),
        [pltpu.VMEM((rows, 3 * columns), bf16)],
        6 * rows * features * columns,
        6 * features * columns + 2 * rows * features,
        prefetch=1,
    )(order, *parts, weights, weights, extra)


def weight_grad_kernel(spans, pieces, order_ref, piece_ref, gain_ref, *refs):
    x_refs, g_refs, out_ref = refs[:pieces], refs[pieces:-1], refs[-1]

    for piece, x_ref in enumerate(x_refs):

        @pl.when(pl.program_id(0) == piece)
        def _(x_ref=x_ref):
            for j in range(3):
                total = None
                for (slot, first), g_ref in zip(spans, g_refs):
                    some = x_ref[order_ref[slot], first : first + g_ref.shape[1], :]
                    term = lax.dot_general(
                        some, g_ref[j], (((0,), (0,)), ((), ())), preferred_element_type=f32
                    )
                    total = term if total is None else total + term
                out_ref[j] = total * gain_ref[0]


def weight_grad(columns, places, grads, order, gains):
    shards, rows, width = columns[0].shape
    pieces = len(columns)
    out = grads[0][2].shape[2]
    arrays = [array for _, _, array in grads]
    return call(
        functools.partial(weight_grad_kernel, [(slot, first) for slot, first, _ in grads], pieces),
        (pieces,),
        [pl.BlockSpec((1, width, 1), lambda i, order, places: (places[i], 0, 0))]
        + [whole(array.shape) for array in list(columns) + arrays],
        pl.BlockSpec((3, width, out), lambda i, order, places: (0, places[i], 0)),
        jax.ShapeDtypeStruct((3, pieces * width, out), f32),
        [],
        6 * shards * pieces * rows * width * out,
        2 * shards * pieces * rows * width + 6 * shards * rows * out + 12 * pieces * width * out,
        prefetch=2,
    )(order, places, gains, *columns, *arrays)


def fir(source, taps, target, mixed, mixed_taps, base, rows, forward):
    stride = rows // 8
    steps = stride // 4
    tap_count = taps.shape[0]
    quarter = tap_count // 4
    span = steps + quarter

    def row(position):
        return base + (position if forward else stride - 1 - position)

    def combine(x):
        even, odd, low, high = x[0] + x[2], x[1] + x[3], x[0] + x[1], x[2] + x[3]
        return [x[0], x[2], even, x[1], x[3], odd, low, high, even + odd]

    def mix(n, carry):
        first = 4 * (n - quarter)
        values = [source[pl.ds(row(first + p), 8, stride=stride), :] for p in range(4)]
        for c, value in enumerate(combine(values)):
            mixed[c, n] = value
        return carry

    lax.fori_loop(0, span, mix, 0, unroll=7 if span % 7 == 0 else 1)
    for c, value in enumerate(combine([taps[pl.ds(p, quarter, stride=4), :] for p in range(4)])):
        mixed_taps[c * quarter : (c + 1) * quarter, :] = value

    chunk = 8
    outs = steps + 1

    def product(c, carry):
        sums = [jnp.zeros((8, LANES), f32)] * outs
        for k0 in range(0, quarter, chunk):
            loaded = [mixed[c, quarter - 1 - k0 - (chunk - 1) + n] for n in range(outs + chunk - 1)]
            for k in range(chunk):
                tap = mixed_taps[pl.ds(c * quarter + k0 + k, 1), :]
                for p in range(outs):
                    sums[p] = sums[p] + tap * loaded[p + chunk - 1 - k]
        for p in range(outs):
            mixed[c, p] = sums[p]
        return carry

    lax.fori_loop(0, 9, product, 0, unroll=3)

    def finish(p, carry):
        now = [mixed[c, p + 1] for c in range(9)]
        old = [mixed[c, p] for c in range(6)]
        even_0, even_1 = now[0] + old[1], now[2] - now[0] - now[1]
        odd_0, odd_1 = now[3] + old[4], now[5] - now[3] - now[4]
        odd_old = old[5] - old[3] - old[4]
        both_0, both_1 = now[6] + mixed[7, p], now[8] - now[6] - now[7]
        values = [even_0 + odd_old, both_0 - even_0 - odd_0, even_1 + odd_0, both_1 - even_1 - odd_1]
        for n, value in enumerate(values):
            target[pl.ds(row(4 * p + n) - base, 8, stride=stride), :] = value
        return carry

    lax.fori_loop(0, steps, finish, 0, unroll=True)


def fir_scratch(rows, tap_count):
    return [
        pltpu.VMEM((9, rows // 32 + tap_count // 4, 8, LANES), f32),
        pltpu.VMEM((9 * tap_count // 4, LANES), f32),
    ]


def short_sum(source, short, j, first, rows, sign):
    total = None
    for i in range(short.shape[1]):
        term = short[j, i : i + 1, :] * source[first + sign * i : first + sign * i + rows, :]
        total = term if total is None else total + term
    return total


def look_up(token_ref, onehot):
    grid = lax.broadcasted_iota(jnp.int32, onehot.shape, 1)
    onehot[...] = (grid == token_ref[...]).astype(f32).astype(bf16)


def first_forward_kernel(
    front, rows, places, token_ref, e_ref, short_ref, medium_ref, *refs,
):
    p_refs = refs[: len(places)]
    refs = refs[len(places) :]
    middle_ref, filtered_ref, onehot, table, projected, gated, taps, kept, *mixed = refs
    window, vocab = onehot.shape

    @pl.when(pl.program_id(0) == 0)
    def _():
        look_up(token_ref, onehot)

    taps[...] = medium_ref[...].astype(f32)
    extended = rows + 2 * EDGE
    for j in range(3):
        for place, p_ref in zip(places, p_refs):
            table[place : place + p_ref.shape[1], j * LANES : (j + 1) * LANES] = p_ref[j]
    looked = jnp.dot(onehot[...], table[...], preferred_element_type=f32)
    product = None
    for j in (1, 2, 0):
        projected[...] = looked[:, j * LANES : (j + 1) * LANES]
        if j == 0:
            kept[...] = short_sum(projected, short_ref, j, front - EDGE, extended, -1)
        else:
            feature = short_sum(projected, short_ref, j, 8, window - 8, -1)
            product = feature if product is None else product * feature
    gated[8:, :] = product.astype(bf16).astype(f32)
    fir(gated, taps, projected, *mixed, front - EDGE, extended, True)
    filtered = projected[:extended, :]
    filtered_ref[...] = filtered[EDGE:, :]
    embedded = jnp.dot(onehot[front - EDGE :, :], e_ref[...], preferred_element_type=f32)
    middle_ref[...] = (embedded + kept[...] * filtered).astype(bf16)


def first_forward(tokens, tables, embedding, short, medium, rows, front):
    share = tables[0][2].shape[1]
    places = [slot * share + first for slot, first, _ in tables]
    tables = [table for _, _, table in tables]
    extended = rows + 2 * EDGE
    window = front + rows + EDGE
    vocab = embedding.shape[0]
    columns = embedding.shape[1]
    shapes = [
        jax.ShapeDtypeStruct((extended, columns), bf16),
        jax.ShapeDtypeStruct((rows + EDGE, columns), f32),
    ]
    return call(
        functools.partial(first_forward_kernel, front, rows, places),
        (columns // LANES,),
        [pl.BlockSpec((window, 1), lambda i, *_: (0, 0))]
        + [lanes(a.shape) for a in (embedding, short, medium, *tables)],
        [lanes(s.shape) for s in shapes],
        shapes,
        [
            pltpu.VMEM((window, vocab), bf16),
            pltpu.VMEM((vocab, 3 * LANES), bf16),
            pltpu.VMEM((window, LANES), f32),
            pltpu.VMEM((window, LANES), f32),
            pltpu.VMEM((medium.shape[0], LANES), f32),
            pltpu.VMEM((extended, LANES), f32),
        ]
        + fir_scratch(extended, medium.shape[0]),
        8 * window * vocab * columns + 250 * VECTOR * rows * columns,
        8 * window * columns,
    )(tokens[:window], embedding, short, medium, *tables)


def first_features_kernel(places, token_ref, short_ref, *refs):
    p_refs = refs[: len(places)]
    feature_ref, onehot, table, projected = refs[len(places) :]

    @pl.when(pl.program_id(0) == 0)
    def _():
        look_up(token_ref, onehot)

    for j in range(3):
        for place, p_ref in zip(places, p_refs):
            table[place : place + p_ref.shape[1], :] = p_ref[j]
        projected[...] = jnp.dot(onehot[...], table[...], preferred_element_type=f32)
        feature_ref[j] = short_sum(projected, short_ref, j, EDGE, feature_ref.shape[1], -1)


def first_features(tokens, tables, short):
    share = tables[0][2].shape[1]
    places = [slot * share + first for slot, first, _ in tables]
    vocab = share * (1 + max(slot for slot, _, _ in tables))
    tables = [table for _, _, table in tables]
    window = tokens.shape[0]
    columns = tables[0].shape[2]
    shape = jax.ShapeDtypeStruct((3, window - EDGE, columns), f32)
    return call(
        functools.partial(first_features_kernel, places),
        (columns // LANES,),
        [whole((window, 1))] + [lanes(a.shape) for a in (short, *tables)],
        lanes(shape.shape),
        shape,
        [
            pltpu.VMEM((window, vocab), bf16),
            pltpu.VMEM((vocab, LANES), bf16),
            pltpu.VMEM((window, LANES), f32),
        ],
        6 * window * vocab * columns + 50 * VECTOR * window * columns,
        16 * window * columns,
    )(tokens, short, *tables)


def first_backward_kernel(
    rows, token_ref, above_ref, halo_ref, feature_ref, filtered_ref, short_ref, medium_ref,
    out_ref, onehot, signal, grad_gated, taps, held, *mixed,
):
    vocab = onehot.shape[0]
    parts = out_ref.shape[0]

    @pl.when(pl.program_id(0) == 0)
    def _():
        grid = lax.broadcasted_iota(jnp.int32, (vocab, rows), 0)
        onehot[...] = (grid == token_ref[...]).astype(f32).astype(bf16)

    taps[...] = medium_ref[...].astype(f32)
    extended = rows + EDGE
    above = jnp.concatenate([above_ref[...], halo_ref[...]], axis=0).astype(f32)
    signal[...] = (above * feature_ref[0]).astype(bf16).astype(f32)
    fir(signal, taps, grad_gated, *mixed, 0, extended + EDGE, False)

    def keep(j, value):
        held[...] = value.astype(bf16).astype(f32)
        grad = short_sum(held, short_ref, j, 0, rows, 1).astype(bf16)
        total = jnp.dot(onehot[...], grad, preferred_element_type=f32).astype(bf16)
        for part in range(parts):
            size = vocab // parts
            out_ref[part, j] = total[part * size : (part + 1) * size, :]

    keep(0, above[:extended, :] * filtered_ref[...])
    keep(1, grad_gated[:extended, :] * feature_ref[2, :extended, :])
    keep(2, grad_gated[:extended, :] * feature_ref[1, :extended, :])
    total = jnp.dot(onehot[...], above_ref[...], preferred_element_type=f32).astype(bf16)
    for part in range(parts):
        size = vocab // parts
        out_ref[part, 3] = total[part * size : (part + 1) * size, :]


def first_backward(tokens, above, halo, features, filtered, short, medium, vocab, parts):
    rows = above.shape[0]
    columns = above.shape[1]
    later = rows + halo.shape[0]
    operands = (above, halo, features, filtered, short, medium)
    shape = jax.ShapeDtypeStruct((parts, 4, vocab // parts, columns), bf16)
    return call(
        functools.partial(first_backward_kernel, rows),
        (columns // LANES,),
        [whole((1, rows))] + [lanes(a.shape) for a in operands],
        lanes(shape.shape),
        shape,
        [
            pltpu.VMEM((vocab, rows), bf16),
            pltpu.VMEM((later, LANES), f32),
            pltpu.VMEM((rows + 2 * EDGE, LANES), f32),
            pltpu.VMEM((medium.shape[0], LANES), f32),
            pltpu.VMEM((rows + EDGE, LANES), f32),
        ]
        + fir_scratch(rows + 2 * EDGE, medium.shape[0]),
        8 * rows * vocab * columns + 250 * VECTOR * rows * columns,
        16 * later * columns,
    )(tokens, *operands)


SEGMENTS = 8
SHIFT = 8


def summed(terms):
    while len(terms) > 1:
        terms = [a + b for a, b in zip(terms[::2], terms[1::2])] + terms[len(terms) // 2 * 2 :]
    return terms[0]


def scan_modes(source, decays, states, length, forward, residues, target):
    first = 0 if forward else SHIFT

    def step(i, held):
        position = first + (i if forward else length - 1 - i)
        value = source[pl.ds(position, SEGMENTS, stride=length), :]
        held = tuple(d * s + value for d, s in zip(decays, held))
        target[pl.ds(position, SEGMENTS, stride=length), :] = summed(
            [r * s for r, s in zip(residues, held)]
        )
        return held

    return lax.fori_loop(0, length, step, tuple(states), unroll=8)


def spread(ref, count):
    return [jnp.broadcast_to(ref[m : m + 1, :], (SEGMENTS, LANES)) for m in range(count)]


def second_features_kernel(
    shards, p_ref, short_ref, above_ref, rate_ref,
    feature_ref, gated_ref, signal_ref, segment_ref, closing_ref, projected, gated, signal, decay,
):
    extended = above_ref.shape[0]
    modes = rate_ref.shape[0]
    length = (extended - EDGE) // SEGMENTS
    product = None
    for j in range(3):
        projected[...] = p_ref[j].astype(f32)
        feature = short_sum(projected, short_ref, j, EDGE, extended, -1)
        feature_ref[j] = feature
        if j == 0:
            rounded = (above_ref[...].astype(f32) * feature).astype(bf16)
            signal_ref[...] = rounded
            signal[...] = rounded.astype(f32)
        else:
            product = feature if product is None else product * feature
    rounded = product.astype(bf16)
    gated_ref[...] = rounded
    gated[...] = rounded.astype(f32)
    rates = rate_ref[...]
    decay[...] = jnp.exp(-rates)
    decays = spread(decay, modes)

    def step(i, held):
        ahead = gated[pl.ds(i, SEGMENTS, stride=length), :]
        back = signal[pl.ds(SHIFT + length - 1 - i, SEGMENTS, stride=length), :]
        return tuple(
            d * s + value
            for values, value in zip((held[:modes], held[modes:]), (ahead, back))
            for d, s in zip(decays, values)
        )

    zeros = (jnp.zeros((SEGMENTS, LANES), f32),) * (2 * modes)
    ends = lax.fori_loop(0, length, step, zeros, unroll=8)
    for way in range(2):
        for m in range(modes):
            segment_ref[way, pl.ds(m, SEGMENTS, stride=modes), :] = ends[way * modes + m]
        stride = jnp.exp(-rates * length)
        total = jnp.zeros((modes, LANES), f32)
        for n in range(SEGMENTS):
            at = n if way == 0 else SEGMENTS - 1 - n
            total = stride * total + segment_ref[way, at * modes : (at + 1) * modes, :]
        for shard in range(shards):
            closing_ref[shard, way] = total


def second_features(projected, short, above, rates, shards):
    extended, columns = above.shape
    modes = rates.shape[0]
    shapes = [
        jax.ShapeDtypeStruct((3, extended, columns), f32),
        jax.ShapeDtypeStruct((extended, columns), bf16),
        jax.ShapeDtypeStruct((extended, columns), bf16),
        jax.ShapeDtypeStruct((2, SEGMENTS * modes, columns), f32),
        jax.ShapeDtypeStruct((shards, 2, modes, columns), f32),
    ]
    return call(
        functools.partial(second_features_kernel, shards),
        (columns // LANES,),
        [lanes(a.shape) for a in (projected, short, above, rates)],
        [lanes(s.shape) for s in shapes],
        shapes,
        [
            pltpu.VMEM((extended + EDGE, LANES), f32),
            pltpu.VMEM((extended, LANES), f32),
            pltpu.VMEM((extended, LANES), f32),
            pltpu.VMEM((modes, LANES), f32),
        ],
        120 * VECTOR * extended * columns,
        24 * extended * columns,
    )(projected, short, above, rates)


def second_filter_kernel(
    shards, seq_ref, feature_ref, gated_ref, signal_ref, segment_ref, closing_ref, rate_ref,
    residue_ref, above_ref, middle_ref, p_ref, short_ref, scale_ref,
    out_ref, top_ref, bottom_ref, term_ref,
    entering, source, filtered, grad_gated, decay, residue, ends, held,
):
    rows = out_ref.shape[0]
    modes = rate_ref.shape[0]
    length = rows // SEGMENTS
    reach = rows + SHIFT
    me = seq_ref[0]
    rates = rate_ref[...]
    decay[...] = jnp.exp(-rates)
    residue[...] = residue_ref[...]
    stride = jnp.exp(-rates * length)
    for way, (values, target) in enumerate(((gated_ref, filtered), (signal_ref, grad_gated))):
        source[way] = values[...].astype(f32)
        state = jnp.zeros((modes, LANES), f32)
        for shard in range(shards):
            ahead = me - 1 - shard if way == 0 else shard - me - 1
            weight = jnp.exp(-rates * (rows * jnp.maximum(ahead, 0)).astype(f32))
            state = state + jnp.where(ahead >= 0, weight * closing_ref[shard, way], 0.0)
        for n in range(SEGMENTS):
            at = n if way == 0 else SEGMENTS - 1 - n
            entering[at * modes : (at + 1) * modes, :] = state
            state = stride * state + segment_ref[way, at * modes : (at + 1) * modes, :]
        ends[way] = state
        starts = [entering[pl.ds(m, SEGMENTS, stride=modes), :] for m in range(modes)]
        scan_modes(
            source.at[way], spread(decay, modes), starts, length, way == 0,
            spread(residue, modes), target,
        )

    upper = lax.broadcasted_iota(jnp.int32, (SEGMENTS, LANES), 0) < SEGMENTS // 2
    decays, residues = spread(decay, modes), spread(residue, modes)
    states = [
        jnp.where(upper, a, b)
        for a, b in zip(spread(ends.at[0], modes), spread(ends.at[1], modes))
    ]
    for i in range(SHIFT):
        after, before = rows + i, SHIFT - 1 - i
        value = jnp.where(upper, source[0, after : after + 1, :], source[1, before : before + 1, :])
        states = [d * s + value for d, s in zip(decays, states)]
        result = summed([r * s for r, s in zip(residues, states)])
        filtered[after : after + 1, :] = result[:1, :]
        grad_gated[before : before + 1, :] = result[SEGMENTS // 2 : SEGMENTS // 2 + 1, :]

    out_ref[...] = (
        middle_ref[EDGE : EDGE + rows, :].astype(f32) + feature_ref[0, :rows, :] * filtered[:rows, :]
    ).astype(bf16)
    above = above_ref[...].astype(f32)[:reach, :]
    scale = scale_ref[EDGE : EDGE + rows, :]
    terms = None
    for j in range(3):
        if j == 0:
            grad = above * filtered[...]
        else:
            grad = grad_gated[...] * feature_ref[3 - j, :reach, :]
        held[...] = grad.astype(bf16).astype(f32)
        grad = short_sum(held, short_ref, j, 0, rows, 1)
        term = grad * p_ref[j, EDGE : EDGE + rows, :].astype(f32)
        terms = term if terms is None else terms + term
        scaled = (grad * scale).astype(bf16)
        top_ref[j] = scaled[: rows // 2, :]
        bottom_ref[j] = scaled[rows // 2 :, :]
    total = jnp.sum(terms, axis=1, keepdims=True)

    @pl.when(pl.program_id(0) == 0)
    def _():
        term_ref[...] = total

    @pl.when(pl.program_id(0) > 0)
    def _():
        term_ref[...] += total


def second_filter(
    seq, features, gated, signal, segments, closings, rates, residues, above, middle, projected,
    short, scale,
):
    extended, columns = above.shape
    rows = extended - EDGE
    modes = rates.shape[0]
    shapes = [
        jax.ShapeDtypeStruct((rows, columns), bf16),
        jax.ShapeDtypeStruct((3, rows // 2, columns), bf16),
        jax.ShapeDtypeStruct((3, rows // 2, columns), bf16),
        jax.ShapeDtypeStruct((rows, 1), f32),
    ]
    operands = (
        features, gated, signal, segments, closings, rates, residues, above, middle, projected, short,
    )
    return call(
        functools.partial(second_filter_kernel, closings.shape[0]),
        (columns // LANES,),
        [lanes(a.shape) for a in operands] + [whole(scale.shape)],
        [lanes(s.shape) for s in shapes[:3]] + [whole((rows, 1))],
        shapes,
        [pltpu.VMEM((SEGMENTS * modes, LANES), f32), pltpu.VMEM((2, extended, LANES), f32)]
        + [pltpu.VMEM((rows + SHIFT, LANES), f32)] * 2
        + [pltpu.VMEM((modes, LANES), f32)] * 2
        + [pltpu.VMEM((2, modes, LANES), f32), pltpu.VMEM((rows + SHIFT, LANES), f32)],
        250 * VECTOR * rows * columns,
        40 * rows * columns,
        prefetch=1,
    )(seq, *operands, scale)


def shift(value, axis, by):
    devices = lax.axis_size(axis)
    pairs = [(i, i + by) for i in range(devices) if 0 <= i + by < devices]
    return lax.ppermute(value, axis, pairs)


def gather_ch(value):
    return lax.all_gather(value, "ch", axis=0, tiled=False)


def scatter_ch(value):
    return lax.psum_scatter(value, "ch", scatter_dimension=0, tiled=False)


def exchange_seq(value):
    return lax.all_to_all(value, "seq", split_axis=0, concat_axis=0, tiled=True)


def gather_seq(value):
    return exchange_seq(jnp.broadcast_to(value[None], (lax.axis_size("seq"),) + value.shape))


def seq_ring():
    devices = lax.axis_size("seq")
    if devices % 2:
        return list(range(devices))
    return list(range(0, devices, 2)) + list(range(devices - 1, 0, -2))


def seq_hop(value, by):
    ring = seq_ring()
    pairs = [(ring[i], ring[(i + by) % len(ring)]) for i in range(len(ring))]
    return lax.ppermute(value, "seq", pairs)


def ring_gather(parts):
    shards = lax.axis_size("seq")
    firsts = [0, parts[0].shape[1]][: len(parts)]
    out = [(0, first, part) for first, part in zip(firsts, parts)]
    up = down = parts
    for step in range(1, (shards + 1) // 2):
        up, down = [seq_hop(a, 1) for a in up], [seq_hop(a, -1) for a in down]
        out += [(shards - step, first, part) for first, part in zip(firsts, up)]
        out += [(step, first, part) for first, part in zip(firsts, down)]
    if shards % 2 == 0:
        if len(parts) == 1:
            half = parts[0].shape[1] // 2
            up, down = [up[0][:, :half]], [down[0][:, half:]]
        else:
            half = firsts[1]
        out += [(shards // 2, 0, seq_hop(up[0], 1)), (shards // 2, half, seq_hop(down[-1], -1))]
    return out


def ring_order():
    ring = seq_ring()
    twice = jnp.array(ring + ring, jnp.int32)
    place = jnp.argmax(twice[: len(ring)] == lax.axis_index("seq")).astype(jnp.int32)
    return lax.dynamic_slice_in_dim(twice, place, len(ring), 0)


def ch_hop(value, by):
    devices = lax.axis_size("ch")
    pairs = [(i, (i + 2 * by) % devices) for i in range(devices)]
    return lax.ppermute(value, "ch", pairs)


def sibling(value):
    return lax.ppermute(value, "ch", [(i, i ^ 1) for i in range(lax.axis_size("ch"))])


def scatter_order():
    devices = lax.axis_size("ch")
    me = lax.axis_index("ch")
    places = jnp.arange(devices // 2, dtype=jnp.int32)
    return jnp.stack([(2 * places + other) % devices for other in (me, me ^ 1)], axis=1).reshape(-1)


def added(*terms):
    return functools.reduce(lambda a, b: a + b, [t.astype(f32) for t in terms])


def ring_scatter(pieces, other_pieces, near, far):
    half = pieces.shape[0]
    other_pieces, *near = tie(other_pieces, *near)
    mine = added(pieces, sibling(other_pieces)).astype(bf16)
    if half == 1:
        return mine[0].astype(f32), near, far
    steps = (half - 1) // 2
    rows = mine.shape[1]
    middle = rows // 32 * 16
    up = down = None
    if half % 2 == 0:
        opposite = mine[half // 2]
        up, down = ch_hop(opposite[:middle], 1), ch_hop(opposite[middle:], -1)
        if half == 2:
            return added(mine[0], jnp.concatenate([up, down], axis=0)), near, far
    for step in range(steps, 0, -1):
        first, second = mine[step], mine[half - step]
        if up is not None and step == steps and half % 2 == 0:
            first = jnp.concatenate(
                [added(first[:middle], up).astype(bf16), first[middle:]], axis=0
            )
            second = jnp.concatenate(
                [second[:middle], added(second[middle:], down).astype(bf16)], axis=0
            )
        elif up is not None:
            first, second = added(first, up).astype(bf16), added(second, down).astype(bf16)
        up, down = ch_hop(first, 1), ch_hop(second, -1)
    up, down, *far = tie(up, down, *far)
    return added(mine[0], up, down), near, far


def tie(*values):
    return lax.optimization_barrier(values)


def per_device(
    token_ids,
    embedding,
    gain_first,
    gain_second,
    weights_first,
    weights_second,
    short_first,
    short_second,
    medium,
    residues,
    decay_rates,
    cotangent,
):
    shards = lax.axis_size("seq")
    pieces = lax.axis_size("ch")
    seq = lax.axis_index("seq")
    vocab, width = embedding.shape
    rows = token_ids.shape[0]
    features = width * pieces
    taps, tap_count = medium.shape[0], short_first.shape[0]
    front = round_up(EDGE + taps - 1 + tap_count - 1, 16)
    back = round_up(2 * EDGE + taps - 1, 16)
    w_first, w_second = (jnp.transpose(w, (1, 0, 2)) for w in (weights_first, weights_second))
    s_first, s_second = (jnp.transpose(s, (1, 0, 2)) for s in (short_first, short_second))

    order = ring_order()
    each = pieces // shards
    share = vocab // shards
    at = seq * share

    gains = jnp.concatenate(
        [gain_first[None], gain_second[None], jnp.zeros((EDGE - 2, width), bf16)], axis=0
    )
    own_embedding = lax.dynamic_slice_in_dim(embedding, at, share, 0)
    gathered = gather_ch(jnp.concatenate([own_embedding, gains], axis=0))
    tokens = lax.all_gather(token_ids, "seq", axis=0, tiled=True)
    slots = jnp.zeros(shards, jnp.int32).at[order].set(jnp.arange(shards, dtype=jnp.int32))
    turned = jnp.take(embedding.reshape(shards, share, width), order, axis=0)
    turned = turned.reshape(vocab, width)
    tokens = jnp.take(slots, tokens // share) * share + tokens % share
    tokens = jnp.pad(tokens, (front, back), constant_values=-1)
    tokens = lax.dynamic_slice_in_dim(tokens, seq * rows, front + rows + back, 0)
    behind = shift(cotangent[:EDGE], "seq", -1)
    cotangents = jnp.concatenate([cotangent, behind], axis=0)
    tokens, turned, cotangents, gathered = tie(tokens[:, None], turned, cotangents, gathered)
    gains_first = gathered[:, share : share + 1, :].astype(f32)
    gains_second = gathered[:, share + 1 : share + 2, :].astype(f32)
    own_table, own_scale = project(gathered, gathered, share, 0, w_first, share)
    tables = ring_gather([own_table])

    middle, filtered_first = first_forward(tokens, tables, turned, s_first, medium, rows, front)
    later, held = tie(tokens[front - EDGE :], middle)
    features_first = first_features(later, tables, s_first)

    middles = gather_ch(middle)
    block = exchange_seq(gathered[:, :share, :].reshape(shards, each, share, width))
    blocks = [block[:, i] for i in range(each)]
    block_gains = [
        jnp.swapaxes(lax.dynamic_slice_in_dim(g, seq * each, each, 0), 1, 2)
        for g in (gains_first, gains_second)
    ]
    core = lax.axis_index("ch") % each
    places = jnp.stack([core, 1 - core]).astype(jnp.int32)
    straight, scattered = jnp.arange(pieces, dtype=jnp.int32), scatter_order()
    blank = jnp.zeros((EDGE, width), bf16)
    features_first, places, straight, scattered, blank, middles, *rest = tie(
        features_first, places, straight, scattered, blank, middles, *blocks, *block_gains
    )
    blocks, block_gains = rest[:each], rest[each:]
    own = middles.reshape(shards, each, rows + 2 * EDGE, width)
    own = lax.dynamic_slice(own, (0, core, EDGE, 0), (shards, 1, rows, width))
    projected, scale = project(middles, gathered, share, 1, w_second, rows + 2 * EDGE)
    features_second, gated, signal, segments, closing = second_features(
        projected, s_second, cotangents, decay_rates, shards
    )
    own, closings = tie(own[:, 0], exchange_seq(closing))
    columns = exchange_seq(own)
    output, *grads, terms = second_filter(
        seq[None], features_second, gated, signal, segments, closings,
        decay_rates, residues, cotangents, middle, projected, s_second, scale,
    )
    scale = scale[EDGE : EDGE + rows]
    pieces_of = ring_gather(grads)
    (partial,) = project_back(grads, w_second, straight, blank, False)
    partial, columns = tie(partial, columns)
    other = sibling(columns)
    partial_sum = scatter_ch(partial)
    terms = lax.psum(terms[:, 0], "ch")
    partial_sum, other, *arrays = tie(partial_sum, other, *[a for _, _, a in pieces_of[2:-2]])
    pieces_of[2:-2] = [old[:2] + (new,) for old, new in zip(pieces_of[2:-2], arrays)]
    grad_normed = partial_sum.astype(f32)
    as_float = middle[EDGE : EDGE + rows].astype(f32)
    grad_middle = (
        cotangent.astype(f32)
        + gain_second.astype(f32) * grad_normed
        - as_float * (scale * scale) * terms[:, None] / features
    ).astype(bf16)
    grad_gain_second = jnp.sum(grad_normed * as_float, axis=0)

    halo = shift(grad_middle[:back], "seq", -1)
    halo, far_up, far_down = tie(halo, pieces_of[-2][2], pieces_of[-1][2])
    pieces_of[-2:] = [pieces_of[-2][:2] + (far_up,), pieces_of[-1][:2] + (far_down,)]
    sums = first_backward(
        token_ids[None], grad_middle, halo, features_first, filtered_first, s_first, medium, vocab,
        shards,
    )
    sums = exchange_seq(sums)
    grad_weights_second = weight_grad(
        [columns, other], places, pieces_of, order, block_gains[1]
    )
    sums, grad_weights_second = tie(sums, grad_weights_second)
    own_sums = jnp.sum(sums.astype(f32), axis=0)
    terms = jnp.sum(own_sums[:3] * own_table.astype(f32), axis=(0, 2))
    own_grads = (own_sums[:3] * own_scale[None]).astype(bf16)
    all_grads = ring_gather([own_grads])
    extra_rows = -(-share // width)
    extra = jnp.pad(terms, (0, EDGE * width - share)).reshape(EDGE, width).astype(bf16)
    partial, other_partial = project_back([own_grads], w_first, scattered, extra, True)
    grad_normed, near, far = ring_scatter(
        partial, other_partial, [a for _, _, a in all_grads[1:-2]], [a for _, _, a in all_grads[-2:]]
    )
    all_grads[1:] = [old[:2] + (new,) for old, new in zip(all_grads[1:], near + far)]
    terms = grad_normed[share : share + extra_rows].reshape(-1)[:share]
    grad_normed = grad_normed[:share]
    grad_weights_first = weight_grad(blocks, straight, all_grads, order, block_gains[0])

    as_float = own_embedding.astype(f32)
    grad_embedding = (
        own_sums[3]
        + gain_first.astype(f32) * grad_normed
        - as_float * (own_scale * own_scale) * terms[:, None] / features
    )
    grad_gain_first = jnp.sum(grad_normed * as_float, axis=0)
    last = jnp.concatenate(
        [
            grad_embedding,
            grad_gain_first[None],
            grad_gain_second[None],
            jnp.zeros((EDGE - 2, width), f32),
        ],
        axis=0,
    ).astype(bf16)
    last = gather_seq(last).astype(f32)
    return (
        output,
        last[:, :share].reshape(vocab, width),
        jnp.sum(last[:, share], axis=0),
        jnp.sum(last[:, share + 1], axis=0),
        jnp.transpose(grad_weights_first, (1, 0, 2)),
        jnp.transpose(grad_weights_second, (1, 0, 2)),
    )


def solution(mesh):
    placed = (
        P("seq"),
        P(None, "ch"),
        P("ch"),
        P("ch"),
        P(None, None, "ch"),
        P(None, None, "ch"),
        P(None, None, "ch"),
        P(None, None, "ch"),
        P(None, "ch"),
        P(None, "ch"),
        P(None, "ch"),
        P("seq", "ch"),
    )
    return jax.shard_map(
        per_device,
        mesh=mesh,
        in_specs=placed,
        out_specs=(
            P("seq", "ch"),
            P(None, "ch"),
            P("ch"),
            P("ch"),
            P("seq", None, "ch"),
            P("seq", None, "ch"),
        ),
        check_vma=False,
    )
```

```python
import functools

import jax
import jax.numpy as jnp
from jax import lax
from jax.experimental import pallas as pl
from jax.experimental.pallas import tpu as pltpu
from jax.sharding import PartitionSpec as P

epsilon = 1e-06
f32 = jnp.float32
bf16 = jnp.bfloat16
LANES = 128
EDGE = 16
VECTOR = 160


def round_up(value, multiple):
    return -(-value // multiple) * multiple


def call(kernel, grid, in_specs, out_specs, out_shape, scratch, flops, moved, prefetch=0):
    return pl.pallas_call(
        kernel,
        grid_spec=pltpu.PrefetchScalarGridSpec(
            num_scalar_prefetch=prefetch,
            grid=grid,
            in_specs=in_specs,
            out_specs=out_specs,
            scratch_shapes=scratch,
        ),
        out_shape=out_shape,
        compiler_params=pltpu.CompilerParams(vmem_limit_bytes=54 * 2**20),
        cost_estimate=pl.CostEstimate(flops=flops, bytes_accessed=moved, transcendentals=0),
    )


def whole(shape):
    return pl.BlockSpec(shape, lambda i, *_: (0,) * len(shape))


def lanes(shape):
    return pl.BlockSpec(shape[:-1] + (LANES,), lambda i, *_: (0,) * (len(shape) - 1) + (i,))


def project_kernel(
    per_step, features, rows, gain_row, x_ref, gain_ref, w_ref, p_ref, scale_ref, total, squares
):
    step = pl.program_id(0)
    width = x_ref.shape[2]

    @pl.when(step == 0)
    def _():
        total[...] = jnp.zeros_like(total)
        squares[...] = jnp.zeros_like(squares)

    for part in range(per_step):
        x = x_ref[part, :rows, :].astype(f32)
        square = x * x
        running = squares[...]
        for lane in range(width // LANES):
            running = running + square[:, lane * LANES : (lane + 1) * LANES]
        squares[...] = running
        gain = gain_ref[part, gain_row : gain_row + 1, :].astype(f32)
        scaled = (x * gain).astype(bf16)
        for j in range(3):
            total[j] += jnp.dot(
                scaled, w_ref[j, part * width : (part + 1) * width, :], preferred_element_type=f32
            )

    @pl.when(step == pl.num_programs(0) - 1)
    def _():
        mean = jnp.sum(squares[...], axis=1, keepdims=True) / features
        scale = lax.rsqrt(mean + epsilon)
        scale_ref[...] = scale
        for j in range(3):
            p_ref[j] = (total[j] * scale).astype(bf16)


def project(chunks, gains, gain_block, gain_row, weights, rows):
    count, _, width = chunks.shape
    features, columns = weights.shape[1:]
    per_step = 2 if count % 2 == 0 else 1
    return call(
        functools.partial(project_kernel, per_step, features, rows, gain_row),
        (count // per_step,),
        [
            pl.BlockSpec((per_step, chunks.shape[1], width), lambda i: (i, 0, 0)),
            pl.BlockSpec((per_step, EDGE, width), lambda i: (i, gain_block // EDGE, 0)),
            pl.BlockSpec((3, per_step * width, columns), lambda i: (0, i, 0)),
        ],
        [whole((3, rows, columns)), whole((rows, 1))],
        [
            jax.ShapeDtypeStruct((3, rows, columns), bf16),
            jax.ShapeDtypeStruct((rows, 1), f32),
        ],
        [pltpu.VMEM((3, rows, columns), f32), pltpu.VMEM((rows, LANES), f32)],
        6 * rows * features * columns,
        6 * features * columns + 2 * rows * features,
    )(chunks, gains, weights)


def back_kernel(parts, apart, order_ref, *refs):
    g_refs, w_refs = refs[:parts], refs[parts : parts + 2]
    extra_ref, *o_refs, grads = refs[parts + 2 :]
    rows, columns = grads.shape[0], grads.shape[1] // 3

    @pl.when(pl.program_id(0) == 0)
    def _():
        first = 0
        for g_ref in g_refs:
            more = g_ref.shape[1]
            for j in range(3):
                grads[first : first + more, j * columns : (j + 1) * columns] = g_ref[j]
            first += more

    for piece, w_ref in enumerate(w_refs):
        o_ref, at = (o_refs[piece], 0) if apart else (o_refs[0], piece)
        weights = jnp.concatenate([w_ref[j] for j in range(3)], axis=1)
        o_ref[at, :rows, :] = lax.dot_general(
            grads[...], weights, (((1,), (1,)), ((), ())), preferred_element_type=f32
        ).astype(bf16)
        if o_ref.shape[1] > rows:
            o_ref[at, rows:, :] = extra_ref[...]


def project_back(parts, weights, order, extra, apart):
    columns = parts[0].shape[2]
    rows = sum(part.shape[1] for part in parts)
    features = weights.shape[1]
    count = order.shape[0]
    width = features // count
    high = rows + (extra.shape[0] if apart else 0)
    each = 1 if apart else 2
    out = jax.ShapeDtypeStruct((count * each // 2, high, width), bf16)
    return call(
        functools.partial(back_kernel, len(parts), apart),
        (count // 2,),
        [whole(part.shape) for part in parts]
        + [
            pl.BlockSpec((3, width, columns), lambda i, order: (0, order[2 * i], 0)),
            pl.BlockSpec((3, width, columns), lambda i, order: (0, order[2 * i + 1], 0)),
            whole(extra.shape),
        ],
        [pl.BlockSpec((each, high, width), lambda i, *_: (i, 0, 0))] * (2 // each),
        [out] * (2 // each),
        [pltpu.VMEM((rows, 3 * columns), bf16)],
        6 * rows * features * columns,
        6 * features * columns + 2 * rows * features,
        prefetch=1,
    )(order, *parts, weights, weights, extra)


def weight_grad_kernel(spans, pieces, order_ref, piece_ref, gain_ref, *refs):
    x_refs, g_refs, out_ref = refs[:pieces], refs[pieces:-1], refs[-1]
    gain = jnp.broadcast_to(gain_ref[0], (8, gain_ref.shape[2])).T[:, :1]

    for piece, x_ref in enumerate(x_refs):

        @pl.when(pl.program_id(0) == piece)
        def _(x_ref=x_ref):
            for j in range(3):
                total = None
                for (slot, first), g_ref in zip(spans, g_refs):
                    some = x_ref[order_ref[slot], first : first + g_ref.shape[1], :]
                    term = lax.dot_general(
                        some, g_ref[j], (((0,), (0,)), ((), ())), preferred_element_type=f32
                    )
                    total = term if total is None else total + term
                out_ref[j] = total * gain


def weight_grad(columns, places, grads, order, gains):
    shards, rows, width = columns[0].shape
    pieces = len(columns)
    out = grads[0][2].shape[2]
    arrays = [array for _, _, array in grads]
    return call(
        functools.partial(weight_grad_kernel, [(slot, first) for slot, first, _ in grads], pieces),
        (pieces,),
        [pl.BlockSpec((1, 1, width), lambda i, order, places: (places[i], 0, 0))]
        + [whole(array.shape) for array in list(columns) + arrays],
        pl.BlockSpec((3, width, out), lambda i, order, places: (0, places[i], 0)),
        jax.ShapeDtypeStruct((3, pieces * width, out), f32),
        [],
        6 * shards * pieces * rows * width * out,
        2 * shards * pieces * rows * width + 6 * shards * rows * out + 12 * pieces * width * out,
        prefetch=2,
    )(order, places, gains, *columns, *arrays)


def fir(source, taps, target, mixed, mixed_taps, base, rows, forward):
    stride = rows // 8
    steps = stride // 4
    tap_count = taps.shape[0]
    quarter = tap_count // 4
    span = steps + quarter

    def row(position):
        return base + (position if forward else stride - 1 - position)

    def combine(x):
        even, odd, low, high = x[0] + x[2], x[1] + x[3], x[0] + x[1], x[2] + x[3]
        return [x[0], x[2], even, x[1], x[3], odd, low, high, even + odd]

    def mix(n, carry):
        first = 4 * (n - quarter)
        values = [source[pl.ds(row(first + p), 8, stride=stride), :] for p in range(4)]
        for c, value in enumerate(combine(values)):
            mixed[c, n] = value
        return carry

    lax.fori_loop(0, span, mix, 0, unroll=7 if span % 7 == 0 else 1)
    for c, value in enumerate(combine([taps[pl.ds(p, quarter, stride=4), :] for p in range(4)])):
        mixed_taps[c * quarter : (c + 1) * quarter, :] = value

    chunk = 8
    outs = steps + 1

    def product(c, carry):
        sums = [jnp.zeros((8, LANES), f32)] * outs
        for k0 in range(0, quarter, chunk):
            loaded = [mixed[c, quarter - 1 - k0 - (chunk - 1) + n] for n in range(outs + chunk - 1)]
            for k in range(chunk):
                tap = mixed_taps[pl.ds(c * quarter + k0 + k, 1), :]
                for p in range(outs):
                    sums[p] = sums[p] + tap * loaded[p + chunk - 1 - k]
        for p in range(outs):
            mixed[c, p] = sums[p]
        return carry

    lax.fori_loop(0, 9, product, 0, unroll=3)

    def finish(p, carry):
        now = [mixed[c, p + 1] for c in range(9)]
        old = [mixed[c, p] for c in range(6)]
        even_0, even_1 = now[0] + old[1], now[2] - now[0] - now[1]
        odd_0, odd_1 = now[3] + old[4], now[5] - now[3] - now[4]
        odd_old = old[5] - old[3] - old[4]
        both_0, both_1 = now[6] + mixed[7, p], now[8] - now[6] - now[7]
        values = [even_0 + odd_old, both_0 - even_0 - odd_0, even_1 + odd_0, both_1 - even_1 - odd_1]
        for n, value in enumerate(values):
            target[pl.ds(row(4 * p + n) - base, 8, stride=stride), :] = value
        return carry

    lax.fori_loop(0, steps, finish, 0, unroll=True)


def fir_scratch(rows, tap_count):
    return [
        pltpu.VMEM((9, rows // 32 + tap_count // 4, 8, LANES), f32),
        pltpu.VMEM((9 * tap_count // 4, LANES), f32),
    ]


def short_sum(source, short, j, first, rows, sign):
    total = None
    for i in range(short.shape[1]):
        term = short[j, i : i + 1, :] * source[first + sign * i : first + sign * i + rows, :]
        total = term if total is None else total + term
    return total


def look_up(token_ref, onehot):
    grid = lax.broadcasted_iota(jnp.int32, onehot.shape, 1)
    onehot[...] = (grid == token_ref[...]).astype(f32).astype(bf16)


def first_forward_kernel(
    front, rows, places, token_ref, e_ref, short_ref, medium_ref, *refs,
):
    p_refs = refs[: len(places)]
    refs = refs[len(places) :]
    middle_ref, filtered_ref, onehot, table, projected, gated, taps, kept, *mixed = refs
    window, vocab = onehot.shape

    @pl.when(pl.program_id(0) == 0)
    def _():
        look_up(token_ref, onehot)

    taps[...] = medium_ref[...].astype(f32)
    extended = rows + 2 * EDGE
    for j in range(3):
        for place, p_ref in zip(places, p_refs):
            table[place : place + p_ref.shape[1], j * LANES : (j + 1) * LANES] = p_ref[j]
    looked = jnp.dot(onehot[...], table[...], preferred_element_type=f32)
    product = None
    for j in (1, 2, 0):
        projected[...] = looked[:, j * LANES : (j + 1) * LANES]
        if j == 0:
            kept[...] = short_sum(projected, short_ref, j, front - EDGE, extended, -1)
        else:
            feature = short_sum(projected, short_ref, j, 8, window - 8, -1)
            product = feature if product is None else product * feature
    gated[8:, :] = product.astype(bf16).astype(f32)
    fir(gated, taps, projected, *mixed, front - EDGE, extended, True)
    filtered = projected[:extended, :]
    filtered_ref[...] = filtered[EDGE:, :]
    embedded = jnp.dot(onehot[front - EDGE :, :], e_ref[...], preferred_element_type=f32)
    middle_ref[...] = (embedded + kept[...] * filtered).astype(bf16)


def first_forward(tokens, tables, embedding, short, medium, rows, front):
    share = tables[0][2].shape[1]
    places = [slot * share + first for slot, first, _ in tables]
    tables = [table for _, _, table in tables]
    extended = rows + 2 * EDGE
    window = front + rows + EDGE
    vocab = embedding.shape[0]
    columns = embedding.shape[1]
    shapes = [
        jax.ShapeDtypeStruct((extended, columns), bf16),
        jax.ShapeDtypeStruct((rows + EDGE, columns), f32),
    ]
    return call(
        functools.partial(first_forward_kernel, front, rows, places),
        (columns // LANES,),
        [pl.BlockSpec((window, 1), lambda i, *_: (0, 0))]
        + [lanes(a.shape) for a in (embedding, short, medium, *tables)],
        [lanes(s.shape) for s in shapes],
        shapes,
        [
            pltpu.VMEM((window, vocab), bf16),
            pltpu.VMEM((vocab, 3 * LANES), bf16),
            pltpu.VMEM((window, LANES), f32),
            pltpu.VMEM((window, LANES), f32),
            pltpu.VMEM((medium.shape[0], LANES), f32),
            pltpu.VMEM((extended, LANES), f32),
        ]
        + fir_scratch(extended, medium.shape[0]),
        8 * window * vocab * columns + 250 * VECTOR * rows * columns,
        8 * window * columns,
    )(tokens[:window], embedding, short, medium, *tables)


def first_features_kernel(places, token_ref, short_ref, *refs):
    p_refs = refs[: len(places)]
    feature_ref, onehot, table, projected = refs[len(places) :]

    @pl.when(pl.program_id(0) == 0)
    def _():
        look_up(token_ref, onehot)

    for j in range(3):
        for place, p_ref in zip(places, p_refs):
            table[place : place + p_ref.shape[1], :] = p_ref[j]
        projected[...] = jnp.dot(onehot[...], table[...], preferred_element_type=f32)
        feature_ref[j] = short_sum(projected, short_ref, j, EDGE, feature_ref.shape[1], -1)


def first_features(tokens, tables, short):
    share = tables[0][2].shape[1]
    places = [slot * share + first for slot, first, _ in tables]
    vocab = share * (1 + max(slot for slot, _, _ in tables))
    tables = [table for _, _, table in tables]
    window = tokens.shape[0]
    columns = tables[0].shape[2]
    shape = jax.ShapeDtypeStruct((3, window - EDGE, columns), f32)
    return call(
        functools.partial(first_features_kernel, places),
        (columns // LANES,),
        [whole((window, 1))] + [lanes(a.shape) for a in (short, *tables)],
        lanes(shape.shape),
        shape,
        [
            pltpu.VMEM((window, vocab), bf16),
            pltpu.VMEM((vocab, LANES), bf16),
            pltpu.VMEM((window, LANES), f32),
        ],
        6 * window * vocab * columns + 50 * VECTOR * window * columns,
        16 * window * columns,
    )(tokens, short, *tables)


def first_backward_kernel(
    rows, token_ref, above_ref, halo_ref, feature_ref, filtered_ref, short_ref, medium_ref,
    out_ref, onehot, signal, grad_gated, taps, held, *mixed,
):
    vocab = onehot.shape[0]
    parts = out_ref.shape[0]

    @pl.when(pl.program_id(0) == 0)
    def _():
        grid = lax.broadcasted_iota(jnp.int32, (vocab, rows), 0)
        onehot[...] = (grid == token_ref[...]).astype(f32).astype(bf16)

    taps[...] = medium_ref[...].astype(f32)
    extended = rows + EDGE
    above = jnp.concatenate([above_ref[...], halo_ref[...]], axis=0).astype(f32)
    signal[...] = (above * feature_ref[0]).astype(bf16).astype(f32)
    fir(signal, taps, grad_gated, *mixed, 0, extended + EDGE, False)

    def keep(j, value):
        held[...] = value.astype(bf16).astype(f32)
        grad = short_sum(held, short_ref, j, 0, rows, 1).astype(bf16)
        total = jnp.dot(onehot[...], grad, preferred_element_type=f32).astype(bf16)
        for part in range(parts):
            size = vocab // parts
            out_ref[part, j] = total[part * size : (part + 1) * size, :]

    keep(0, above[:extended, :] * filtered_ref[...])
    keep(1, grad_gated[:extended, :] * feature_ref[2, :extended, :])
    keep(2, grad_gated[:extended, :] * feature_ref[1, :extended, :])
    total = jnp.dot(onehot[...], above_ref[...], preferred_element_type=f32).astype(bf16)
    for part in range(parts):
        size = vocab // parts
        out_ref[part, 3] = total[part * size : (part + 1) * size, :]


def first_backward(tokens, above, halo, features, filtered, short, medium, vocab, parts):
    rows = above.shape[0]
    columns = above.shape[1]
    later = rows + halo.shape[0]
    operands = (above, halo, features, filtered, short, medium)
    shape = jax.ShapeDtypeStruct((parts, 4, vocab // parts, columns), bf16)
    return call(
        functools.partial(first_backward_kernel, rows),
        (columns // LANES,),
        [whole((1, rows))] + [lanes(a.shape) for a in operands],
        lanes(shape.shape),
        shape,
        [
            pltpu.VMEM((vocab, rows), bf16),
            pltpu.VMEM((later, LANES), f32),
            pltpu.VMEM((rows + 2 * EDGE, LANES), f32),
            pltpu.VMEM((medium.shape[0], LANES), f32),
            pltpu.VMEM((rows + EDGE, LANES), f32),
        ]
        + fir_scratch(rows + 2 * EDGE, medium.shape[0]),
        8 * rows * vocab * columns + 250 * VECTOR * rows * columns,
        16 * later * columns,
    )(tokens, *operands)


SEGMENTS = 8
SHIFT = 8


def summed(terms):
    while len(terms) > 1:
        terms = [a + b for a, b in zip(terms[::2], terms[1::2])] + terms[len(terms) // 2 * 2 :]
    return terms[0]


def scan_modes(source, decays, states, length, forward, residues, target):
    first = 0 if forward else SHIFT

    def step(i, held):
        position = first + (i if forward else length - 1 - i)
        value = source[pl.ds(position, SEGMENTS, stride=length), :]
        held = tuple(d * s + value for d, s in zip(decays, held))
        target[pl.ds(position, SEGMENTS, stride=length), :] = summed(
            [r * s for r, s in zip(residues, held)]
        )
        return held

    return lax.fori_loop(0, length, step, tuple(states), unroll=8)


def spread(ref, count):
    return [jnp.broadcast_to(ref[m : m + 1, :], (SEGMENTS, LANES)) for m in range(count)]


def second_features_kernel(
    shards, p_ref, short_ref, above_ref, rate_ref,
    feature_ref, gated_ref, signal_ref, segment_ref, closing_ref, projected, gated, signal, decay,
):
    extended = above_ref.shape[0]
    modes = rate_ref.shape[0]
    length = (extended - EDGE) // SEGMENTS
    product = None
    for j in range(3):
        projected[...] = p_ref[j].astype(f32)
        feature = short_sum(projected, short_ref, j, EDGE, extended, -1)
        feature_ref[j] = feature
        if j == 0:
            rounded = (above_ref[...].astype(f32) * feature).astype(bf16)
            signal_ref[...] = rounded
            signal[...] = rounded.astype(f32)
        else:
            product = feature if product is None else product * feature
    rounded = product.astype(bf16)
    gated_ref[...] = rounded
    gated[...] = rounded.astype(f32)
    rates = rate_ref[...]
    decay[...] = jnp.exp(-rates)
    decays = spread(decay, modes)

    def step(i, held):
        ahead = gated[pl.ds(i, SEGMENTS, stride=length), :]
        back = signal[pl.ds(SHIFT + length - 1 - i, SEGMENTS, stride=length), :]
        return tuple(
            d * s + value
            for values, value in zip((held[:modes], held[modes:]), (ahead, back))
            for d, s in zip(decays, values)
        )

    zeros = (jnp.zeros((SEGMENTS, LANES), f32),) * (2 * modes)
    ends = lax.fori_loop(0, length, step, zeros, unroll=8)
    for way in range(2):
        for m in range(modes):
            segment_ref[way, pl.ds(m, SEGMENTS, stride=modes), :] = ends[way * modes + m]
        stride = jnp.exp(-rates * length)
        total = jnp.zeros((modes, LANES), f32)
        for n in range(SEGMENTS):
            at = n if way == 0 else SEGMENTS - 1 - n
            total = stride * total + segment_ref[way, at * modes : (at + 1) * modes, :]
        for shard in range(shards):
            closing_ref[shard, way] = total


def second_features(projected, short, above, rates, shards):
    extended, columns = above.shape
    modes = rates.shape[0]
    shapes = [
        jax.ShapeDtypeStruct((3, extended, columns), f32),
        jax.ShapeDtypeStruct((extended, columns), bf16),
        jax.ShapeDtypeStruct((extended, columns), bf16),
        jax.ShapeDtypeStruct((2, SEGMENTS * modes, columns), f32),
        jax.ShapeDtypeStruct((shards, 2, modes, columns), f32),
    ]
    return call(
        functools.partial(second_features_kernel, shards),
        (columns // LANES,),
        [lanes(a.shape) for a in (projected, short, above, rates)],
        [lanes(s.shape) for s in shapes],
        shapes,
        [
            pltpu.VMEM((extended + EDGE, LANES), f32),
            pltpu.VMEM((extended, LANES), f32),
            pltpu.VMEM((extended, LANES), f32),
            pltpu.VMEM((modes, LANES), f32),
        ],
        120 * VECTOR * extended * columns,
        24 * extended * columns,
    )(projected, short, above, rates)


def second_filter_kernel(
    shards, seq_ref, feature_ref, gated_ref, signal_ref, segment_ref, closing_ref, rate_ref,
    residue_ref, above_ref, middle_ref, p_ref, short_ref, scale_ref,
    out_ref, top_ref, bottom_ref, term_ref,
    entering, source, filtered, grad_gated, decay, residue, ends, held,
):
    rows = out_ref.shape[0]
    modes = rate_ref.shape[0]
    length = rows // SEGMENTS
    reach = rows + SHIFT
    me = seq_ref[0]
    rates = rate_ref[...]
    decay[...] = jnp.exp(-rates)
    residue[...] = residue_ref[...]
    stride = jnp.exp(-rates * length)
    for way, (values, target) in enumerate(((gated_ref, filtered), (signal_ref, grad_gated))):
        source[way] = values[...].astype(f32)
        state = jnp.zeros((modes, LANES), f32)
        for shard in range(shards):
            ahead = me - 1 - shard if way == 0 else shard - me - 1
            weight = jnp.exp(-rates * (rows * jnp.maximum(ahead, 0)).astype(f32))
            state = state + jnp.where(ahead >= 0, weight * closing_ref[shard, way], 0.0)
        for n in range(SEGMENTS):
            at = n if way == 0 else SEGMENTS - 1 - n
            entering[at * modes : (at + 1) * modes, :] = state
            state = stride * state + segment_ref[way, at * modes : (at + 1) * modes, :]
        ends[way] = state
        starts = [entering[pl.ds(m, SEGMENTS, stride=modes), :] for m in range(modes)]
        scan_modes(
            source.at[way], spread(decay, modes), starts, length, way == 0,
            spread(residue, modes), target,
        )

    upper = lax.broadcasted_iota(jnp.int32, (SEGMENTS, LANES), 0) < SEGMENTS // 2
    decays, residues = spread(decay, modes), spread(residue, modes)
    states = [
        jnp.where(upper, a, b)
        for a, b in zip(spread(ends.at[0], modes), spread(ends.at[1], modes))
    ]
    for i in range(SHIFT):
        after, before = rows + i, SHIFT - 1 - i
        value = jnp.where(upper, source[0, after : after + 1, :], source[1, before : before + 1, :])
        states = [d * s + value for d, s in zip(decays, states)]
        result = summed([r * s for r, s in zip(residues, states)])
        filtered[after : after + 1, :] = result[:1, :]
        grad_gated[before : before + 1, :] = result[SEGMENTS // 2 : SEGMENTS // 2 + 1, :]

    out_ref[...] = (
        middle_ref[EDGE : EDGE + rows, :].astype(f32) + feature_ref[0, :rows, :] * filtered[:rows, :]
    ).astype(bf16)
    above = above_ref[...].astype(f32)[:reach, :]
    scale = scale_ref[EDGE : EDGE + rows, :]
    terms = None
    for j in range(3):
        if j == 0:
            grad = above * filtered[...]
        else:
            grad = grad_gated[...] * feature_ref[3 - j, :reach, :]
        held[...] = grad.astype(bf16).astype(f32)
        grad = short_sum(held, short_ref, j, 0, rows, 1)
        term = grad * p_ref[j, EDGE : EDGE + rows, :].astype(f32)
        terms = term if terms is None else terms + term
        scaled = (grad * scale).astype(bf16)
        top_ref[j] = scaled[: rows // 2, :]
        bottom_ref[j] = scaled[rows // 2 :, :]
    total = jnp.sum(terms, axis=1, keepdims=True)

    @pl.when(pl.program_id(0) == 0)
    def _():
        term_ref[...] = total

    @pl.when(pl.program_id(0) > 0)
    def _():
        term_ref[...] += total


def second_filter(
    seq, features, gated, signal, segments, closings, rates, residues, above, middle, projected,
    short, scale,
):
    extended, columns = above.shape
    rows = extended - EDGE
    modes = rates.shape[0]
    shapes = [
        jax.ShapeDtypeStruct((rows, columns), bf16),
        jax.ShapeDtypeStruct((3, rows // 2, columns), bf16),
        jax.ShapeDtypeStruct((3, rows // 2, columns), bf16),
        jax.ShapeDtypeStruct((rows, 1), f32),
    ]
    operands = (
        features, gated, signal, segments, closings, rates, residues, above, middle, projected, short,
    )
    return call(
        functools.partial(second_filter_kernel, closings.shape[0]),
        (columns // LANES,),
        [lanes(a.shape) for a in operands] + [whole(scale.shape)],
        [lanes(s.shape) for s in shapes[:3]] + [whole((rows, 1))],
        shapes,
        [pltpu.VMEM((SEGMENTS * modes, LANES), f32), pltpu.VMEM((2, extended, LANES), f32)]
        + [pltpu.VMEM((rows + SHIFT, LANES), f32)] * 2
        + [pltpu.VMEM((modes, LANES), f32)] * 2
        + [pltpu.VMEM((2, modes, LANES), f32), pltpu.VMEM((rows + SHIFT, LANES), f32)],
        250 * VECTOR * rows * columns,
        40 * rows * columns,
        prefetch=1,
    )(seq, *operands, scale)


def shift(value, axis, by):
    devices = lax.axis_size(axis)
    pairs = [(i, i + by) for i in range(devices) if 0 <= i + by < devices]
    return lax.ppermute(value, axis, pairs)


def gather_ch(value):
    return lax.all_gather(value, "ch", axis=0, tiled=False)


def scatter_ch(value):
    return lax.psum_scatter(value, "ch", scatter_dimension=0, tiled=False)


def exchange_seq(value):
    return lax.all_to_all(value, "seq", split_axis=0, concat_axis=0, tiled=True)


def gather_seq(value):
    return exchange_seq(jnp.broadcast_to(value[None], (lax.axis_size("seq"),) + value.shape))


def seq_ring():
    devices = lax.axis_size("seq")
    if devices % 2:
        return list(range(devices))
    return list(range(0, devices, 2)) + list(range(devices - 1, 0, -2))


def seq_hop(value, by):
    ring = seq_ring()
    pairs = [(ring[i], ring[(i + by) % len(ring)]) for i in range(len(ring))]
    return lax.ppermute(value, "seq", pairs)


def ring_gather(parts):
    shards = lax.axis_size("seq")
    firsts = [0, parts[0].shape[1]][: len(parts)]
    out = [(0, first, part) for first, part in zip(firsts, parts)]
    up = down = parts
    for step in range(1, (shards + 1) // 2):
        up, down = [seq_hop(a, 1) for a in up], [seq_hop(a, -1) for a in down]
        out += [(shards - step, first, part) for first, part in zip(firsts, up)]
        out += [(step, first, part) for first, part in zip(firsts, down)]
    if shards % 2 == 0:
        if len(parts) == 1:
            half = parts[0].shape[1] // 2
            up, down = [up[0][:, :half]], [down[0][:, half:]]
        else:
            half = firsts[1]
        out += [(shards // 2, 0, seq_hop(up[0], 1)), (shards // 2, half, seq_hop(down[-1], -1))]
    return out


def ring_order():
    ring = seq_ring()
    twice = jnp.array(ring + ring, jnp.int32)
    place = jnp.argmax(twice[: len(ring)] == lax.axis_index("seq")).astype(jnp.int32)
    return lax.dynamic_slice_in_dim(twice, place, len(ring), 0)


def ch_hop(value, by):
    devices = lax.axis_size("ch")
    pairs = [(i, (i + 2 * by) % devices) for i in range(devices)]
    return lax.ppermute(value, "ch", pairs)


def sibling(value):
    return lax.ppermute(value, "ch", [(i, i ^ 1) for i in range(lax.axis_size("ch"))])


def scatter_order():
    devices = lax.axis_size("ch")
    me = lax.axis_index("ch")
    places = jnp.arange(devices // 2, dtype=jnp.int32)
    return jnp.stack([(2 * places + other) % devices for other in (me, me ^ 1)], axis=1).reshape(-1)


def added(*terms):
    return functools.reduce(lambda a, b: a + b, [t.astype(f32) for t in terms])


def ring_scatter(pieces, other_pieces, near, far):
    half = pieces.shape[0]
    other_pieces, *near = tie(other_pieces, *near)
    mine = added(pieces, sibling(other_pieces)).astype(bf16)
    if half == 1:
        return mine[0].astype(f32), near, far
    steps = (half - 1) // 2
    rows = mine.shape[1]
    middle = rows // 32 * 16
    up = down = None
    if half % 2 == 0:
        opposite = mine[half // 2]
        up, down = ch_hop(opposite[:middle], 1), ch_hop(opposite[middle:], -1)
        if half == 2:
            return added(mine[0], jnp.concatenate([up, down], axis=0)), near, far
    for step in range(steps, 0, -1):
        first, second = mine[step], mine[half - step]
        if up is not None and step == steps and half % 2 == 0:
            first = jnp.concatenate(
                [added(first[:middle], up).astype(bf16), first[middle:]], axis=0
            )
            second = jnp.concatenate(
                [second[:middle], added(second[middle:], down).astype(bf16)], axis=0
            )
        elif up is not None:
            first, second = added(first, up).astype(bf16), added(second, down).astype(bf16)
        up, down = ch_hop(first, 1), ch_hop(second, -1)
    up, down, *far = tie(up, down, *far)
    return added(mine[0], up, down), near, far


def tie(*values):
    return lax.optimization_barrier(values)


def per_device(
    token_ids,
    embedding,
    gain_first,
    gain_second,
    weights_first,
    weights_second,
    short_first,
    short_second,
    medium,
    residues,
    decay_rates,
    cotangent,
):
    shards = lax.axis_size("seq")
    pieces = lax.axis_size("ch")
    seq = lax.axis_index("seq")
    vocab, width = embedding.shape
    rows = token_ids.shape[0]
    features = width * pieces
    taps, tap_count = medium.shape[0], short_first.shape[0]
    front = round_up(EDGE + taps - 1 + tap_count - 1, 16)
    back = round_up(2 * EDGE + taps - 1, 16)
    w_first, w_second = (jnp.transpose(w, (1, 0, 2)) for w in (weights_first, weights_second))
    s_first, s_second = (jnp.transpose(s, (1, 0, 2)) for s in (short_first, short_second))

    order = ring_order()
    each = pieces // shards
    share = vocab // shards
    at = seq * share

    row = lax.broadcasted_iota(jnp.int32, (EDGE, width), 0)
    gains = jnp.where(row == 0, gain_first, jnp.where(row == 1, gain_second, jnp.zeros((), bf16)))
    own_embedding = lax.dynamic_slice_in_dim(embedding, at, share, 0)
    gathered = gather_ch(jnp.concatenate([own_embedding, gains], axis=0))
    tokens = lax.all_gather(token_ids, "seq", axis=0, tiled=True)
    slots = jnp.zeros(shards, jnp.int32).at[order].set(jnp.arange(shards, dtype=jnp.int32))
    turned = jnp.take(embedding.reshape(shards, share, width), order, axis=0)
    turned = turned.reshape(vocab, width)
    tokens = jnp.take(slots, tokens // share) * share + tokens % share
    tokens = jnp.pad(tokens, (front, back), constant_values=-1)
    tokens = lax.dynamic_slice_in_dim(tokens, seq * rows, front + rows + back, 0)
    behind = shift(cotangent[:EDGE], "seq", -1)
    cotangents = jnp.concatenate([cotangent, behind], axis=0)
    tokens, turned, cotangents, gathered = tie(tokens[:, None], turned, cotangents, gathered)
    gains_first = gathered[:, share : share + 1, :].astype(f32)
    gains_second = gathered[:, share + 1 : share + 2, :].astype(f32)
    own_table, own_scale = project(gathered, gathered, share, 0, w_first, share)
    tables = ring_gather([own_table])

    middle, filtered_first = first_forward(tokens, tables, turned, s_first, medium, rows, front)
    later, held = tie(tokens[front - EDGE :], middle)
    features_first = first_features(later, tables, s_first)

    middles = gather_ch(middle)
    block = exchange_seq(gathered[:, :share, :].reshape(shards, each, share, width))
    blocks = [block[:, i] for i in range(each)]
    block_gains = [
        lax.dynamic_slice_in_dim(g, seq * each, each, 0) for g in (gains_first, gains_second)
    ]
    core = lax.axis_index("ch") % each
    places = jnp.stack([core, 1 - core]).astype(jnp.int32)
    straight, scattered = jnp.arange(pieces, dtype=jnp.int32), scatter_order()
    blank = jnp.zeros((EDGE, width), bf16)
    features_first, places, straight, scattered, blank, middles, *rest = tie(
        features_first, places, straight, scattered, blank, middles, *blocks, *block_gains
    )
    blocks, block_gains = rest[:each], rest[each:]
    own = middles.reshape(shards, each, rows + 2 * EDGE, width)
    own = lax.dynamic_slice(own, (0, core, EDGE, 0), (shards, 1, rows, width))
    projected, scale = project(middles, gathered, share, 1, w_second, rows + 2 * EDGE)
    features_second, gated, signal, segments, closing = second_features(
        projected, s_second, cotangents, decay_rates, shards
    )
    own, closings = tie(own[:, 0], exchange_seq(closing))
    columns = exchange_seq(own)
    output, *grads, terms = second_filter(
        seq[None], features_second, gated, signal, segments, closings,
        decay_rates, residues, cotangents, middle, projected, s_second, scale,
    )
    scale = scale[EDGE : EDGE + rows]
    pieces_of = ring_gather(grads)
    (partial,) = project_back(grads, w_second, straight, blank, False)
    partial, columns = tie(partial, columns)
    other = sibling(columns)
    partial_sum = scatter_ch(partial)
    terms = lax.psum(terms[:, 0], "ch")
    partial_sum, other, *arrays = tie(partial_sum, other, *[a for _, _, a in pieces_of[2:-2]])
    pieces_of[2:-2] = [old[:2] + (new,) for old, new in zip(pieces_of[2:-2], arrays)]
    grad_normed = partial_sum.astype(f32)
    as_float = middle[EDGE : EDGE + rows].astype(f32)
    grad_middle = (
        cotangent.astype(f32)
        + gain_second.astype(f32) * grad_normed
        - as_float * (scale * scale) * terms[:, None] / features
    ).astype(bf16)
    grad_gain_second = jnp.sum(grad_normed * as_float, axis=0)

    halo = shift(grad_middle[:back], "seq", -1)
    halo, far_up, far_down = tie(halo, pieces_of[-2][2], pieces_of[-1][2])
    pieces_of[-2:] = [pieces_of[-2][:2] + (far_up,), pieces_of[-1][:2] + (far_down,)]
    sums = first_backward(
        token_ids[None], grad_middle, halo, features_first, filtered_first, s_first, medium, vocab,
        shards,
    )
    sums = exchange_seq(sums)
    grad_weights_second = weight_grad(
        [columns, other], places, pieces_of, order, block_gains[1]
    )
    sums, grad_weights_second = tie(sums, grad_weights_second)
    own_sums = jnp.sum(sums.astype(f32), axis=0)
    terms = jnp.sum(own_sums[:3] * own_table.astype(f32), axis=(0, 2))
    own_grads = (own_sums[:3] * own_scale[None]).astype(bf16)
    all_grads = ring_gather([own_grads])
    extra_rows = -(-share // width)
    extra = jnp.pad(terms, (0, EDGE * width - share)).reshape(EDGE, width).astype(bf16)
    partial, other_partial = project_back([own_grads], w_first, scattered, extra, True)
    grad_normed, near, far = ring_scatter(
        partial, other_partial, [a for _, _, a in all_grads[1:-2]], [a for _, _, a in all_grads[-2:]]
    )
    all_grads[1:] = [old[:2] + (new,) for old, new in zip(all_grads[1:], near + far)]
    terms = grad_normed[share : share + extra_rows].reshape(-1)[:share]
    grad_normed = grad_normed[:share]
    grad_weights_first = weight_grad(blocks, straight, all_grads, order, block_gains[0])

    as_float = own_embedding.astype(f32)
    grad_embedding = (
        own_sums[3]
        + gain_first.astype(f32) * grad_normed
        - as_float * (own_scale * own_scale) * terms[:, None] / features
    )
    grad_gain_first = jnp.sum(grad_normed * as_float, axis=0)
    last = jnp.concatenate(
        [
            grad_embedding,
            grad_gain_first[None],
            grad_gain_second[None],
            jnp.zeros((EDGE - 2, width), f32),
        ],
        axis=0,
    ).astype(bf16)
    last = gather_seq(last).astype(f32)
    return (
        output,
        last[:, :share].reshape(vocab, width),
        jnp.sum(last[:, share], axis=0),
        jnp.sum(last[:, share + 1], axis=0),
        jnp.transpose(grad_weights_first, (1, 0, 2)),
        jnp.transpose(grad_weights_second, (1, 0, 2)),
    )


def solution(mesh):
    placed = (
        P("seq"),
        P(None, "ch"),
        P("ch"),
        P("ch"),
        P(None, None, "ch"),
        P(None, None, "ch"),
        P(None, None, "ch"),
        P(None, None, "ch"),
        P(None, "ch"),
        P(None, "ch"),
        P(None, "ch"),
        P("seq", "ch"),
    )
    return jax.shard_map(
        per_device,
        mesh=mesh,
        in_specs=placed,
        out_specs=(
            P("seq", "ch"),
            P(None, "ch"),
            P("ch"),
            P("ch"),
            P("seq", None, "ch"),
            P("seq", None, "ch"),
        ),
        check_vma=False,
    )
```

```python
import functools

import jax
import jax.numpy as jnp
from jax import lax
from jax.experimental import pallas as pl
from jax.experimental.pallas import tpu as pltpu
from jax.sharding import PartitionSpec as P

epsilon = 1e-06
f32 = jnp.float32
bf16 = jnp.bfloat16
LANES = 128
EDGE = 16
VECTOR = 160


def round_up(value, multiple):
    return -(-value // multiple) * multiple


def call(kernel, grid, in_specs, out_specs, out_shape, scratch, flops, moved, prefetch=0):
    return pl.pallas_call(
        kernel,
        grid_spec=pltpu.PrefetchScalarGridSpec(
            num_scalar_prefetch=prefetch,
            grid=grid,
            in_specs=in_specs,
            out_specs=out_specs,
            scratch_shapes=scratch,
        ),
        out_shape=out_shape,
        compiler_params=pltpu.CompilerParams(vmem_limit_bytes=54 * 2**20),
        cost_estimate=pl.CostEstimate(flops=flops, bytes_accessed=moved, transcendentals=0),
    )


def whole(shape):
    return pl.BlockSpec(shape, lambda i, *_: (0,) * len(shape))


def lanes(shape):
    return pl.BlockSpec(shape[:-1] + (LANES,), lambda i, *_: (0,) * (len(shape) - 1) + (i,))


def project_kernel(
    per_step, features, rows, gain_row, x_ref, gain_ref, w_ref, p_ref, scale_ref, total, squares
):
    step = pl.program_id(0)
    width = x_ref.shape[2]

    @pl.when(step == 0)
    def _():
        total[...] = jnp.zeros_like(total)
        squares[...] = jnp.zeros_like(squares)

    for part in range(per_step):
        x = x_ref[part, :rows, :].astype(f32)
        square = x * x
        running = squares[...]
        for lane in range(width // LANES):
            running = running + square[:, lane * LANES : (lane + 1) * LANES]
        squares[...] = running
        gain = gain_ref[part, gain_row : gain_row + 1, :].astype(f32)
        scaled = (x * gain).astype(bf16)
        for j in range(3):
            total[j] += jnp.dot(
                scaled, w_ref[j, part * width : (part + 1) * width, :], preferred_element_type=f32
            )

    @pl.when(step == pl.num_programs(0) - 1)
    def _():
        mean = jnp.sum(squares[...], axis=1, keepdims=True) / features
        scale = lax.rsqrt(mean + epsilon)
        scale_ref[...] = scale
        for j in range(3):
            p_ref[j] = (total[j] * scale).astype(bf16)


def project(chunks, gains, gain_block, gain_row, weights, rows):
    count, _, width = chunks.shape
    features, columns = weights.shape[1:]
    per_step = 2 if count % 2 == 0 else 1
    return call(
        functools.partial(project_kernel, per_step, features, rows, gain_row),
        (count // per_step,),
        [
            pl.BlockSpec((per_step, chunks.shape[1], width), lambda i: (i, 0, 0)),
            pl.BlockSpec((per_step, EDGE, width), lambda i: (i, gain_block // EDGE, 0)),
            pl.BlockSpec((3, per_step * width, columns), lambda i: (0, i, 0)),
        ],
        [whole((3, rows, columns)), whole((rows, 1))],
        [
            jax.ShapeDtypeStruct((3, rows, columns), bf16),
            jax.ShapeDtypeStruct((rows, 1), f32),
        ],
        [pltpu.VMEM((3, rows, columns), f32), pltpu.VMEM((rows, LANES), f32)],
        6 * rows * features * columns,
        6 * features * columns + 2 * rows * features,
    )(chunks, gains, weights)


def back_kernel(parts, apart, order_ref, *refs):
    g_refs, w_refs = refs[:parts], refs[parts : parts + 2]
    extra_ref, *o_refs, grads = refs[parts + 2 :]
    rows, columns = grads.shape[0], grads.shape[1] // 3

    @pl.when(pl.program_id(0) == 0)
    def _():
        first = 0
        for g_ref in g_refs:
            more = g_ref.shape[1]
            for j in range(3):
                grads[first : first + more, j * columns : (j + 1) * columns] = g_ref[j]
            first += more

    for piece, w_ref in enumerate(w_refs):
        o_ref, at = (o_refs[piece], 0) if apart else (o_refs[0], piece)
        weights = jnp.concatenate([w_ref[j] for j in range(3)], axis=1)
        o_ref[at, :rows, :] = lax.dot_general(
            grads[...], weights, (((1,), (1,)), ((), ())), preferred_element_type=f32
        ).astype(bf16)
        if o_ref.shape[1] > rows:
            o_ref[at, rows:, :] = extra_ref[...]


def project_back(parts, weights, order, extra, apart):
    columns = parts[0].shape[2]
    rows = sum(part.shape[1] for part in parts)
    features = weights.shape[1]
    count = order.shape[0]
    width = features // count
    high = rows + (extra.shape[0] if apart else 0)
    each = 1 if apart else 2
    out = jax.ShapeDtypeStruct((count * each // 2, high, width), bf16)
    return call(
        functools.partial(back_kernel, len(parts), apart),
        (count // 2,),
        [whole(part.shape) for part in parts]
        + [
            pl.BlockSpec((3, width, columns), lambda i, order: (0, order[2 * i], 0)),
            pl.BlockSpec((3, width, columns), lambda i, order: (0, order[2 * i + 1], 0)),
            whole(extra.shape),
        ],
        [pl.BlockSpec((each, high, width), lambda i, *_: (i, 0, 0))] * (2 // each),
        [out] * (2 // each),
        [pltpu.VMEM((rows, 3 * columns), bf16)],
        6 * rows * features * columns,
        6 * features * columns + 2 * rows * features,
        prefetch=1,
    )(order, *parts, weights, weights, extra)


def weight_grad_kernel(spans, pieces, order_ref, piece_ref, gain_ref, *refs):
    x_refs, g_refs, out_ref = refs[:pieces], refs[pieces:-1], refs[-1]
    gain = jnp.broadcast_to(gain_ref[0], (8, gain_ref.shape[2])).T[:, :1]

    for piece, x_ref in enumerate(x_refs):

        @pl.when(pl.program_id(0) == piece)
        def _(x_ref=x_ref):
            for j in range(3):
                total = None
                for (slot, first), g_ref in zip(spans, g_refs):
                    some = x_ref[order_ref[slot], first : first + g_ref.shape[1], :]
                    term = lax.dot_general(
                        some, g_ref[j], (((0,), (0,)), ((), ())), preferred_element_type=f32
                    )
                    total = term if total is None else total + term
                out_ref[j] = total * gain


def weight_grad(columns, places, grads, order, gains):
    shards, rows, width = columns[0].shape
    pieces = len(columns)
    out = grads[0][2].shape[2]
    arrays = [array for _, _, array in grads]
    return call(
        functools.partial(weight_grad_kernel, [(slot, first) for slot, first, _ in grads], pieces),
        (pieces,),
        [pl.BlockSpec((1, 1, width), lambda i, order, places: (places[i], 0, 0))]
        + [whole(array.shape) for array in list(columns) + arrays],
        pl.BlockSpec((3, width, out), lambda i, order, places: (0, places[i], 0)),
        jax.ShapeDtypeStruct((3, pieces * width, out), f32),
        [],
        6 * shards * pieces * rows * width * out,
        2 * shards * pieces * rows * width + 6 * shards * rows * out + 12 * pieces * width * out,
        prefetch=2,
    )(order, places, gains, *columns, *arrays)


def fir(source, taps, target, mixed, mixed_taps, base, rows, forward):
    stride = rows // 8
    steps = stride // 4
    tap_count = taps.shape[0]
    quarter = tap_count // 4
    span = steps + quarter

    def row(position):
        return base + (position if forward else stride - 1 - position)

    def combine(x):
        even, odd, low, high = x[0] + x[2], x[1] + x[3], x[0] + x[1], x[2] + x[3]
        return [x[0], x[2], even, x[1], x[3], odd, low, high, even + odd]

    def mix(n, carry):
        first = 4 * (n - quarter)
        values = [source[pl.ds(row(first + p), 8, stride=stride), :] for p in range(4)]
        for c, value in enumerate(combine(values)):
            mixed[c, n] = value
        return carry

    lax.fori_loop(0, span, mix, 0, unroll=7 if span % 7 == 0 else 1)
    for c, value in enumerate(combine([taps[pl.ds(p, quarter, stride=4), :] for p in range(4)])):
        mixed_taps[c * quarter : (c + 1) * quarter, :] = value

    chunk = 8
    outs = steps + 1

    def product(c, carry):
        sums = [jnp.zeros((8, LANES), f32)] * outs
        for k0 in range(0, quarter, chunk):
            loaded = [mixed[c, quarter - 1 - k0 - (chunk - 1) + n] for n in range(outs + chunk - 1)]
            for k in range(chunk):
                tap = mixed_taps[pl.ds(c * quarter + k0 + k, 1), :]
                for p in range(outs):
                    sums[p] = sums[p] + tap * loaded[p + chunk - 1 - k]
        for p in range(outs):
            mixed[c, p] = sums[p]
        return carry

    lax.fori_loop(0, 9, product, 0, unroll=3)

    def finish(p, carry):
        now = [mixed[c, p + 1] for c in range(9)]
        old = [mixed[c, p] for c in range(6)]
        even_0, even_1 = now[0] + old[1], now[2] - now[0] - now[1]
        odd_0, odd_1 = now[3] + old[4], now[5] - now[3] - now[4]
        odd_old = old[5] - old[3] - old[4]
        both_0, both_1 = now[6] + mixed[7, p], now[8] - now[6] - now[7]
        values = [even_0 + odd_old, both_0 - even_0 - odd_0, even_1 + odd_0, both_1 - even_1 - odd_1]
        for n, value in enumerate(values):
            target[pl.ds(row(4 * p + n) - base, 8, stride=stride), :] = value
        return carry

    lax.fori_loop(0, steps, finish, 0, unroll=True)


def fir_scratch(rows, tap_count):
    return [
        pltpu.VMEM((9, rows // 32 + tap_count // 4, 8, LANES), f32),
        pltpu.VMEM((9 * tap_count // 4, LANES), f32),
    ]


def short_sum(source, short, j, first, rows, sign):
    total = None
    for i in range(short.shape[1]):
        term = short[j, i : i + 1, :] * source[first + sign * i : first + sign * i + rows, :]
        total = term if total is None else total + term
    return total


def look_up(token_ref, onehot):
    grid = lax.broadcasted_iota(jnp.int32, onehot.shape, 1)
    onehot[...] = (grid == token_ref[...]).astype(f32).astype(bf16)


def first_forward_kernel(
    front, rows, places, token_ref, e_ref, short_ref, medium_ref, *refs,
):
    p_refs = refs[: len(places)]
    refs = refs[len(places) :]
    middle_ref, filtered_ref, onehot, table, projected, gated, taps, kept, *mixed = refs
    window, vocab = onehot.shape

    @pl.when(pl.program_id(0) == 0)
    def _():
        look_up(token_ref, onehot)

    taps[...] = medium_ref[...].astype(f32)
    extended = rows + 2 * EDGE
    for j in range(3):
        for place, p_ref in zip(places, p_refs):
            table[place : place + p_ref.shape[1], j * LANES : (j + 1) * LANES] = p_ref[j]
    looked = jnp.dot(onehot[...], table[...], preferred_element_type=f32)
    product = None
    for j in (1, 2, 0):
        projected[...] = looked[:, j * LANES : (j + 1) * LANES]
        if j == 0:
            kept[...] = short_sum(projected, short_ref, j, front - EDGE, extended, -1)
        else:
            feature = short_sum(projected, short_ref, j, 8, window - 8, -1)
            product = feature if product is None else product * feature
    gated[8:, :] = product.astype(bf16).astype(f32)
    fir(gated, taps, projected, *mixed, front - EDGE, extended, True)
    filtered = projected[:extended, :]
    filtered_ref[...] = filtered[EDGE:, :]
    embedded = jnp.dot(onehot[front - EDGE :, :], e_ref[...], preferred_element_type=f32)
    middle_ref[...] = (embedded + kept[...] * filtered).astype(bf16)


def first_forward(tokens, tables, embedding, short, medium, rows, front):
    share = tables[0][2].shape[1]
    places = [slot * share + first for slot, first, _ in tables]
    tables = [table for _, _, table in tables]
    extended = rows + 2 * EDGE
    window = front + rows + EDGE
    vocab = embedding.shape[0]
    columns = embedding.shape[1]
    shapes = [
        jax.ShapeDtypeStruct((extended, columns), bf16),
        jax.ShapeDtypeStruct((rows + EDGE, columns), f32),
    ]
    return call(
        functools.partial(first_forward_kernel, front, rows, places),
        (columns // LANES,),
        [pl.BlockSpec((window, 1), lambda i, *_: (0, 0))]
        + [lanes(a.shape) for a in (embedding, short, medium, *tables)],
        [lanes(s.shape) for s in shapes],
        shapes,
        [
            pltpu.VMEM((window, vocab), bf16),
            pltpu.VMEM((vocab, 3 * LANES), bf16),
            pltpu.VMEM((window, LANES), f32),
            pltpu.VMEM((window, LANES), f32),
            pltpu.VMEM((medium.shape[0], LANES), f32),
            pltpu.VMEM((extended, LANES), f32),
        ]
        + fir_scratch(extended, medium.shape[0]),
        8 * window * vocab * columns + 250 * VECTOR * rows * columns,
        8 * window * columns,
    )(tokens[:window], embedding, short, medium, *tables)


def first_features_kernel(places, token_ref, short_ref, *refs):
    p_refs = refs[: len(places)]
    feature_ref, onehot, table, projected = refs[len(places) :]

    @pl.when(pl.program_id(0) == 0)
    def _():
        look_up(token_ref, onehot)

    for j in range(3):
        for place, p_ref in zip(places, p_refs):
            table[place : place + p_ref.shape[1], :] = p_ref[j]
        projected[...] = jnp.dot(onehot[...], table[...], preferred_element_type=f32)
        feature_ref[j] = short_sum(projected, short_ref, j, EDGE, feature_ref.shape[1], -1)


def first_features(tokens, tables, short):
    share = tables[0][2].shape[1]
    places = [slot * share + first for slot, first, _ in tables]
    vocab = share * (1 + max(slot for slot, _, _ in tables))
    tables = [table for _, _, table in tables]
    window = tokens.shape[0]
    columns = tables[0].shape[2]
    shape = jax.ShapeDtypeStruct((3, window - EDGE, columns), f32)
    return call(
        functools.partial(first_features_kernel, places),
        (columns // LANES,),
        [whole((window, 1))] + [lanes(a.shape) for a in (short, *tables)],
        lanes(shape.shape),
        shape,
        [
            pltpu.VMEM((window, vocab), bf16),
            pltpu.VMEM((vocab, LANES), bf16),
            pltpu.VMEM((window, LANES), f32),
        ],
        6 * window * vocab * columns + 50 * VECTOR * window * columns,
        16 * window * columns,
    )(tokens, short, *tables)


def first_backward_kernel(
    rows, token_ref, above_ref, halo_ref, feature_ref, filtered_ref, short_ref, medium_ref,
    out_ref, onehot, signal, grad_gated, taps, held, *mixed,
):
    vocab = onehot.shape[0]
    parts = out_ref.shape[0]

    @pl.when(pl.program_id(0) == 0)
    def _():
        grid = lax.broadcasted_iota(jnp.int32, (vocab, rows), 0)
        onehot[...] = (grid == token_ref[...]).astype(f32).astype(bf16)

    taps[...] = medium_ref[...].astype(f32)
    extended = rows + EDGE
    above = jnp.concatenate([above_ref[...], halo_ref[...]], axis=0).astype(f32)
    signal[...] = (above * feature_ref[0]).astype(bf16).astype(f32)
    fir(signal, taps, grad_gated, *mixed, 0, extended + EDGE, False)

    def keep(j, value):
        held[...] = value.astype(bf16).astype(f32)
        grad = short_sum(held, short_ref, j, 0, rows, 1).astype(bf16)
        total = jnp.dot(onehot[...], grad, preferred_element_type=f32).astype(bf16)
        for part in range(parts):
            size = vocab // parts
            out_ref[part, j] = total[part * size : (part + 1) * size, :]

    keep(0, above[:extended, :] * filtered_ref[...])
    keep(1, grad_gated[:extended, :] * feature_ref[2, :extended, :])
    keep(2, grad_gated[:extended, :] * feature_ref[1, :extended, :])
    total = jnp.dot(onehot[...], above_ref[...], preferred_element_type=f32).astype(bf16)
    for part in range(parts):
        size = vocab // parts
        out_ref[part, 3] = total[part * size : (part + 1) * size, :]


def first_backward(tokens, above, halo, features, filtered, short, medium, vocab, parts):
    rows = above.shape[0]
    columns = above.shape[1]
    later = rows + halo.shape[0]
    operands = (above, halo, features, filtered, short, medium)
    shape = jax.ShapeDtypeStruct((parts, 4, vocab // parts, columns), bf16)
    return call(
        functools.partial(first_backward_kernel, rows),
        (columns // LANES,),
        [whole((1, rows))] + [lanes(a.shape) for a in operands],
        lanes(shape.shape),
        shape,
        [
            pltpu.VMEM((vocab, rows), bf16),
            pltpu.VMEM((later, LANES), f32),
            pltpu.VMEM((rows + 2 * EDGE, LANES), f32),
            pltpu.VMEM((medium.shape[0], LANES), f32),
            pltpu.VMEM((rows + EDGE, LANES), f32),
        ]
        + fir_scratch(rows + 2 * EDGE, medium.shape[0]),
        8 * rows * vocab * columns + 250 * VECTOR * rows * columns,
        16 * later * columns,
    )(tokens, *operands)


SEGMENTS = 8
SHIFT = 8


def summed(terms):
    while len(terms) > 1:
        terms = [a + b for a, b in zip(terms[::2], terms[1::2])] + terms[len(terms) // 2 * 2 :]
    return terms[0]


def scan_modes(source, decays, states, length, forward, residues, target):
    first = 0 if forward else SHIFT

    def step(i, held):
        position = first + (i if forward else length - 1 - i)
        value = source[pl.ds(position, SEGMENTS, stride=length), :]
        held = tuple(d * s + value for d, s in zip(decays, held))
        target[pl.ds(position, SEGMENTS, stride=length), :] = summed(
            [r * s for r, s in zip(residues, held)]
        )
        return held

    return lax.fori_loop(0, length, step, tuple(states), unroll=16)


def spread(ref, count):
    return [jnp.broadcast_to(ref[m : m + 1, :], (SEGMENTS, LANES)) for m in range(count)]


def second_features_kernel(
    shards, p_ref, short_ref, above_ref, rate_ref,
    feature_ref, gated_ref, signal_ref, segment_ref, closing_ref, projected, gated, signal, decay,
):
    extended = above_ref.shape[0]
    modes = rate_ref.shape[0]
    length = (extended - EDGE) // SEGMENTS
    product = None
    for j in range(3):
        projected[...] = p_ref[j].astype(f32)
        feature = short_sum(projected, short_ref, j, EDGE, extended, -1)
        feature_ref[j] = feature
        if j == 0:
            rounded = (above_ref[...].astype(f32) * feature).astype(bf16)
            signal_ref[...] = rounded
            signal[...] = rounded.astype(f32)
        else:
            product = feature if product is None else product * feature
    rounded = product.astype(bf16)
    gated_ref[...] = rounded
    gated[...] = rounded.astype(f32)
    rates = rate_ref[...]
    decay[...] = jnp.exp(-rates)
    decays = spread(decay, modes)

    def step(i, held):
        ahead = gated[pl.ds(i, SEGMENTS, stride=length), :]
        back = signal[pl.ds(SHIFT + length - 1 - i, SEGMENTS, stride=length), :]
        return tuple(
            d * s + value
            for values, value in zip((held[:modes], held[modes:]), (ahead, back))
            for d, s in zip(decays, values)
        )

    zeros = (jnp.zeros((SEGMENTS, LANES), f32),) * (2 * modes)
    ends = lax.fori_loop(0, length, step, zeros, unroll=16)
    for way in range(2):
        for m in range(modes):
            segment_ref[way, pl.ds(m, SEGMENTS, stride=modes), :] = ends[way * modes + m]
        stride = jnp.exp(-rates * length)
        total = jnp.zeros((modes, LANES), f32)
        for n in range(SEGMENTS):
            at = n if way == 0 else SEGMENTS - 1 - n
            total = stride * total + segment_ref[way, at * modes : (at + 1) * modes, :]
        for shard in range(shards):
            closing_ref[shard, way] = total


def second_features(projected, short, above, rates, shards):
    extended, columns = above.shape
    modes = rates.shape[0]
    shapes = [
        jax.ShapeDtypeStruct((3, extended, columns), f32),
        jax.ShapeDtypeStruct((extended, columns), bf16),
        jax.ShapeDtypeStruct((extended, columns), bf16),
        jax.ShapeDtypeStruct((2, SEGMENTS * modes, columns), f32),
        jax.ShapeDtypeStruct((shards, 2, modes, columns), f32),
    ]
    return call(
        functools.partial(second_features_kernel, shards),
        (columns // LANES,),
        [lanes(a.shape) for a in (projected, short, above, rates)],
        [lanes(s.shape) for s in shapes],
        shapes,
        [
            pltpu.VMEM((extended + EDGE, LANES), f32),
            pltpu.VMEM((extended, LANES), f32),
            pltpu.VMEM((extended, LANES), f32),
            pltpu.VMEM((modes, LANES), f32),
        ],
        120 * VECTOR * extended * columns,
        24 * extended * columns,
    )(projected, short, above, rates)


def second_filter_kernel(
    shards, seq_ref, feature_ref, gated_ref, signal_ref, segment_ref, closing_ref, rate_ref,
    residue_ref, above_ref, middle_ref, p_ref, short_ref, scale_ref,
    out_ref, top_ref, bottom_ref, term_ref,
    entering, source, filtered, grad_gated, decay, residue, ends, held,
):
    rows = out_ref.shape[0]
    modes = rate_ref.shape[0]
    length = rows // SEGMENTS
    reach = rows + SHIFT
    me = seq_ref[0]
    rates = rate_ref[...]
    decay[...] = jnp.exp(-rates)
    residue[...] = residue_ref[...]
    stride = jnp.exp(-rates * length)
    for way, (values, target) in enumerate(((gated_ref, filtered), (signal_ref, grad_gated))):
        source[way] = values[...].astype(f32)
        state = jnp.zeros((modes, LANES), f32)
        for shard in range(shards):
            ahead = me - 1 - shard if way == 0 else shard - me - 1
            weight = jnp.exp(-rates * (rows * jnp.maximum(ahead, 0)).astype(f32))
            state = state + jnp.where(ahead >= 0, weight * closing_ref[shard, way], 0.0)
        for n in range(SEGMENTS):
            at = n if way == 0 else SEGMENTS - 1 - n
            entering[at * modes : (at + 1) * modes, :] = state
            state = stride * state + segment_ref[way, at * modes : (at + 1) * modes, :]
        ends[way] = state
        starts = [entering[pl.ds(m, SEGMENTS, stride=modes), :] for m in range(modes)]
        scan_modes(
            source.at[way], spread(decay, modes), starts, length, way == 0,
            spread(residue, modes), target,
        )

    upper = lax.broadcasted_iota(jnp.int32, (SEGMENTS, LANES), 0) < SEGMENTS // 2
    decays, residues = spread(decay, modes), spread(residue, modes)
    states = [
        jnp.where(upper, a, b)
        for a, b in zip(spread(ends.at[0], modes), spread(ends.at[1], modes))
    ]
    for i in range(SHIFT):
        after, before = rows + i, SHIFT - 1 - i
        value = jnp.where(upper, source[0, after : after + 1, :], source[1, before : before + 1, :])
        states = [d * s + value for d, s in zip(decays, states)]
        result = summed([r * s for r, s in zip(residues, states)])
        filtered[after : after + 1, :] = result[:1, :]
        grad_gated[before : before + 1, :] = result[SEGMENTS // 2 : SEGMENTS // 2 + 1, :]

    out_ref[...] = (
        middle_ref[EDGE : EDGE + rows, :].astype(f32) + feature_ref[0, :rows, :] * filtered[:rows, :]
    ).astype(bf16)
    above = above_ref[...].astype(f32)[:reach, :]
    scale = scale_ref[EDGE : EDGE + rows, :]
    terms = None
    for j in range(3):
        if j == 0:
            grad = above * filtered[...]
        else:
            grad = grad_gated[...] * feature_ref[3 - j, :reach, :]
        held[...] = grad.astype(bf16).astype(f32)
        grad = short_sum(held, short_ref, j, 0, rows, 1)
        term = grad * p_ref[j, EDGE : EDGE + rows, :].astype(f32)
        terms = term if terms is None else terms + term
        scaled = (grad * scale).astype(bf16)
        top_ref[j] = scaled[: rows // 2, :]
        bottom_ref[j] = scaled[rows // 2 :, :]
    total = jnp.sum(terms, axis=1, keepdims=True)

    @pl.when(pl.program_id(0) == 0)
    def _():
        term_ref[...] = total

    @pl.when(pl.program_id(0) > 0)
    def _():
        term_ref[...] += total


def second_filter(
    seq, features, gated, signal, segments, closings, rates, residues, above, middle, projected,
    short, scale,
):
    extended, columns = above.shape
    rows = extended - EDGE
    modes = rates.shape[0]
    shapes = [
        jax.ShapeDtypeStruct((rows, columns), bf16),
        jax.ShapeDtypeStruct((3, rows // 2, columns), bf16),
        jax.ShapeDtypeStruct((3, rows // 2, columns), bf16),
        jax.ShapeDtypeStruct((rows, 1), f32),
    ]
    operands = (
        features, gated, signal, segments, closings, rates, residues, above, middle, projected, short,
    )
    return call(
        functools.partial(second_filter_kernel, closings.shape[0]),
        (columns // LANES,),
        [lanes(a.shape) for a in operands] + [whole(scale.shape)],
        [lanes(s.shape) for s in shapes[:3]] + [whole((rows, 1))],
        shapes,
        [pltpu.VMEM((SEGMENTS * modes, LANES), f32), pltpu.VMEM((2, extended, LANES), f32)]
        + [pltpu.VMEM((rows + SHIFT, LANES), f32)] * 2
        + [pltpu.VMEM((modes, LANES), f32)] * 2
        + [pltpu.VMEM((2, modes, LANES), f32), pltpu.VMEM((rows + SHIFT, LANES), f32)],
        250 * VECTOR * rows * columns,
        40 * rows * columns,
        prefetch=1,
    )(seq, *operands, scale)


def shift(value, axis, by):
    devices = lax.axis_size(axis)
    pairs = [(i, i + by) for i in range(devices) if 0 <= i + by < devices]
    return lax.ppermute(value, axis, pairs)


def gather_ch(value):
    return lax.all_gather(value, "ch", axis=0, tiled=False)


def scatter_ch(value):
    return lax.psum_scatter(value, "ch", scatter_dimension=0, tiled=False)


def exchange_seq(value):
    return lax.all_to_all(value, "seq", split_axis=0, concat_axis=0, tiled=True)


def gather_seq(value):
    return exchange_seq(jnp.broadcast_to(value[None], (lax.axis_size("seq"),) + value.shape))


def seq_ring():
    devices = lax.axis_size("seq")
    if devices % 2:
        return list(range(devices))
    return list(range(0, devices, 2)) + list(range(devices - 1, 0, -2))


def seq_hop(value, by):
    ring = seq_ring()
    pairs = [(ring[i], ring[(i + by) % len(ring)]) for i in range(len(ring))]
    return lax.ppermute(value, "seq", pairs)


def ring_gather(parts):
    shards = lax.axis_size("seq")
    firsts = [0, parts[0].shape[1]][: len(parts)]
    out = [(0, first, part) for first, part in zip(firsts, parts)]
    up = down = parts
    for step in range(1, (shards + 1) // 2):
        up, down = [seq_hop(a, 1) for a in up], [seq_hop(a, -1) for a in down]
        out += [(shards - step, first, part) for first, part in zip(firsts, up)]
        out += [(step, first, part) for first, part in zip(firsts, down)]
    if shards % 2 == 0:
        if len(parts) == 1:
            half = parts[0].shape[1] // 2
            up, down = [up[0][:, :half]], [down[0][:, half:]]
        else:
            half = firsts[1]
        out += [(shards // 2, 0, seq_hop(up[0], 1)), (shards // 2, half, seq_hop(down[-1], -1))]
    return out


def ring_order():
    ring = seq_ring()
    twice = jnp.array(ring + ring, jnp.int32)
    place = jnp.argmax(twice[: len(ring)] == lax.axis_index("seq")).astype(jnp.int32)
    return lax.dynamic_slice_in_dim(twice, place, len(ring), 0)


def ch_hop(value, by):
    devices = lax.axis_size("ch")
    pairs = [(i, (i + 2 * by) % devices) for i in range(devices)]
    return lax.ppermute(value, "ch", pairs)


def sibling(value):
    return lax.ppermute(value, "ch", [(i, i ^ 1) for i in range(lax.axis_size("ch"))])


def scatter_order():
    devices = lax.axis_size("ch")
    me = lax.axis_index("ch")
    places = jnp.arange(devices // 2, dtype=jnp.int32)
    return jnp.stack([(2 * places + other) % devices for other in (me, me ^ 1)], axis=1).reshape(-1)


def added(*terms):
    return functools.reduce(lambda a, b: a + b, [t.astype(f32) for t in terms])


def ring_scatter(pieces, other_pieces, near, far):
    half = pieces.shape[0]
    other_pieces, *near = tie(other_pieces, *near)
    mine = added(pieces, sibling(other_pieces)).astype(bf16)
    if half == 1:
        return mine[0].astype(f32), near, far
    steps = (half - 1) // 2
    rows = mine.shape[1]
    middle = rows // 32 * 16
    up = down = None
    if half % 2 == 0:
        opposite = mine[half // 2]
        up, down = ch_hop(opposite[:middle], 1), ch_hop(opposite[middle:], -1)
        if half == 2:
            return added(mine[0], jnp.concatenate([up, down], axis=0)), near, far
    for step in range(steps, 0, -1):
        first, second = mine[step], mine[half - step]
        if up is not None and step == steps and half % 2 == 0:
            first = jnp.concatenate(
                [added(first[:middle], up).astype(bf16), first[middle:]], axis=0
            )
            second = jnp.concatenate(
                [second[:middle], added(second[middle:], down).astype(bf16)], axis=0
            )
        elif up is not None:
            first, second = added(first, up).astype(bf16), added(second, down).astype(bf16)
        up, down = ch_hop(first, 1), ch_hop(second, -1)
    up, down, *far = tie(up, down, *far)
    return added(mine[0], up, down), near, far


def tie(*values):
    return lax.optimization_barrier(values)


def per_device(
    token_ids,
    embedding,
    gain_first,
    gain_second,
    weights_first,
    weights_second,
    short_first,
    short_second,
    medium,
    residues,
    decay_rates,
    cotangent,
):
    shards = lax.axis_size("seq")
    pieces = lax.axis_size("ch")
    seq = lax.axis_index("seq")
    vocab, width = embedding.shape
    rows = token_ids.shape[0]
    features = width * pieces
    taps, tap_count = medium.shape[0], short_first.shape[0]
    front = round_up(EDGE + taps - 1 + tap_count - 1, 16)
    back = round_up(2 * EDGE + taps - 1, 16)
    w_first, w_second = (jnp.transpose(w, (1, 0, 2)) for w in (weights_first, weights_second))
    s_first, s_second = (jnp.transpose(s, (1, 0, 2)) for s in (short_first, short_second))

    order = ring_order()
    each = pieces // shards
    share = vocab // shards
    at = seq * share

    row = lax.broadcasted_iota(jnp.int32, (EDGE, width), 0)
    gains = jnp.where(row == 0, gain_first, jnp.where(row == 1, gain_second, jnp.zeros((), bf16)))
    own_embedding = lax.dynamic_slice_in_dim(embedding, at, share, 0)
    gathered = gather_ch(jnp.concatenate([own_embedding, gains], axis=0))
    tokens = lax.all_gather(token_ids, "seq", axis=0, tiled=True)
    slots = jnp.zeros(shards, jnp.int32).at[order].set(jnp.arange(shards, dtype=jnp.int32))
    turned = jnp.take(embedding.reshape(shards, share, width), order, axis=0)
    turned = turned.reshape(vocab, width)
    tokens = jnp.take(slots, tokens // share) * share + tokens % share
    tokens = jnp.pad(tokens, (front, back), constant_values=-1)
    tokens = lax.dynamic_slice_in_dim(tokens, seq * rows, front + rows + back, 0)
    behind = shift(cotangent[:EDGE], "seq", -1)
    cotangents = jnp.concatenate([cotangent, behind], axis=0)
    tokens, turned, cotangents, gathered = tie(tokens[:, None], turned, cotangents, gathered)
    gains_first = gathered[:, share : share + 1, :].astype(f32)
    gains_second = gathered[:, share + 1 : share + 2, :].astype(f32)
    own_table, own_scale = project(gathered, gathered, share, 0, w_first, share)
    tables = ring_gather([own_table])

    middle, filtered_first = first_forward(tokens, tables, turned, s_first, medium, rows, front)
    later, held = tie(tokens[front - EDGE :], middle)
    features_first = first_features(later, tables, s_first)

    middles = gather_ch(middle)
    block = exchange_seq(gathered[:, :share, :].reshape(shards, each, share, width))
    blocks = [block[:, i] for i in range(each)]
    block_gains = [
        lax.dynamic_slice_in_dim(g, seq * each, each, 0) for g in (gains_first, gains_second)
    ]
    core = lax.axis_index("ch") % each
    places = jnp.stack([core, 1 - core]).astype(jnp.int32)
    straight, scattered = jnp.arange(pieces, dtype=jnp.int32), scatter_order()
    blank = jnp.zeros((EDGE, width), bf16)
    features_first, places, straight, scattered, blank, middles, *rest = tie(
        features_first, places, straight, scattered, blank, middles, *blocks, *block_gains
    )
    blocks, block_gains = rest[:each], rest[each:]
    own = middles.reshape(shards, each, rows + 2 * EDGE, width)
    own = lax.dynamic_slice(own, (0, core, EDGE, 0), (shards, 1, rows, width))
    projected, scale = project(middles, gathered, share, 1, w_second, rows + 2 * EDGE)
    features_second, gated, signal, segments, closing = second_features(
        projected, s_second, cotangents, decay_rates, shards
    )
    own, closings = tie(own[:, 0], exchange_seq(closing))
    columns = exchange_seq(own)
    output, *grads, terms = second_filter(
        seq[None], features_second, gated, signal, segments, closings,
        decay_rates, residues, cotangents, middle, projected, s_second, scale,
    )
    scale = scale[EDGE : EDGE + rows]
    pieces_of = ring_gather(grads)
    (partial,) = project_back(grads, w_second, straight, blank, False)
    partial, columns = tie(partial, columns)
    other = sibling(columns)
    partial_sum = scatter_ch(partial)
    terms = lax.psum(terms[:, 0], "ch")
    partial_sum, other, *arrays = tie(partial_sum, other, *[a for _, _, a in pieces_of[2:-2]])
    pieces_of[2:-2] = [old[:2] + (new,) for old, new in zip(pieces_of[2:-2], arrays)]
    grad_normed = partial_sum.astype(f32)
    as_float = middle[EDGE : EDGE + rows].astype(f32)
    grad_middle = (
        cotangent.astype(f32)
        + gain_second.astype(f32) * grad_normed
        - as_float * (scale * scale) * terms[:, None] / features
    ).astype(bf16)
    grad_gain_second = jnp.sum(grad_normed * as_float, axis=0)

    halo = shift(grad_middle[:back], "seq", -1)
    halo, far_up, far_down = tie(halo, pieces_of[-2][2], pieces_of[-1][2])
    pieces_of[-2:] = [pieces_of[-2][:2] + (far_up,), pieces_of[-1][:2] + (far_down,)]
    sums = first_backward(
        token_ids[None], grad_middle, halo, features_first, filtered_first, s_first, medium, vocab,
        shards,
    )
    sums = exchange_seq(sums)
    grad_weights_second = weight_grad(
        [columns, other], places, pieces_of, order, block_gains[1]
    )
    sums, grad_weights_second = tie(sums, grad_weights_second)
    own_sums = jnp.sum(sums.astype(f32), axis=0)
    terms = jnp.sum(own_sums[:3] * own_table.astype(f32), axis=(0, 2))
    own_grads = (own_sums[:3] * own_scale[None]).astype(bf16)
    all_grads = ring_gather([own_grads])
    extra_rows = -(-share // width)
    extra = jnp.pad(terms, (0, EDGE * width - share)).reshape(EDGE, width).astype(bf16)
    partial, other_partial = project_back([own_grads], w_first, scattered, extra, True)
    grad_normed, near, far = ring_scatter(
        partial, other_partial, [a for _, _, a in all_grads[1:-2]], [a for _, _, a in all_grads[-2:]]
    )
    all_grads[1:] = [old[:2] + (new,) for old, new in zip(all_grads[1:], near + far)]
    terms = grad_normed[share : share + extra_rows].reshape(-1)[:share]
    grad_normed = grad_normed[:share]
    grad_weights_first = weight_grad(blocks, straight, all_grads, order, block_gains[0])

    as_float = own_embedding.astype(f32)
    grad_embedding = (
        own_sums[3]
        + gain_first.astype(f32) * grad_normed
        - as_float * (own_scale * own_scale) * terms[:, None] / features
    )
    grad_gain_first = jnp.sum(grad_normed * as_float, axis=0)
    last = jnp.concatenate(
        [
            grad_embedding,
            grad_gain_first[None],
            grad_gain_second[None],
            jnp.zeros((EDGE - 2, width), f32),
        ],
        axis=0,
    ).astype(bf16)
    last = gather_seq(last).astype(f32)
    return (
        output,
        last[:, :share].reshape(vocab, width),
        jnp.sum(last[:, share], axis=0),
        jnp.sum(last[:, share + 1], axis=0),
        jnp.transpose(grad_weights_first, (1, 0, 2)),
        jnp.transpose(grad_weights_second, (1, 0, 2)),
    )


def solution(mesh):
    placed = (
        P("seq"),
        P(None, "ch"),
        P("ch"),
        P("ch"),
        P(None, None, "ch"),
        P(None, None, "ch"),
        P(None, None, "ch"),
        P(None, None, "ch"),
        P(None, "ch"),
        P(None, "ch"),
        P(None, "ch"),
        P("seq", "ch"),
    )
    return jax.shard_map(
        per_device,
        mesh=mesh,
        in_specs=placed,
        out_specs=(
            P("seq", "ch"),
            P(None, "ch"),
            P("ch"),
            P("ch"),
            P("seq", None, "ch"),
            P("seq", None, "ch"),
        ),
        check_vma=False,
    )
```
